32 devices in a mesh: dp: 8 (over y, x, core), tensor: 4 (over z).
Axes of the slice: x: 2, y: 2, z: 4, core: 2. Of those that a mesh axis runs over, the one named last changes fastest.
Arguments:
- tokens: bfloat16 [5120, 2048], P(('dp', 'tensor')), may hold values from -6 to 6
- lengths: int32 [8, 3], P('dp'), may hold values from 1 to 512, 640 in all within a row
- attn_gain: bfloat16 [2048], P('dp'), may hold values from 0.5 to 1.5
- w_query: bfloat16 [2048, 2048], P('dp', 'tensor'), may hold values from -0.125 to 0.125
- w_key: bfloat16 [2048, 256], P('dp', 'tensor'), may hold values from -0.125 to 0.125
- w_value: bfloat16 [2048, 256], P('dp', 'tensor'), may hold values from -0.125 to 0.125
- w_output: bfloat16 [2048, 2048], P('tensor', 'dp'), may hold values from -2 to 2
- ffn_gain: bfloat16 [2048], P('dp'), may hold values from 0.5 to 1.5
- w_gate: bfloat16 [2048, 5632], P('dp', 'tensor'), may hold values from -0.125 to 0.125
- w_up: bfloat16 [2048, 5632], P('dp', 'tensor'), may hold values from -0.125 to 0.125
- w_down: bfloat16 [5632, 2048], P('tensor', 'dp'), may hold values from -0.078125 to 0.078125
- cotangent: bfloat16 [5120, 2048], P(('dp', 'tensor')), may hold values from -6 to 6
Outputs:
- block_out: bfloat16 [5120, 2048], P(('dp', 'tensor'))
- grad_tokens: bfloat16 [5120, 2048], P(('dp', 'tensor'))
- grad_attn_gain: float32 [2048], P('dp')
- grad_query: float32 [2048, 2048], P('dp', 'tensor')
- grad_key: float32 [2048, 256], P('dp', 'tensor')
- grad_value: float32 [2048, 256], P('dp', 'tensor')
- grad_output: float32 [2048, 2048], P('tensor', 'dp')
- grad_ffn_gain: float32 [2048], P('dp')
- grad_gate: float32 [2048, 5632], P('dp', 'tensor')
- grad_up: float32 [2048, 5632], P('dp', 'tensor')
- grad_down: float32 [5632, 2048], P('tensor', 'dp')
The draws below stay inside these ranges and needn't reach their ends.
Inputs may be any that keep to these rules, and one draw needn't show every extreme that they name: Each row lists the lengths of the sequences packed in order into one group of 640 tokens; a row sums to 640 and its largest entry is exactly 512.
All inputs are finite; a program needn't handle non-finite values.
Results may differ from the reference program's by a relative error of at most 0.025.
Values may be sent and summed in bfloat16 or wider, within the bound.
No kernel may reach another device: no remote copies, remote signals or barrier semaphores. Data moves between devices by JAX's collectives and lax.ppermute only.
A program may use at most 192 MiB of HBM per device.

```python
import math
import jax
import jax.numpy as jnp
import numpy as np
from jax import lax

D = 2048
HEADS = 32
KV_HEADS = 4
HEAD_DIM = 64
FF = 5632
TOK_DP = 640
SEQS = 3
LONGEST = 512
TOKENS = 5120
N_DP = 8


def block_scale(key, shape, shards, low, top_value):
    level, own = 1.0, jax.random.fold_in(key, 6)
    for axis_at, shards_of in shards:
        steps = jnp.exp(jax.random.uniform(jax.random.fold_in(own, axis_at), (shards_of,), jnp.float32, low / len(shards), top_value / len(shards)))
        level = level * jnp.repeat(steps, shape[axis_at] // shards_of).reshape([-1 if axis == axis_at else 1 for axis in range(len(shape))])
    return level


def profile(number_of, total, most, slope):
    weights = [(1 << 20) // math.isqrt(standing ** slope) + 1 for standing in range(2, number_of + 1)]
    surplus, holding = total - most - (number_of - 1), [1] * (number_of - 1)
    while surplus > 0:
        candidates = [i for i in range(number_of - 1) if holding[i] < most]
        whole, left = sum([weights[i] for i in candidates]), surplus
        for i in candidates:
            extra = min(most - holding[i], max(1, left * weights[i] // whole), surplus)
            holding[i] = holding[i] + extra
            surplus = surplus - extra
    return np.array([most] + holding)


def uneven(rng, count, total, reach, lean):
    if count == 2:
        one = jax.random.randint(rng, (), max(1, total - reach), min(reach, total - 1) + 1)
        return jnp.stack([one, total - one])
    sizes = jnp.asarray(profile(count, total, reach, lean), jnp.int32)
    twos = (count - 1) // 2
    donor, receiver = sizes[1:1 + 2 * twos:2], sizes[2:2 + 2 * twos:2]
    room = jnp.minimum(donor - 1, reach - receiver)
    shifted = jax.random.randint(jax.random.fold_in(rng, 1), (twos,), 0, 1 << 20) % (room + 1)
    sizes = sizes.at[1:1 + 2 * twos:2].set(donor - shifted).at[2:2 + 2 * twos:2].set(receiver + shifted)
    return sizes[jax.random.permutation(jax.random.fold_in(rng, 2), count)]


def normal_values(rng, shape, width, limit, pieces=(), kind=jnp.bfloat16):
    values = width * jax.random.normal(rng, shape, jnp.float32)
    if pieces:
        values = values * block_scale(rng, shape, pieces, -0.22, 0.18)
    return jnp.clip(values, -limit, limit).astype(kind)


def setup_inputs(seed: int = 0) -> dict:
    splits = jax.random.split(jax.random.key(seed), 13)
    return {
        "tokens": normal_values(splits[0], (TOKENS, D), 1.0, 6.0, ((0, 32),)),
        "lengths": jax.vmap(lambda own: uneven(own, SEQS, TOK_DP, LONGEST, 2))(jax.random.split(splits[1], N_DP)).reshape((N_DP, SEQS)).astype(jnp.int32),
        "attn_gain": jnp.clip(1.0 + 0.1 * jax.random.normal(splits[2], (D,), jnp.float32), 0.5, 1.5).astype(jnp.bfloat16),
        "w_query": normal_values(splits[3], (D, HEADS * HEAD_DIM), D ** -0.5, 0.125, ((0, 8), (1, 4))),
        "w_key": normal_values(splits[4], (D, KV_HEADS * HEAD_DIM), D ** -0.5, 0.125, ((0, 8), (1, 4))),
        "w_value": normal_values(splits[5], (D, KV_HEADS * HEAD_DIM), D ** -0.5, 0.125, ((0, 8), (1, 4))),
        "w_output": normal_values(splits[6], (HEADS * HEAD_DIM, D), 8 ** -0.5, 2.0, ((0, 4), (1, 8))),
        "ffn_gain": jnp.clip(1.0 + 0.1 * jax.random.normal(splits[7], (D,), jnp.float32), 0.5, 1.5).astype(jnp.bfloat16),
        "w_gate": normal_values(splits[8], (D, FF), D ** -0.5, 0.125, ((0, 8), (1, 4))),
        "w_up": normal_values(splits[9], (D, FF), D ** -0.5, 0.125, ((0, 8), (1, 4))),
        "w_down": normal_values(splits[10], (FF, D), FF ** -0.5, 0.078125, ((0, 4), (1, 8))),
        "cotangent": normal_values(splits[11], (TOKENS, D), 1.0, 6.0, ((0, 32),)),
    }


EPS = 1e-05
ROPE_BASE = 10000.0
NEG_FILL = -1e+30

@jax.custom_vjp
def low(v):
    return lax.optimization_barrier(v.astype(jnp.bfloat16)).astype(jnp.float32)

@jax.custom_vjp
def low_back(v):
    return v

def low_keep(v):
    return (low(v), None)

def low_pass(kept, grad):
    return (grad,)

def back_keep(v):
    return (v, None)

def back_low(kept, grad):
    return (low(grad),)
low.defvjp(low_keep, low_pass)
low_back.defvjp(back_keep, back_low)

def seq_layout(row_lengths, total):
    places = jnp.arange(total, dtype=jnp.int32)
    ends = jnp.cumsum(row_lengths).astype(jnp.int32)
    starts = ends - row_lengths
    segment = lax.optimization_barrier(jnp.sum((places[:, None] >= ends[None, :]).astype(jnp.int32), axis=1))
    owner = segment[:, None] == jnp.arange(row_lengths.shape[0], dtype=jnp.int32)[None, :]
    begin = lax.optimization_barrier(jnp.sum(jnp.where(owner, starts[None, :], 0), axis=1)).astype(jnp.int32)
    return (segment, places - begin)

def rope_tables(position, head_dim):
    half = head_dim // 2
    freqs = ROPE_BASE ** (-(jnp.arange(half, dtype=jnp.float32) * 2.0 / head_dim))
    angles = position.astype(jnp.float32)[:, None] * freqs[None, :]
    cosine = jnp.cos(angles)
    sine = jnp.sin(angles)
    return (jnp.concatenate([cosine, cosine], 1), jnp.concatenate([sine, sine], 1))

def rotate(values, cosine, sine):
    half = values.shape[-1] // 2
    turned = jnp.concatenate([-values[..., half:], values[..., :half]], -1)
    return values * cosine[:, None, :] + turned * sine[:, None, :]

def forward(values, params, segment, cosine, sine):
    attn_gain, w_query, w_key, w_value, w_output, ffn_gain, w_gate, w_up, w_down = params
    highest = lax.Precision.HIGHEST
    scale = 1.0 / math.sqrt(HEAD_DIM)
    count_rows = values.shape[0]
    group = HEADS // KV_HEADS
    inv_one = lax.rsqrt(lax.optimization_barrier(jnp.mean(values * values, -1, keepdims=True)) + EPS)
    normed = low(values * inv_one * attn_gain)
    query = low_back(jnp.dot(normed, w_query, precision=highest)).reshape(count_rows, HEADS, HEAD_DIM)
    key = low_back(jnp.dot(normed, w_key, precision=highest)).reshape(count_rows, KV_HEADS, HEAD_DIM)
    value = low(low_back(jnp.dot(normed, w_value, precision=highest))).reshape(count_rows, KV_HEADS, HEAD_DIM)
    query = low(rotate(query, cosine, sine))
    key = low(rotate(key, cosine, sine))
    q_heads = query.reshape(count_rows, KV_HEADS, group, HEAD_DIM).transpose(1, 0, 2, 3)
    k_heads = key.transpose(1, 0, 2)
    v_heads = value.transpose(1, 0, 2)
    places = jnp.arange(count_rows, dtype=jnp.int32)
    allowed = (segment[:, None] == segment[None, :]) & (places[None, :] <= places[:, None])

    def one_head(parts):
        q_part, k_part, v_part = parts
        scores = low_back(jnp.einsum('qgd,kd->gqk', q_part, k_part, precision=highest) * scale)
        scores = jnp.where(allowed[None], scores, NEG_FILL)
        prob = low(jax.nn.softmax(scores, axis=-1))
        return jnp.einsum('gqk,kd->qgd', prob, v_part, precision=highest)
    mixed = lax.map(jax.checkpoint(one_head), (q_heads, k_heads, v_heads))
    mixed = low(low_back(mixed.transpose(1, 0, 2, 3).reshape(count_rows, HEADS * HEAD_DIM)))
    hidden = values + low_back(jnp.dot(mixed, w_output, precision=highest))
    inv_two = lax.rsqrt(lax.optimization_barrier(jnp.mean(hidden * hidden, -1, keepdims=True)) + EPS)
    normed_two = low(hidden * inv_two * ffn_gain)
    gate = low_back(jnp.dot(normed_two, w_gate, precision=highest))
    up_part = low_back(jnp.dot(normed_two, w_up, precision=highest))
    activation = low(jax.nn.silu(gate) * up_part)
    return hidden + low_back(jnp.dot(activation, w_down, precision=highest))

def reference(tokens, lengths, attn_gain, w_query, w_key, w_value, w_output, ffn_gain, w_gate, w_up, w_down, cotangent):
    weights = tuple((w.astype(jnp.float32) for w in (attn_gain, w_query, w_key, w_value, w_output, ffn_gain, w_gate, w_up, w_down)))
    groups = tokens.reshape(N_DP, TOK_DP, D)
    cot_groups = cotangent.reshape(N_DP, TOK_DP, D)

    def one_group(total, inputs):
        rows, row_lengths, row_cot = inputs
        segment, position = seq_layout(row_lengths, TOK_DP)
        cosine, sine = rope_tables(position, HEAD_DIM)

        def layer(values, *params):
            return forward(values, params, segment, cosine, sine)
        result, pullback = jax.vjp(layer, rows.astype(jnp.float32), *weights)
        grads = pullback(row_cot.astype(jnp.float32))
        total = tuple((t + g for t, g in zip(total, grads[1:])))
        return (total, (result.astype(jnp.bfloat16), grads[0].astype(jnp.bfloat16)))
    start = tuple((jnp.zeros(w.shape, jnp.float32) for w in weights))
    total, (results, grad_rows) = lax.scan(one_group, start, (groups, lengths, cot_groups))
    return (results.reshape(TOKENS, D), grad_rows.reshape(TOKENS, D), total[0], total[1], total[2], total[3], total[4], total[5], total[6], total[7], total[8])
```

```python
import math

import jax
import jax.numpy as jnp
from jax import lax
from jax.sharding import PartitionSpec as P

HEAD_DIM = 64


EPS = 1e-05
ROPE_BASE = 10000.0
NEG_FILL = -1e30


def seq_layout(row_lengths, places):
    ends = jnp.cumsum(row_lengths)
    starts = ends - row_lengths
    segment = jnp.sum((places[:, None] >= ends[None, :]).astype(jnp.int32), axis=1)
    owner = segment[:, None] == jnp.arange(row_lengths.shape[0], dtype=jnp.int32)[None, :]
    begin = jnp.sum(jnp.where(owner, starts[None, :], 0), axis=1)
    return (segment, places - begin)


def rope_tables(position, head_dim):
    half = head_dim // 2
    freqs = ROPE_BASE ** (-(jnp.arange(half, dtype=jnp.float32) * 2.0 / head_dim))
    angles = position.astype(jnp.float32)[:, None] * freqs[None, :]
    cosine = jnp.cos(angles)
    sine = jnp.sin(angles)
    return (jnp.concatenate([cosine, cosine], 1), jnp.concatenate([sine, sine], 1))


def rotate(values, cosine, sine):
    half = values.shape[-1] // 2
    turned = jnp.concatenate([-values[..., half:], values[..., :half]], -1)
    return values * cosine[:, None, :] + turned * sine[:, None, :]


def unrotate(grads, cosine, sine):
    half = grads.shape[-1] // 2
    scaled = grads * sine[:, None, :]
    back = jnp.concatenate([scaled[..., half:], -scaled[..., :half]], -1)
    return grads * cosine[:, None, :] + back


def dot(left, right):
    return jnp.dot(left, right, preferred_element_type=jnp.float32)


def inner(left, right):
    return lax.dot_general(
        left, right, (((0,), (0,)), ((), ())), preferred_element_type=jnp.float32
    )


def outer_t(left, right):
    return lax.dot_general(
        left, right, (((1,), (1,)), ((), ())), preferred_element_type=jnp.float32
    )


def norm_back(d_normed, unit, inv, gain):
    scaled = d_normed * gain
    return inv * (scaled - unit * jnp.mean(scaled * unit, -1, keepdims=True))


def turn_by(block, step):
    count = lax.axis_size("tensor")
    return lax.ppermute(block, "tensor", [(i, (i + step) % count) for i in range(count)])


def spread(block):
    count = lax.axis_size("tensor")
    return [block] + [turn_by(block, step) for step in range(1, count)]


def collect(total):
    count = lax.axis_size("tensor")
    rows = total.shape[0] // count
    parts = [total[k * rows : (k + 1) * rows] for k in range(count)]
    return [parts[0]] + [turn_by(parts[k], -k) for k in range(1, count)]


def sum_of(parts):
    total = parts[0].astype(jnp.float32)
    for part in parts[1:]:
        total = total + part.astype(jnp.float32)
    return total


def body(
    tokens,
    lengths,
    attn_gain,
    w_query,
    w_key,
    w_value,
    w_output,
    ffn_gain,
    w_gate,
    w_up,
    w_down,
    cotangent,
):
    bf16 = jnp.bfloat16
    scale = 1.0 / math.sqrt(HEAD_DIM)
    count = lax.axis_size("tensor")
    local_rows = tokens.shape[0]
    group_rows = local_rows * count
    width = w_query.shape[1]
    kv_width = w_key.shape[1]
    hidden_units = w_gate.shape[1]
    kv_local = kv_width // HEAD_DIM
    q_local = width // HEAD_DIM
    group = q_local // kv_local

    token_parts = spread(tokens)
    attn_pack = lax.all_gather(
        jnp.concatenate([w_query, w_output.T, w_key, w_value], 1), "dp", axis=0, tiled=True
    )
    gains = lax.all_gather(
        jnp.stack([attn_gain, ffn_gain])[None], "dp", axis=0, tiled=True
    ).astype(jnp.float32)
    gain_one = gains[:, 0].reshape(-1)
    gain_two = gains[:, 1].reshape(-1)
    ffn_pack = lax.all_gather(
        jnp.concatenate([w_gate, w_up, w_down.T], 1), "dp", axis=0, tiled=True
    )
    cot_parts = lax.all_gather(cotangent, "tensor", axis=0, tiled=False)
    me = lax.axis_index("tensor")
    order = (me + count - jnp.arange(count, dtype=jnp.int32)) % count
    cot_full = jnp.take(cot_parts, order, axis=0).reshape(group_rows, -1)

    full_query = attn_pack[:, :width]
    full_output = attn_pack[:, width : 2 * width]
    full_kv = attn_pack[:, 2 * width :]
    full_gate = ffn_pack[:, :hidden_units]
    full_up = ffn_pack[:, hidden_units : 2 * hidden_units]
    full_down = ffn_pack[:, 2 * hidden_units :]

    places = (order[:, None] * local_rows + jnp.arange(local_rows, dtype=jnp.int32)[None]).reshape(
        -1
    )
    segment, position = seq_layout(lengths[0], places)
    cosine, sine = rope_tables(position, HEAD_DIM)
    allowed = (segment[:, None] == segment[None, :]) & (places[None, :] <= places[:, None])
    resid_full = jnp.concatenate(token_parts, 0).astype(jnp.float32)
    inv_full = lax.rsqrt(jnp.mean(resid_full * resid_full, -1, keepdims=True) + EPS)
    normed_one = (resid_full * inv_full * gain_one).astype(bf16)
    query = dot(normed_one, full_query).reshape(group_rows, q_local, HEAD_DIM)
    query = (
        rotate(query, cosine, sine).astype(bf16).reshape(group_rows, kv_local, group, HEAD_DIM)
    )
    key_value = dot(normed_one, full_kv)
    key = key_value[:, :kv_width].reshape(group_rows, kv_local, HEAD_DIM)
    key = rotate(key, cosine, sine).astype(bf16)
    value = key_value[:, kv_width:].astype(bf16).reshape(group_rows, kv_local, HEAD_DIM)
    scores = jnp.einsum("qcgd,kcd->cgqk", query, key, preferred_element_type=jnp.float32) * scale
    scores = jnp.where(allowed[None, None], scores, NEG_FILL)
    row_max = jnp.max(scores, -1, keepdims=True)
    raised = jnp.exp(scores - row_max)
    row_total = jnp.sum(raised, -1, keepdims=True)
    log_sums = row_max + jnp.log(row_total)
    prob = (raised / row_total).astype(bf16)
    attended = (
        jnp.einsum("cgqk,kcd->qcgd", prob, value, preferred_element_type=jnp.float32)
        .reshape(group_rows, width)
        .astype(bf16)
    )
    resid = tokens.astype(jnp.float32)
    hidden = resid + sum_of(collect(outer_t(attended, full_output).astype(bf16)))

    inv_two = lax.rsqrt(jnp.mean(hidden * hidden, -1, keepdims=True) + EPS)
    unit_two = hidden * inv_two
    normed_two = jnp.concatenate(spread((unit_two * gain_two).astype(bf16)), 0)
    gate = dot(normed_two, full_gate)
    up_part = dot(normed_two, full_up)
    sigma = jax.nn.sigmoid(gate)
    swish = gate * sigma
    activation = (swish * up_part).astype(bf16)
    d_act = dot(cot_full, full_down)
    d_gate = (d_act * up_part * (sigma * (1.0 + gate * (1.0 - sigma)))).astype(bf16)
    d_up = (d_act * swish).astype(bf16)
    d_normed_two = sum_of(
        collect((outer_t(d_gate, full_gate) + outer_t(d_up, full_up)).astype(bf16))
    )
    ffn_grads = lax.psum_scatter(
        jnp.concatenate(
            [
                inner(normed_two, d_gate).astype(bf16),
                inner(normed_two, d_up).astype(bf16),
                inner(cot_full, activation).astype(bf16),
            ],
            1,
        ),
        "dp",
        scatter_dimension=0,
        tiled=True,
    ).astype(jnp.float32)
    down_parts = outer_t(activation, full_down).astype(bf16).reshape(count, local_rows, -1)
    down_parts = jnp.take(down_parts, order, axis=0)
    block_out = (
        hidden
        + lax.psum_scatter(down_parts, "tensor", scatter_dimension=0, tiled=False).astype(
            jnp.float32
        )
    ).astype(bf16)

    gain_two_part = jnp.sum(d_normed_two * unit_two, 0)
    d_hidden = cotangent.astype(jnp.float32) + norm_back(d_normed_two, unit_two, inv_two, gain_two)
    d_hidden_full = jnp.concatenate(spread(d_hidden.astype(bf16)), 0)
    grad_output_local = inner(d_hidden_full, attended).astype(bf16)
    d_attended = (
        dot(d_hidden_full, full_output).astype(bf16).reshape(group_rows, kv_local, group, HEAD_DIM)
    )
    scores = jnp.einsum("qcgd,kcd->cgqk", query, key, preferred_element_type=jnp.float32) * scale
    scores = jnp.where(allowed[None, None], scores, NEG_FILL)
    prob = jnp.exp(scores - log_sums)
    d_prob = jnp.einsum("qcgd,kcd->cgqk", d_attended, value, preferred_element_type=jnp.float32)
    delta = jnp.sum(prob * d_prob, -1, keepdims=True)
    d_scores = (prob * (d_prob - delta)).astype(bf16)
    d_query = jnp.einsum("cgqk,kcd->qcgd", d_scores, key, preferred_element_type=jnp.float32)
    d_key = jnp.einsum("cgqk,qcgd->kcd", d_scores, query, preferred_element_type=jnp.float32)
    d_value = jnp.einsum(
        "cgqk,qcgd->kcd", prob.astype(bf16), d_attended, preferred_element_type=jnp.float32
    )
    d_query = d_query.reshape(group_rows, q_local, HEAD_DIM) * scale
    d_query = unrotate(d_query, cosine, sine).reshape(group_rows, width).astype(bf16)
    d_key = unrotate(d_key * scale, cosine, sine).reshape(group_rows, kv_width).astype(bf16)
    d_value = d_value.reshape(group_rows, kv_width).astype(bf16)
    d_kv = jnp.concatenate([d_key, d_value], 1)
    d_normed_full = outer_t(d_query, full_query) + outer_t(d_kv, full_kv)
    d_normed_one = sum_of(collect(d_normed_full.astype(bf16)))
    gain_one_part = jnp.sum(d_normed_full * (resid_full * inv_full), 0)
    inv_one = inv_full[:local_rows]
    grad_tokens = (
        d_hidden + norm_back(d_normed_one, resid * inv_one, inv_one, gain_one)
    ).astype(bf16)
    attn_grads = lax.psum_scatter(
        jnp.concatenate(
            [
                inner(normed_one, d_query).astype(bf16),
                grad_output_local,
                inner(normed_one, d_kv).astype(bf16),
            ],
            1,
        ),
        "dp",
        scatter_dimension=0,
        tiled=True,
    ).astype(jnp.float32)
    gain_grads = lax.psum(jnp.stack([gain_one_part, gain_two_part]), ("dp", "tensor"))
    own = attn_gain.shape[0]
    gain_grads = lax.dynamic_slice_in_dim(gain_grads, lax.axis_index("dp") * own, own, 1)
    return (
        block_out,
        grad_tokens,
        gain_grads[0],
        attn_grads[:, :width],
        attn_grads[:, 2 * width : 2 * width + kv_width],
        attn_grads[:, 2 * width + kv_width :],
        attn_grads[:, width : 2 * width].T,
        gain_grads[1],
        ffn_grads[:, :hidden_units],
        ffn_grads[:, hidden_units : 2 * hidden_units],
        ffn_grads[:, 2 * hidden_units :].T,
    )


def solution(mesh):
    return jax.shard_map(
        body,
        mesh=mesh,
        in_specs=(
            P(("dp", "tensor"), None),
            P("dp", None),
            P("dp"),
            P("dp", "tensor"),
            P("dp", "tensor"),
            P("dp", "tensor"),
            P("tensor", "dp"),
            P("dp"),
            P("dp", "tensor"),
            P("dp", "tensor"),
            P("tensor", "dp"),
            P(("dp", "tensor"), None),
        ),
        out_specs=(
            P(("dp", "tensor"), None),
            P(("dp", "tensor"), None),
            P("dp"),
            P("dp", "tensor"),
            P("dp", "tensor"),
            P("dp", "tensor"),
            P("tensor", "dp"),
            P("dp"),
            P("dp", "tensor"),
            P("dp", "tensor"),
            P("tensor", "dp"),
        ),
        check_vma=False,
    )
```

```python
import functools
import math

import jax
import jax.numpy as jnp
from jax import lax
from jax.experimental import pallas as pl
from jax.experimental.pallas import tpu as pltpu
from jax.sharding import PartitionSpec as P

HEAD_DIM = 64
EPS = 1e-05
ROPE_BASE = 10000.0
NEG_FILL = -1e30
MIB = 1024 * 1024


def seq_layout(row_lengths, places):
    ends = jnp.cumsum(row_lengths)
    starts = ends - row_lengths
    segment = jnp.sum((places[:, None] >= ends[None, :]).astype(jnp.int32), axis=1)
    owner = segment[:, None] == jnp.arange(row_lengths.shape[0], dtype=jnp.int32)[None, :]
    begin = jnp.sum(jnp.where(owner, starts[None, :], 0), axis=1)
    return (segment, places - begin)


def rope_tables(position):
    half = HEAD_DIM // 2
    freqs = ROPE_BASE ** (-(jnp.arange(half, dtype=jnp.float32) * 2.0 / HEAD_DIM))
    angles = freqs[:, None] * position.astype(jnp.float32)[None, :]
    return (jnp.cos(angles), jnp.sin(angles))


def dot(left, right):
    return jnp.dot(left, right, preferred_element_type=jnp.float32)


def inner(left, right):
    return lax.dot_general(
        left, right, (((0,), (0,)), ((), ())), preferred_element_type=jnp.float32
    )


def outer_t(left, right):
    return lax.dot_general(
        left, right, (((1,), (1,)), ((), ())), preferred_element_type=jnp.float32
    )


def norm_back(d_normed, unit, inv, gain):
    scaled = d_normed * gain
    return inv * (scaled - unit * jnp.mean(scaled * unit, -1, keepdims=True))


def swap(block, *pairs):
    return lax.ppermute(block, "tensor", [p for i, j in pairs for p in ((i, j), (j, i))])


def outward(block):
    return lax.ppermute(block, "tensor", [(1, 0), (2, 3)])


def inward(block):
    return lax.ppermute(block, "tensor", [(0, 1), (3, 2)])


def spread(block):
    two = swap(block, (0, 2), (1, 3))
    one = swap(block, (0, 1), (2, 3))
    three = swap(block, (1, 2))
    return [one, two, three]


def whole(block, one, two, three, far):
    me = lax.axis_index("tensor")
    return jnp.concatenate([block, one, two, jnp.where((me == 1) | (me == 2), three, far)], 0)


def split(total):
    count = lax.axis_size("tensor")
    rows = total.shape[0] // count
    return [total[k * rows : (k + 1) * rows] for k in range(count)]


def add(left, right):
    return (left.astype(jnp.float32) + right.astype(jnp.float32)).astype(left.dtype)


def collect(total, *others):
    parts = split(total)
    far = inward(parts[3])
    far, parts, *others = lax.optimization_barrier((far, parts, *others))
    one = swap(parts[1], (0, 1), (2, 3))
    three = swap(parts[3], (1, 2))
    two = swap(add(parts[2], far), (0, 2), (1, 3))
    return ([parts[0], one, two, three], *others)


def after(value, *others):
    return lax.optimization_barrier((value, *others))[0]


def grads_kernel(count, *refs):
    lefts, rights, out = refs[:count], refs[count:-1], refs[-1]
    at = 0
    for left, right in zip(lefts, rights):
        width = right.shape[1]
        out[:, at : at + width] = inner(left[...], right[...]).astype(out.dtype)
        at += width
    for extra in rights[count:]:
        width = extra.shape[1]
        out[:, at : at + width] = extra[...]
        at += width


def grads_of(pairs, extras=()):
    rows, depth = pairs[0][0].shape
    block = min(256, depth)
    width = sum(right.shape[1] for _, right in pairs) + sum(e.shape[1] for e in extras)
    return pl.pallas_call(
        lambda *refs: grads_kernel(len(pairs), *refs),
        grid=(depth // block,),
        out_shape=jax.ShapeDtypeStruct((depth, width), jnp.bfloat16),
        in_specs=[pl.BlockSpec((rows, block), lambda i: (0, i)) for _ in pairs]
        + [pl.BlockSpec(right.shape, lambda i: (0, 0)) for _, right in pairs]
        + [pl.BlockSpec((block, e.shape[1]), lambda i: (i, 0)) for e in extras],
        out_specs=pl.BlockSpec((block, width), lambda i: (i, 0)),
        cost_estimate=pl.CostEstimate(
            flops=2 * rows * depth * width,
            bytes_accessed=2 * (depth * width + rows * width + 2 * rows * depth),
            transcendentals=0,
        ),
        compiler_params=pltpu.CompilerParams(vmem_limit_bytes=40 * MIB),
    )(*[left for left, _ in pairs], *[right for _, right in pairs], *extras)


def sum_of(parts):
    total = parts[0].astype(jnp.float32)
    for part in parts[1:]:
        total = total + part.astype(jnp.float32)
    return total


def turn(block, cosine, sine):
    half = HEAD_DIM // 2
    first, second = block[:half], block[half:]
    return jnp.concatenate([first * cosine - second * sine, second * cosine + first * sine], 0)

def mask_bias(row_ref, col_ref, bias):
    allowed = (col_ref[:, 0:1] == row_ref[0:1, :]) & (col_ref[:, 1:2] <= row_ref[1:2, :])
    bias[...] = jnp.where(allowed, 0.0, NEG_FILL)

def attend_kernel(q_width, kv_width, x_ref, gain_ref, pack_ref, cos_ref, sin_ref, row_ref, col_ref,
                  out_ref, normed_ref, heads_ref, attended_ref, sums_ref, bias):
    bf16 = jnp.bfloat16
    scale = 1.0 / math.sqrt(HEAD_DIM)
    q_heads, kv_heads = q_width // HEAD_DIM, kv_width // HEAD_DIM
    qkv = q_width + 2 * kv_width
    x = x_ref[...].astype(jnp.float32)
    inv = lax.rsqrt(jnp.mean(x * x, -1, keepdims=True) + EPS)
    normed_ref[...] = (x * inv * gain_ref[...]).astype(bf16)
    mask_bias(row_ref, col_ref, bias)
    cosine, sine = cos_ref[...], sin_ref[...]
    heads = dot(normed_ref[...], pack_ref[:, :qkv]).T
    for h in range(q_heads + kv_heads):
        at = h * HEAD_DIM
        turned = turn(heads[at : at + HEAD_DIM], cosine, sine).astype(bf16)
        heads_ref[at : at + HEAD_DIM] = turned * bf16(scale) if h < q_heads else turned
    heads_ref[q_width + kv_width :] = heads[q_width + kv_width :].astype(bf16)
    parts = []
    for h in range(q_heads):
        c = h * kv_heads // q_heads
        at = q_width + c * HEAD_DIM
        key = heads_ref[at : at + HEAD_DIM].T
        value_t = heads_ref[at + kv_width : at + kv_width + HEAD_DIM]
        scores = dot(key, heads_ref[h * HEAD_DIM : (h + 1) * HEAD_DIM]) + bias[...]
        top = jnp.max(scores, 0, keepdims=True)
        raised = jnp.exp(scores - top)
        total = jnp.sum(raised, 0, keepdims=True)
        sums_ref[h : h + 1] = top + jnp.log(total)
        parts.append(dot(value_t, raised.astype(bf16)) / total)
    attended_ref[...] = jnp.concatenate(parts, 0).T.astype(bf16)
    out_ref[...] = outer_t(attended_ref[...], pack_ref[:, qkv:]).astype(bf16)

def attend(x, gain, pack, cosine, sine, row, col, q_width, kv_width):
    rows, depth = x.shape
    bf16 = jnp.bfloat16
    qkv = q_width + 2 * kv_width
    return pl.pallas_call(
        functools.partial(attend_kernel, q_width, kv_width),
        out_shape=(
            jax.ShapeDtypeStruct((rows, depth), bf16),
            jax.ShapeDtypeStruct((rows, depth), bf16),
            jax.ShapeDtypeStruct((qkv, rows), bf16),
            jax.ShapeDtypeStruct((rows, q_width), bf16),
            jax.ShapeDtypeStruct((q_width // HEAD_DIM, rows), jnp.float32),
        ),
        scratch_shapes=[pltpu.VMEM((rows, rows), jnp.float32)],
        cost_estimate=pl.CostEstimate(
            flops=2 * rows * depth * (qkv + q_width) + 4 * rows * rows * q_width,
            bytes_accessed=2 * (3 * rows * depth + depth * (qkv + q_width)),
            transcendentals=rows * rows * q_width // HEAD_DIM,
        ),
        compiler_params=pltpu.CompilerParams(vmem_limit_bytes=48 * MIB),
    )(x, gain, pack, cosine, sine, row, col)

def attend_back_kernel(q_width, kv_width, g_ref, x_ref, gain_ref, pack_ref, cos_ref, sin_ref, row_ref, col_ref,
                       heads_ref, sums_ref, out_ref, d_qkv_ref, gain_part_ref, bias, d_att_t, d_heads_t):
    bf16 = jnp.bfloat16
    scale = 1.0 / math.sqrt(HEAD_DIM)
    q_heads, kv_heads = q_width // HEAD_DIM, kv_width // HEAD_DIM
    qkv = q_width + 2 * kv_width
    mask_bias(row_ref, col_ref, bias)
    d_att_t[...] = dot(g_ref[...], pack_ref[:, qkv:]).T.astype(bf16)
    cosine, sine = cos_ref[...], sin_ref[...]
    for c in range(kv_heads):
        at = q_width + c * HEAD_DIM
        key_t = heads_ref[at : at + HEAD_DIM]
        key = key_t.T
        value = heads_ref[at + kv_width : at + kv_width + HEAD_DIM].T
        d_key = d_value = 0.0
        for h in range(c * q_heads // kv_heads, (c + 1) * q_heads // kv_heads):
            query_t = heads_ref[h * HEAD_DIM : (h + 1) * HEAD_DIM]
            d_out_t = d_att_t[h * HEAD_DIM : (h + 1) * HEAD_DIM]
            prob = jnp.exp(dot(key, query_t) + bias[...] - sums_ref[h : h + 1])
            d_prob = dot(value, d_out_t)
            delta = jnp.sum(prob * d_prob, 0, keepdims=True)
            d_scores = (prob * (d_prob - delta)).astype(bf16)
            d_value = d_value + outer_t(prob.astype(bf16), d_out_t)
            d_key = d_key + outer_t(d_scores, query_t)
            d_query = dot(key_t, d_scores) * scale
            d_heads_t[h * HEAD_DIM : (h + 1) * HEAD_DIM] = turn(d_query, cosine, -sine)
        d_heads_t[at : at + HEAD_DIM] = turn(d_key.T, cosine, -sine)
        d_heads_t[at + kv_width : at + kv_width + HEAD_DIM] = d_value.T
    d_qkv_ref[...] = d_heads_t[...].T.astype(bf16)
    d_normed = outer_t(d_qkv_ref[...], pack_ref[:, :qkv])
    out_ref[...] = d_normed.astype(bf16)
    x = x_ref[...].astype(jnp.float32)
    inv = lax.rsqrt(jnp.mean(x * x, -1, keepdims=True) + EPS)
    gain_part_ref[...] = jnp.sum(d_normed * (x * inv), 0, keepdims=True)

def attend_back(g, x, gain, pack, cosine, sine, row, col, heads, sums, q_width, kv_width):
    rows, depth = x.shape
    bf16 = jnp.bfloat16
    qkv = q_width + 2 * kv_width
    return pl.pallas_call(
        functools.partial(attend_back_kernel, q_width, kv_width),
        out_shape=(
            jax.ShapeDtypeStruct((rows, depth), bf16),
            jax.ShapeDtypeStruct((rows, qkv), bf16),
            jax.ShapeDtypeStruct((1, depth), jnp.float32),
        ),
        scratch_shapes=[
            pltpu.VMEM((rows, rows), jnp.float32),
            pltpu.VMEM((q_width, rows), bf16),
            pltpu.VMEM((qkv, rows), jnp.float32),
        ],
        cost_estimate=pl.CostEstimate(
            flops=2 * rows * depth * (qkv + q_width) + 10 * rows * rows * q_width,
            bytes_accessed=2 * (3 * rows * depth + depth * (qkv + q_width)),
            transcendentals=rows * rows * q_width // HEAD_DIM,
        ),
        compiler_params=pltpu.CompilerParams(vmem_limit_bytes=56 * MIB),
    )(g, x, gain, pack, cosine, sine, row, col, heads, sums)


def body(
    tokens,
    lengths,
    attn_gain,
    w_query,
    w_key,
    w_value,
    w_output,
    ffn_gain,
    w_gate,
    w_up,
    w_down,
    cotangent,
):
    bf16 = jnp.bfloat16
    count = lax.axis_size("tensor")
    local_rows = tokens.shape[0]
    width = w_query.shape[1]
    kv_width = w_key.shape[1]
    hidden_units = w_gate.shape[1]

    token_parts = spread(tokens)
    attn_pack = lax.all_gather(
        jnp.concatenate([w_query, w_key, w_value, w_output.T], 1), "dp", axis=0, tiled=True
    )
    gains = lax.all_gather(
        jnp.stack([attn_gain, ffn_gain])[None], "dp", axis=0, tiled=True
    ).astype(jnp.float32)
    gain_one = gains[:, 0].reshape(1, -1)
    gain_two = gains[:, 1].reshape(1, -1)
    ffn_pack = lax.all_gather(
        jnp.concatenate([w_gate, w_up, w_down.T], 1),
        "dp",
        axis=0,
        tiled=True,
    )
    token_parts.append(outward(token_parts[1]))
    cot_own, token_parts = lax.optimization_barrier((cotangent, token_parts))
    cot_parts = spread(cot_own)
    full_gate_up = ffn_pack[:, : 2 * hidden_units]
    full_down = ffn_pack[:, 2 * hidden_units :]

    order = lax.axis_index("tensor") ^ jnp.arange(count, dtype=jnp.int32)
    places = (order[:, None] * local_rows + jnp.arange(local_rows, dtype=jnp.int32)[None]).reshape(
        -1
    )
    segment, position = seq_layout(lengths[0], places)
    cosine, sine = rope_tables(position)
    as_row = jnp.stack([segment, places])
    as_column = jnp.stack([segment, places], 1)
    token_rows = whole(tokens, *token_parts)
    out_total, normed_one, heads, attended, log_sums = attend(
        token_rows, gain_one, attn_pack, cosine, sine, as_row, as_column, width, kv_width
    )
    out_parts, cot_parts = collect(out_total, cot_parts)
    cot_parts.append(outward(cot_parts[1]))
    out_parts, cot_parts = lax.optimization_barrier((out_parts, cot_parts))
    resid = tokens.astype(jnp.float32)
    hidden = resid + sum_of(out_parts)

    inv_two = lax.rsqrt(jnp.mean(hidden * hidden, -1, keepdims=True) + EPS)
    unit_two = hidden * inv_two
    own_two = (unit_two * gain_two).astype(bf16)
    two_rows = spread(own_two)
    two_rows.append(outward(two_rows[1]))
    normed_two = whole(own_two, *two_rows)
    gate_up = dot(normed_two, full_gate_up)
    gate = gate_up[:, :hidden_units]
    up_part = gate_up[:, hidden_units:]
    sigma = jax.nn.sigmoid(gate)
    swish = gate * sigma
    activation = (swish * up_part).astype(bf16)
    cot_full = whole(cotangent, *cot_parts)
    d_act = dot(cot_full, full_down)
    d_gate = (d_act * up_part * (sigma * (1.0 + gate * (1.0 - sigma)))).astype(bf16)
    d_up = (d_act * swish).astype(bf16)
    d_gate_up = jnp.concatenate([d_gate, d_up], 1)
    two_total = outer_t(d_gate_up, full_gate_up).astype(bf16)
    two_parts, activation, d_gate_up = collect(two_total, activation, d_gate_up)
    ffn_local = grads_of([(normed_two, d_gate_up), (cot_full, activation)])
    down_total = outer_t(activation, full_down).astype(bf16)
    two_parts, ffn_local, down_total = lax.optimization_barrier((two_parts, ffn_local, down_total))
    ffn_grads = lax.psum_scatter(ffn_local, "dp", scatter_dimension=0, tiled=True)
    d_normed_two = sum_of(two_parts)

    gain_two_part = jnp.sum(d_normed_two * unit_two, 0)
    d_hidden = cotangent.astype(jnp.float32) + norm_back(d_normed_two, unit_two, inv_two, gain_two)
    d_hidden_own = d_hidden.astype(bf16)
    back_rows = spread(d_hidden_own)
    down_parts, back_rows = collect(down_total, back_rows)
    back_rows.append(outward(back_rows[1]))
    d_hidden_full = whole(d_hidden_own, *back_rows)
    one_total, d_qkv, gain_one_part = attend_back(
        d_hidden_full,
        token_rows,
        gain_one,
        attn_pack,
        cosine,
        sine,
        as_row,
        as_column,
        heads,
        log_sums,
        width,
        kv_width,
    )
    one_total, down_parts = lax.optimization_barrier((one_total, down_parts))
    one_parts, d_qkv, gain_one_part = collect(one_total, d_qkv, gain_one_part)
    gain_parts = jnp.stack([gain_one_part[0], gain_two_part])
    gain_parts = sum_of(
        [gain_parts]
        + [
            lax.ppermute(gain_parts, "tensor", [(i, (i + k) % count) for i in range(count)])
            for k in range(1, count)
        ]
    )
    attn_local = grads_of(
        [(normed_one, d_qkv), (d_hidden_full, attended)],
        [jnp.pad(gain_parts.T.astype(bf16), ((0, 0), (0, 126)))],
    )
    attn_local, ffn_grads, one_parts[1:2] = lax.optimization_barrier(
        (attn_local, ffn_grads, one_parts[1:2])
    )
    attn_grads = lax.psum_scatter(attn_local, "dp", scatter_dimension=0, tiled=True).astype(
        jnp.float32
    )
    ffn_grads = ffn_grads.astype(jnp.float32)
    block_out = (hidden + sum_of(down_parts)).astype(bf16)
    inv_one = lax.rsqrt(jnp.mean(resid * resid, -1, keepdims=True) + EPS)
    grad_tokens = (
        d_hidden + norm_back(sum_of(one_parts), resid * inv_one, inv_one, gain_one)
    ).astype(bf16)
    at_output = width + 2 * kv_width
    return (
        block_out,
        grad_tokens,
        attn_grads[:, at_output + width],
        attn_grads[:, :width],
        attn_grads[:, width : width + kv_width],
        attn_grads[:, width + kv_width : at_output],
        attn_grads[:, at_output : at_output + width].T,
        attn_grads[:, at_output + width + 1],
        ffn_grads[:, :hidden_units],
        ffn_grads[:, hidden_units : 2 * hidden_units],
        ffn_grads[:, 2 * hidden_units :].T,
    )


def solution(mesh):
    return jax.shard_map(
        body,
        mesh=mesh,
        in_specs=(
            P(("dp", "tensor"), None),
            P("dp", None),
            P("dp"),
            P("dp", "tensor"),
            P("dp", "tensor"),
            P("dp", "tensor"),
            P("tensor", "dp"),
            P("dp"),
            P("dp", "tensor"),
            P("dp", "tensor"),
            P("tensor", "dp"),
            P(("dp", "tensor"), None),
        ),
        out_specs=(
            P(("dp", "tensor"), None),
            P(("dp", "tensor"), None),
            P("dp"),
            P("dp", "tensor"),
            P("dp", "tensor"),
            P("dp", "tensor"),
            P("tensor", "dp"),
            P("dp"),
            P("dp", "tensor"),
            P("dp", "tensor"),
            P("tensor", "dp"),
        ),
        check_vma=False,
    )
```

```python
import functools
import math

import jax
import jax.numpy as jnp
from jax import lax
from jax.experimental import pallas as pl
from jax.experimental.pallas import tpu as pltpu
from jax.sharding import PartitionSpec as P

HEAD_DIM = 64
EPS = 1e-05
ROPE_BASE = 10000.0
NEG_FILL = -1e30
MIB = 1024 * 1024


def seq_layout(row_lengths, places):
    ends = jnp.cumsum(row_lengths)
    starts = ends - row_lengths
    segment = jnp.sum((places[:, None] >= ends[None, :]).astype(jnp.int32), axis=1)
    owner = segment[:, None] == jnp.arange(row_lengths.shape[0], dtype=jnp.int32)[None, :]
    begin = jnp.sum(jnp.where(owner, starts[None, :], 0), axis=1)
    return (segment, places - begin)


def rope_tables(position):
    half = HEAD_DIM // 2
    freqs = ROPE_BASE ** (-(jnp.arange(half, dtype=jnp.float32) * 2.0 / HEAD_DIM))
    angles = freqs[:, None] * position.astype(jnp.float32)[None, :]
    return (jnp.cos(angles), jnp.sin(angles))


def dot(left, right):
    return jnp.dot(left, right, preferred_element_type=jnp.float32)


def inner(left, right):
    return lax.dot_general(
        left, right, (((0,), (0,)), ((), ())), preferred_element_type=jnp.float32
    )


def outer_t(left, right):
    return lax.dot_general(
        left, right, (((1,), (1,)), ((), ())), preferred_element_type=jnp.float32
    )


def norm_back(d_normed, unit, inv, gain):
    scaled = d_normed * gain
    return inv * (scaled - unit * jnp.mean(scaled * unit, -1, keepdims=True))


def swap(block, *pairs):
    return lax.ppermute(block, "tensor", [p for i, j in pairs for p in ((i, j), (j, i))])


def outward(block):
    return lax.ppermute(block, "tensor", [(1, 0), (2, 3)])


def inward(block):
    return lax.ppermute(block, "tensor", [(0, 1), (3, 2)])


def spread(block):
    one, two, three = begin(block)
    return [one, two, three, outward(two)]


def begin(block):
    return swap(block, (0, 1), (2, 3)), swap(block, (0, 2), (1, 3)), swap(block, (1, 2))


def spread_in_turn(block):
    one, two = swap(block, (0, 1), (2, 3)), swap(block, (0, 2), (1, 3))
    return [one, two, swap(after(block, two), (1, 2)), outward(two)]


def is_inner():
    me = lax.axis_index("tensor")
    return ((me == 1) | (me == 2)).astype(jnp.int32).reshape(1)


def collect(parts, *others, early=True):
    far = inward(parts[3])
    if early:
        three = swap(parts[3], (1, 2))
        far, three, parts, *others = lax.optimization_barrier((far, three, parts, *others))
    else:
        far, parts, *others = lax.optimization_barrier((far, parts, *others))
        three = swap(parts[3], (1, 2))
    one = swap(parts[1], (0, 1), (2, 3))
    two = swap(add(parts[2], far), (0, 2), (1, 3))
    return ([parts[0], one, two, three], *others)


def split(total, count):
    rows = total.shape[0] // count
    return [total[k * rows : (k + 1) * rows] for k in range(count)]


def add(left, right):
    return (left.astype(jnp.float32) + right.astype(jnp.float32)).astype(left.dtype)


def after(value, *others):
    return lax.optimization_barrier((value, *others))[0]


SMEM = pl.BlockSpec(memory_space=pltpu.SMEM)
VMEM = pl.BlockSpec(memory_space=pltpu.VMEM)


ANY = pl.BlockSpec(memory_space=pl.ANY)


def fetch(inner_ref, blocks, into, sems):
    if len(blocks) == 1:
        copies = [pltpu.make_async_copy(blocks[0], into, sems.at[0])]
        copies[0].start()
    else:
        rows = blocks[0].shape[0]
        copies = [
            pltpu.make_async_copy(block, into.at[pl.ds(k * rows, rows)], sems.at[k])
            for k, block in enumerate(blocks[:-2])
        ]
        for copy in copies:
            copy.start()
        k = len(copies)
        place = into.at[pl.ds(k * rows, rows)]
        last = [pltpu.make_async_copy(block, place, sems.at[k]) for block in blocks[-2:]]
        pl.when(inner_ref[0] == 1)(last[0].start)
        pl.when(inner_ref[0] != 1)(last[1].start)
        copies.append(last[0])

    def wait():
        for copy in copies:
            copy.wait()

    return wait


def pack_attention(w_query, w_key, w_value, w_output):
    rows = w_query.shape[0]
    widths = [w_query.shape[1], w_key.shape[1], w_value.shape[1], w_output.shape[0]]

    def kernel(query, key, value, output, out, query_in, output_in, sems):
        wait_query = fetch(None, [query], query_in, sems.at[pl.ds(0, 1)])
        wait_output = fetch(None, [output], output_in, sems.at[pl.ds(1, 1)])
        at = query.shape[1]
        pair = jnp.concatenate([key[...], value[...]], 0).T
        out[:, at : at + pair.shape[1]] = pair
        wait_query()
        out[:, :at] = query_in[...]
        wait_output()
        out[:, at + pair.shape[1] :] = output_in[...].T

    return pl.pallas_call(
        kernel,
        out_shape=jax.ShapeDtypeStruct((rows, sum(widths)), w_query.dtype),
        in_specs=[ANY, VMEM, VMEM, ANY],
        scratch_shapes=[
            pltpu.VMEM(w_query.shape, w_query.dtype),
            pltpu.VMEM(w_output.shape, w_query.dtype),
            pltpu.SemaphoreType.DMA((2,)),
        ],
        compiler_params=pltpu.CompilerParams(vmem_limit_bytes=60 * MIB),
    )(w_query, w_key.T, w_value.T, w_output)


LANES = 128


def pack_ffn(w_gate, w_up, w_down):
    rows, units = w_gate.shape

    def kernel(gate, up, down, out, gate_in, up_in, down_in, sems):
        wait_gate = fetch(None, [gate], gate_in, sems.at[pl.ds(0, 1)])
        wait_up = fetch(None, [up], up_in, sems.at[pl.ds(1, 1)])
        wait_down = fetch(None, [down], down_in, sems.at[pl.ds(2, 1)])
        wait_gate()
        for j in range(units // LANES):
            at = j * LANES
            out[:, 2 * at : 2 * at + LANES] = gate_in[:, at : at + LANES]
        wait_up()
        for j in range(units // LANES):
            at = j * LANES
            out[:, 2 * at + LANES : 2 * at + 2 * LANES] = up_in[:, at : at + LANES]
        wait_down()
        out[:, 2 * units :] = down_in[...].T

    return pl.pallas_call(
        kernel,
        out_shape=jax.ShapeDtypeStruct((rows, 3 * units), w_gate.dtype),
        in_specs=[ANY] * 3,
        scratch_shapes=[
            pltpu.VMEM(w_gate.shape, w_gate.dtype),
            pltpu.VMEM(w_up.shape, w_gate.dtype),
            pltpu.VMEM(w_down.shape, w_gate.dtype),
            pltpu.SemaphoreType.DMA((3,)),
        ],
        compiler_params=pltpu.CompilerParams(vmem_limit_bytes=60 * MIB),
    )(w_gate, w_up, w_down)


def unpack_ffn(packed):
    rows, units = packed.shape[0], packed.shape[1] // 3
    f32 = jnp.float32

    def kernel(ref, gate, up, down):
        for j in range(units // LANES):
            at = j * LANES
            gate[:, at : at + LANES] = ref[:, 2 * at : 2 * at + LANES].astype(f32)
            up[:, at : at + LANES] = ref[:, 2 * at + LANES : 2 * at + 2 * LANES].astype(f32)
            down[at : at + LANES] = ref[:, 2 * units + at : 2 * units + at + LANES].T.astype(f32)

    return pl.pallas_call(
        kernel,
        out_shape=(
            jax.ShapeDtypeStruct((rows, units), f32),
            jax.ShapeDtypeStruct((rows, units), f32),
            jax.ShapeDtypeStruct((units, rows), f32),
        ),
        compiler_params=pltpu.CompilerParams(vmem_limit_bytes=24 * MIB),
    )(packed)


def unpack_attention(packed, width, kv_width):
    rows = packed.shape[0]
    f32 = jnp.float32
    ends = [width, width + kv_width, width + 2 * kv_width, 2 * width + 2 * kv_width]

    def kernel(ref, query, key, value, output, gains):
        query[...] = ref[:, : ends[0]].astype(f32)
        pair = ref[:, ends[0] : ends[2]].T.astype(f32)
        key[...] = pair[:kv_width]
        value[...] = pair[kv_width:]
        output[...] = ref[:, ends[2] : ends[3]].T.astype(f32)
        gains[...] = ref[:, ends[3] :].T.astype(f32)[:8]

    return pl.pallas_call(
        kernel,
        out_shape=(
            jax.ShapeDtypeStruct((rows, width), f32),
            jax.ShapeDtypeStruct((kv_width, rows), f32),
            jax.ShapeDtypeStruct((kv_width, rows), f32),
            jax.ShapeDtypeStruct((width, rows), f32),
            jax.ShapeDtypeStruct((8, rows), f32),
        ),
        compiler_params=pltpu.CompilerParams(vmem_limit_bytes=24 * MIB),
    )(packed)


def grads_kernel(kinds, block, inner_ref, *refs):
    refs = list(refs)
    given = []
    for blocks in kinds:
        given.append((refs[:blocks], refs[blocks]))
        del refs[: blocks + 1]
    extras = refs[: -2 * len(kinds) - 2]
    out, *held, sems = refs[len(extras) :]
    step = pl.program_id(0)
    waits = []
    for k, (left, right) in enumerate(given):
        into = (held[2 * k], held[2 * k + 1])

        def start(left=left, right=right, into=into, k=k):
            return (
                fetch(inner_ref, left, into[0], sems.at[k]),
                fetch(inner_ref, [right], into[1], sems.at[k, pl.ds(4, 1)]),
            )

        waits.append(start)

    def dots(first):
        at = 0
        if first:
            pending = [start() for start in waits]
        for k in range(len(given)):
            left, right = held[2 * k], held[2 * k + 1]
            if first:
                for wait in pending[k]:
                    wait()
            width = right.shape[1]
            columns = pl.ds(pl.multiple_of(step * block, block), block)
            out[:, at : at + width] = inner(left[:, columns], right[...]).astype(out.dtype)
            at += width
        for extra in extras:
            out[:, at : at + extra.shape[1]] = extra[...]
            at += extra.shape[1]

    pl.when(step == 0)(lambda: dots(True))
    pl.when(step != 0)(lambda: dots(False))


def grads_of(here, pairs, extras=(), weight=1):
    bf16 = jnp.bfloat16
    pairs = [
        (list(left) if isinstance(left, (list, tuple)) else [left], right) for left, right in pairs
    ]
    rows, depth = pairs[0][1].shape[0], pairs[0][0][0].shape[1]
    block = min(256, depth)
    width = sum(right.shape[1] for _, right in pairs) + sum(e.shape[1] for e in extras)
    given = [each for left, right in pairs for each in (*left, right)]
    held = [
        pltpu.VMEM(shape, bf16) for _, right in pairs for shape in ((rows, depth), right.shape)
    ]
    return pl.pallas_call(
        functools.partial(grads_kernel, [len(left) for left, _ in pairs], block),
        grid=(depth // block,),
        out_shape=jax.ShapeDtypeStruct((depth, width), bf16),
        in_specs=[SMEM]
        + [ANY] * len(given)
        + [pl.BlockSpec((block, e.shape[1]), lambda i: (i, 0)) for e in extras],
        out_specs=pl.BlockSpec((block, width), lambda i: (i, 0)),
        scratch_shapes=[*held, pltpu.SemaphoreType.DMA((len(pairs), 5))],
        cost_estimate=pl.CostEstimate(
            flops=weight * 2 * rows * depth * width,
            bytes_accessed=weight * 2 * (depth * width + rows * width + 2 * rows * depth),
            transcendentals=0,
        ),
        compiler_params=pltpu.CompilerParams(vmem_limit_bytes=60 * MIB),
    )(here, *given, *extras)


def ffn_kernel(side, inner_ref, *refs):
    blocks = 2 if side == 0 else 3
    lefts, (w_pair, w_down) = [refs[:blocks], refs[blocks : 2 * blocks]], refs[2 * blocks :][:2]
    act_ref, d_pair_ref, rows_ref, cot_ref, sems = refs[-5:]

    @pl.when(pl.program_id(0) == 0)
    def _():
        waits = []
        for k, (into, given) in enumerate(zip((rows_ref, cot_ref), lefts)):
            if side == 0:
                rows = given[0].shape[0]
                for half in range(2):
                    place = into.at[pl.ds(half * rows, rows)]
                    waits.append(fetch(inner_ref, [given[half]], place, sems.at[k, pl.ds(half, 1)]))
            else:
                waits.append(fetch(inner_ref, given, into, sems.at[k]))
        for wait in waits:
            wait()

    pairs = dot(rows_ref[...], w_pair[...])
    d_acts = dot(cot_ref[...], w_down[...])
    for k in range(d_acts.shape[1] // LANES):
        at = k * LANES
        gate, up = pairs[:, 2 * at : 2 * at + LANES], pairs[:, 2 * at + LANES : 2 * at + 2 * LANES]
        d_act = d_acts[:, at : at + LANES]
        sigma = jax.nn.sigmoid(gate)
        swish = gate * sigma
        act_ref[:, at : at + LANES] = (swish * up).astype(act_ref.dtype)
        d_gate = d_act * up * (sigma * (1.0 + gate * (1.0 - sigma)))
        d_pair_ref[:, 2 * at : 2 * at + LANES] = d_gate.astype(d_pair_ref.dtype)
        d_pair_ref[:, 2 * at + LANES : 2 * at + 2 * LANES] = (d_act * swish).astype(
            d_pair_ref.dtype
        )


def ffn(side, here, rows, cots, pack, before=()):
    block, depth = rows[0].shape
    units = pack.shape[1] // 3
    wide = 2 * LANES if (2 * units) % (2 * LANES) == 0 else LANES
    bf16 = jnp.bfloat16
    given = [here, *rows, *cots, pack, pack, *before]
    specs = [SMEM] + [ANY] * (len(rows) + len(cots))
    specs.append(pl.BlockSpec((depth, 2 * wide), lambda j: (0, j)))
    specs.append(pl.BlockSpec((depth, wide), lambda j: (0, 2 * units // wide + j)))
    specs += [ANY for _ in before]
    return pl.pallas_call(
        functools.partial(ffn_kernel, side),
        grid=(pl.cdiv(units, wide),),
        out_shape=(
            jax.ShapeDtypeStruct((4 * block, units), bf16),
            jax.ShapeDtypeStruct((4 * block, 2 * units), bf16),
        ),
        in_specs=specs,
        out_specs=(
            pl.BlockSpec((2 * block, wide), lambda j: (side, j)),
            pl.BlockSpec((2 * block, 2 * wide), lambda j: (side, j)),
        ),
        scratch_shapes=[
            pltpu.VMEM((2 * block, depth), bf16),
            pltpu.VMEM((2 * block, depth), bf16),
            pltpu.SemaphoreType.DMA((2, 2)),
        ],
        input_output_aliases={len(given) - 2: 0, len(given) - 1: 1} if before else {},
        cost_estimate=pl.CostEstimate(
            flops=4 * block * depth * 3 * units,
            bytes_accessed=2 * (depth * 3 * units + 4 * block * depth + 6 * block * units),
            transcendentals=2 * block * units,
        ),
        compiler_params=pltpu.CompilerParams(vmem_limit_bytes=60 * MIB),
    )(*given)


def sum_of(parts):
    total = parts[0].astype(jnp.float32)
    for part in parts[1:]:
        total = total + part.astype(jnp.float32)
    return total


def turn(block, cosine, sine):
    half = HEAD_DIM // 2
    first, second = block[:half], block[half:]
    return jnp.concatenate([first * cosine - second * sine, second * cosine + first * sine], 0)

def mask_bias(row_ref, col_ref, bias):
    allowed = (col_ref[:, 0:1] == row_ref[0:1, :]) & (col_ref[:, 1:2] <= row_ref[1:2, :])
    bias[...] = jnp.where(allowed, 0.0, NEG_FILL)

def attend_kernel(q_width, kv_width, inner_ref, own, one, two, three, far, gain_ref, pack_ref, cos_ref, sin_ref, row_ref, col_ref,
                  out_ref, normed_ref, heads_ref, attended_ref, sums_ref, bias, rows_ref, pack, sems):
    bf16 = jnp.bfloat16
    scale = 1.0 / math.sqrt(HEAD_DIM)
    q_heads, kv_heads = q_width // HEAD_DIM, kv_width // HEAD_DIM
    qkv = q_width + 2 * kv_width
    wait_rows = fetch(inner_ref, (own, one, two, three, far), rows_ref, sems)
    wait_pack = fetch(inner_ref, [pack_ref], pack, sems.at[pl.ds(4, 1)])
    mask_bias(row_ref, col_ref, bias)
    wait_rows()
    x = rows_ref[...].astype(jnp.float32)
    inv = lax.rsqrt(jnp.mean(x * x, -1, keepdims=True) + EPS)
    normed_ref[...] = (x * inv * gain_ref[...]).astype(bf16)
    wait_pack()
    cosine, sine = cos_ref[...], sin_ref[...]
    heads = dot(normed_ref[...], pack[:, :qkv]).T
    for h in range(q_heads + kv_heads):
        at = h * HEAD_DIM
        turned = turn(heads[at : at + HEAD_DIM], cosine, sine).astype(bf16)
        heads_ref[at : at + HEAD_DIM] = turned * bf16(scale) if h < q_heads else turned
    heads_ref[q_width + kv_width :] = heads[q_width + kv_width :].astype(bf16)
    parts = []
    for h in range(q_heads):
        c = h * kv_heads // q_heads
        at = q_width + c * HEAD_DIM
        key = heads_ref[at : at + HEAD_DIM].T
        value_t = heads_ref[at + kv_width : at + kv_width + HEAD_DIM]
        scores = dot(key, heads_ref[h * HEAD_DIM : (h + 1) * HEAD_DIM]) + bias[...]
        top = jnp.max(scores, 0, keepdims=True)
        raised = jnp.exp(scores - top)
        total = jnp.sum(raised, 0, keepdims=True)
        sums_ref[h : h + 1] = top + jnp.log(total)
        parts.append(dot(value_t, raised.astype(bf16)) / total)
    attended_ref[...] = jnp.concatenate(parts, 0).T.astype(bf16)
    out_ref[...] = outer_t(attended_ref[...], pack[:, qkv:]).astype(bf16)

def attend(here, blocks, gain, pack, cosine, sine, row, col, q_width, kv_width):
    rows, depth = 4 * blocks[0].shape[0], blocks[0].shape[1]
    bf16 = jnp.bfloat16
    qkv = q_width + 2 * kv_width
    return pl.pallas_call(
        functools.partial(attend_kernel, q_width, kv_width),
        out_shape=(
            jax.ShapeDtypeStruct((rows, depth), bf16),
            jax.ShapeDtypeStruct((rows, depth), bf16),
            jax.ShapeDtypeStruct((qkv, rows), bf16),
            jax.ShapeDtypeStruct((rows, q_width), bf16),
            jax.ShapeDtypeStruct((q_width // HEAD_DIM, rows), jnp.float32),
        ),
        in_specs=[SMEM] + [ANY] * 5 + [VMEM, ANY] + [VMEM] * 4,
        scratch_shapes=[
            pltpu.VMEM((rows, rows), jnp.float32),
            pltpu.VMEM((rows, depth), bf16),
            pltpu.VMEM(pack.shape, bf16),
            pltpu.SemaphoreType.DMA((5,)),
        ],
        cost_estimate=pl.CostEstimate(
            flops=2 * rows * depth * (qkv + q_width) + 4 * rows * rows * q_width,
            bytes_accessed=2 * (3 * rows * depth + depth * (qkv + q_width)),
            transcendentals=rows * rows * q_width // HEAD_DIM,
        ),
        compiler_params=pltpu.CompilerParams(vmem_limit_bytes=60 * MIB),
    )(here, *blocks, gain, pack, cosine, sine, row, col)

def attend_back_kernel(q_width, kv_width, inner_ref, own, one, two, three, far, normed_ref, gain_ref, pack_ref, cos_ref, sin_ref, row_ref, col_ref,
                       heads_ref, sums_ref, out_ref, d_qkv_ref, gain_part_ref, bias, d_att_t, d_heads_t,
                       rows_ref, normed, pack, sems):
    bf16 = jnp.bfloat16
    scale = 1.0 / math.sqrt(HEAD_DIM)
    q_heads, kv_heads = q_width // HEAD_DIM, kv_width // HEAD_DIM
    qkv = q_width + 2 * kv_width
    wait_rows = fetch(inner_ref, (own, one, two, three, far), rows_ref, sems)
    wait_pack = fetch(inner_ref, [pack_ref], pack, sems.at[pl.ds(4, 1)])
    wait_normed = fetch(inner_ref, [normed_ref], normed, sems.at[pl.ds(5, 1)])
    mask_bias(row_ref, col_ref, bias)
    wait_rows()
    wait_pack()
    d_att_t[...] = dot(rows_ref[...], pack[:, qkv:]).T.astype(bf16)
    cosine, sine = cos_ref[...], sin_ref[...]
    for c in range(kv_heads):
        at = q_width + c * HEAD_DIM
        key_t = heads_ref[at : at + HEAD_DIM]
        key = key_t.T
        value = heads_ref[at + kv_width : at + kv_width + HEAD_DIM].T
        d_key = d_value = 0.0
        for h in range(c * q_heads // kv_heads, (c + 1) * q_heads // kv_heads):
            query_t = heads_ref[h * HEAD_DIM : (h + 1) * HEAD_DIM]
            d_out_t = d_att_t[h * HEAD_DIM : (h + 1) * HEAD_DIM]
            prob = jnp.exp(dot(key, query_t) + bias[...] - sums_ref[h : h + 1])
            d_prob = dot(value, d_out_t)
            delta = jnp.sum(prob * d_prob, 0, keepdims=True)
            d_scores = (prob * (d_prob - delta)).astype(bf16)
            d_value = d_value + outer_t(prob.astype(bf16), d_out_t)
            d_key = d_key + outer_t(d_scores, query_t)
            d_query = dot(key_t, d_scores) * scale
            d_heads_t[h * HEAD_DIM : (h + 1) * HEAD_DIM] = turn(d_query, cosine, -sine)
        d_heads_t[at : at + HEAD_DIM] = turn(d_key.T, cosine, -sine)
        d_heads_t[at + kv_width : at + kv_width + HEAD_DIM] = d_value.T
    d_qkv_ref[...] = d_heads_t[...].T.astype(bf16)
    d_normed = outer_t(d_qkv_ref[...], pack[:, :qkv])
    wait_normed()
    out_ref[...] = d_normed.astype(bf16)
    with_gain = jnp.sum(d_normed * normed[...].astype(jnp.float32), 0, keepdims=True)
    gain_part_ref[...] = with_gain / gain_ref[...]

def attend_back(here, blocks, normed, gain, pack, cosine, sine, row, col, heads, sums, q_width, kv_width):
    rows, depth = normed.shape
    bf16 = jnp.bfloat16
    qkv = q_width + 2 * kv_width
    return pl.pallas_call(
        functools.partial(attend_back_kernel, q_width, kv_width),
        out_shape=(
            jax.ShapeDtypeStruct((rows, depth), bf16),
            jax.ShapeDtypeStruct((rows, qkv), bf16),
            jax.ShapeDtypeStruct((1, depth), jnp.float32),
        ),
        in_specs=[SMEM] + [ANY] * 6 + [VMEM, ANY] + [VMEM] * 6,
        scratch_shapes=[
            pltpu.VMEM((rows, rows), jnp.float32),
            pltpu.VMEM((q_width, rows), bf16),
            pltpu.VMEM((qkv, rows), jnp.float32),
            pltpu.VMEM((rows, depth), bf16),
            pltpu.VMEM((rows, depth), bf16),
            pltpu.VMEM(pack.shape, bf16),
            pltpu.SemaphoreType.DMA((6,)),
        ],
        cost_estimate=pl.CostEstimate(
            flops=2 * rows * depth * (qkv + q_width) + 10 * rows * rows * q_width,
            bytes_accessed=2 * (3 * rows * depth + depth * (qkv + q_width)),
            transcendentals=rows * rows * q_width // HEAD_DIM,
        ),
        compiler_params=pltpu.CompilerParams(vmem_limit_bytes=60 * MIB),
    )(here, *blocks, normed, gain, pack, cosine, sine, row, col, heads, sums)


def body(
    tokens,
    lengths,
    attn_gain,
    w_query,
    w_key,
    w_value,
    w_output,
    ffn_gain,
    w_gate,
    w_up,
    w_down,
    cotangent,
):
    bf16 = jnp.bfloat16
    count = lax.axis_size("tensor")
    local_rows = tokens.shape[0]
    width = w_query.shape[1]
    kv_width = w_key.shape[1]
    hidden_units = w_gate.shape[1]
    here = is_inner()

    token_rows = spread(tokens)
    attn_pack = lax.all_gather(
        pack_attention(w_query, w_key, w_value, w_output), "dp", axis=0, tiled=True
    )
    gains = lax.all_gather(
        jnp.stack([attn_gain, ffn_gain])[None], "dp", axis=0, tiled=True
    ).astype(jnp.float32)
    gain_one = gains[:, 0].reshape(1, -1)
    gain_two = gains[:, 1].reshape(1, -1)
    ffn_pack = lax.all_gather(pack_ffn(w_gate, w_up, w_down), "dp", axis=0, tiled=True)
    cot_own, token_rows = lax.optimization_barrier((cotangent, token_rows))
    cot_rows = list(begin(cot_own))
    full_pair = ffn_pack[:, : 2 * hidden_units]
    full_down = ffn_pack[:, 2 * hidden_units :]

    order = lax.axis_index("tensor") ^ jnp.arange(count, dtype=jnp.int32)
    places = (order[:, None] * local_rows + jnp.arange(local_rows, dtype=jnp.int32)[None]).reshape(
        -1
    )
    segment, position = seq_layout(lengths[0], places)
    cosine, sine = rope_tables(position)
    as_row = jnp.stack([segment, places])
    as_column = jnp.stack([segment, places], 1)
    out_total, normed_one, heads, attended, log_sums = attend(
        here,
        [tokens, *token_rows],
        gain_one,
        attn_pack,
        cosine,
        sine,
        as_row,
        as_column,
        width,
        kv_width,
    )
    out_parts, cot_rows = collect(split(out_total, count), cot_rows, early=False)
    cot_rows.append(outward(cot_rows[1]))
    out_parts, cot_rows = lax.optimization_barrier((out_parts, cot_rows))
    resid = tokens.astype(jnp.float32)
    hidden = resid + sum_of(out_parts)

    inv_two = lax.rsqrt(jnp.mean(hidden * hidden, -1, keepdims=True) + EPS)
    unit_two = hidden * inv_two
    own_two = (unit_two * gain_two).astype(bf16)
    two_rows = spread_in_turn(own_two)
    near = ffn(0, here, [own_two, two_rows[0]], [cotangent, cot_rows[0]], ffn_pack)
    activation, d_pair = ffn(1, here, two_rows[1:], cot_rows[1:], ffn_pack, near)
    half = 2 * local_rows
    two_parts = split(outer_t(d_pair[half:], full_pair).astype(bf16), 2)
    two_parts = split(outer_t(d_pair[:half], full_pair).astype(bf16), 2) + two_parts
    two_parts, activation, d_pair = collect(two_parts, activation, d_pair)
    ffn_local = grads_of(
        here, [([own_two, *two_rows], d_pair), ([cotangent, *cot_rows], activation)]
    )
    down_total = outer_t(activation, full_down).astype(bf16)
    two_parts, ffn_local, down_total = lax.optimization_barrier((two_parts, ffn_local, down_total))
    ffn_grads = lax.psum_scatter(ffn_local, "dp", scatter_dimension=0, tiled=True)
    d_normed_two = sum_of(two_parts)

    gain_two_part = jnp.sum(d_normed_two * unit_two, 0)
    d_hidden = cotangent.astype(jnp.float32) + norm_back(d_normed_two, unit_two, inv_two, gain_two)
    own_back = d_hidden.astype(bf16)
    back_rows = spread_in_turn(own_back)
    down_parts, back_rows = collect(
        split(after(down_total, back_rows[1]), count), back_rows, early=False
    )
    one_total, d_qkv, gain_one_part = attend_back(
        here,
        [own_back, *back_rows],
        normed_one,
        gain_one,
        attn_pack,
        cosine,
        sine,
        as_row,
        as_column,
        heads,
        log_sums,
        width,
        kv_width,
    )
    one_total, down_parts = lax.optimization_barrier((one_total, down_parts))
    gain_parts = jnp.stack([gain_one_part[0], gain_two_part])
    gain_parts = sum_of(
        [gain_parts]
        + [
            lax.ppermute(gain_parts, "tensor", [(i, (i + k) % count) for i in range(count)])
            for k in range(1, count)
        ]
    )
    attn_local = grads_of(
        here,
        [(normed_one, d_qkv), ([own_back, *back_rows], attended)],
        [jnp.pad(gain_parts.T.astype(bf16), ((0, 0), (0, 126)))],
        weight=0,
    )
    one_total, attn_local = lax.optimization_barrier((one_total, attn_local))
    (one_parts,) = collect(split(one_total, count))
    attn_local, ffn_grads = lax.optimization_barrier((attn_local, ffn_grads))
    attn_grads = lax.psum_scatter(attn_local, "dp", scatter_dimension=0, tiled=True)
    ffn_grads = unpack_ffn(ffn_grads)
    block_out = (hidden + sum_of(down_parts)).astype(bf16)
    one_parts, ffn_grads, block_out = lax.optimization_barrier((one_parts, ffn_grads, block_out))
    inv_one = lax.rsqrt(jnp.mean(resid * resid, -1, keepdims=True) + EPS)
    grad_tokens = (
        d_hidden + norm_back(sum_of(one_parts), resid * inv_one, inv_one, gain_one)
    ).astype(bf16)
    grad_query, grad_key, grad_value, grad_output, gain_grads = unpack_attention(
        attn_grads, width, kv_width
    )
    return (
        block_out,
        grad_tokens,
        gain_grads[0],
        grad_query,
        grad_key.T,
        grad_value.T,
        grad_output,
        gain_grads[1],
        *ffn_grads,
    )


def solution(mesh):
    return jax.shard_map(
        body,
        mesh=mesh,
        in_specs=(
            P(("dp", "tensor"), None),
            P("dp", None),
            P("dp"),
            P("dp", "tensor"),
            P("dp", "tensor"),
            P("dp", "tensor"),
            P("tensor", "dp"),
            P("dp"),
            P("dp", "tensor"),
            P("dp", "tensor"),
            P("tensor", "dp"),
            P(("dp", "tensor"), None),
        ),
        out_specs=(
            P(("dp", "tensor"), None),
            P(("dp", "tensor"), None),
            P("dp"),
            P("dp", "tensor"),
            P("dp", "tensor"),
            P("dp", "tensor"),
            P("tensor", "dp"),
            P("dp"),
            P("dp", "tensor"),
            P("dp", "tensor"),
            P("tensor", "dp"),
        ),
        check_vma=False,
    )
```

```python
import functools
import math

import jax
import jax.numpy as jnp
from jax import lax
from jax.experimental import pallas as pl
from jax.experimental.pallas import tpu as pltpu
from jax.sharding import PartitionSpec as P

HEAD_DIM = 64
EPS = 1e-05
ROPE_BASE = 10000.0
NEG_FILL = -1e30
MIB = 1024 * 1024


def seq_layout(row_lengths, places):
    ends = jnp.cumsum(row_lengths)
    starts = ends - row_lengths
    segment = jnp.sum((places[:, None] >= ends[None, :]).astype(jnp.int32), axis=1)
    owner = segment[:, None] == jnp.arange(row_lengths.shape[0], dtype=jnp.int32)[None, :]
    begin = jnp.sum(jnp.where(owner, starts[None, :], 0), axis=1)
    return (segment, places - begin)


def rope_tables(position):
    half = HEAD_DIM // 2
    freqs = ROPE_BASE ** (-(jnp.arange(half, dtype=jnp.float32) * 2.0 / HEAD_DIM))
    angles = freqs[:, None] * position.astype(jnp.float32)[None, :]
    return (jnp.cos(angles), jnp.sin(angles))


def dot(left, right):
    return jnp.dot(left, right, preferred_element_type=jnp.float32)


def inner(left, right):
    return lax.dot_general(
        left, right, (((0,), (0,)), ((), ())), preferred_element_type=jnp.float32
    )


def outer_t(left, right):
    return lax.dot_general(
        left, right, (((1,), (1,)), ((), ())), preferred_element_type=jnp.float32
    )


def norm_back(d_normed, unit, inv, gain):
    scaled = d_normed * gain
    return inv * (scaled - unit * jnp.mean(scaled * unit, -1, keepdims=True))


def swap(block, *pairs):
    return lax.ppermute(block, "tensor", [p for i, j in pairs for p in ((i, j), (j, i))])


def outward(block):
    return lax.ppermute(block, "tensor", [(1, 0), (2, 3)])


def inward(block):
    return lax.ppermute(block, "tensor", [(0, 1), (3, 2)])


def beside(block):
    return swap(block, (0, 1), (2, 3))


def between(block):
    return swap(block, (1, 2))


def apart(block):
    return swap(block, (0, 2), (1, 3))


def spread(block):
    one, two, three = beside(block), apart(block), between(block)
    return [one, two, (three, outward(two))]


def spread_in_turn(block):
    one, two = beside(block), apart(block)
    return [one, two, (between(after(block, two)), outward(two))]


def position():
    me = lax.axis_index("tensor")
    inner_one = ((me == 1) | (me == 2)).astype(jnp.int32)
    return jnp.stack([inner_one, lax.axis_index("dp")])


def collect(parts, *others):
    far, three = inward(parts[3]), between(parts[3])
    far, three, parts, *others = lax.optimization_barrier((far, three, parts, *others))
    return ([parts[0], beside(parts[1]), apart(add(parts[2], far)), three], *others)


def split(total, count):
    rows = total.shape[0] // count
    return [total[k * rows : (k + 1) * rows] for k in range(count)]


def add(left, right):
    return (left.astype(jnp.float32) + right.astype(jnp.float32)).astype(left.dtype)


def after(value, *others):
    return lax.optimization_barrier((value, *others))[0]


SMEM = pl.BlockSpec(memory_space=pltpu.SMEM)
VMEM = pl.BlockSpec(memory_space=pltpu.VMEM)


ANY = pl.BlockSpec(memory_space=pl.ANY)


def fetch(here, blocks, into, sems):
    copies, at = [], 0
    for k, block in enumerate(blocks):
        choices = block if isinstance(block, tuple) else (block,)
        rows = choices[0].shape[0]
        place = into.at[pl.ds(at, rows)]
        options = [pltpu.make_async_copy(each, place, sems.at[k]) for each in choices]
        if len(options) == 1:
            options[0].start()
        else:
            pl.when(here[0] == 1)(options[0].start)
            pl.when(here[0] != 1)(options[1].start)
        copies.append(options[0])
        at += rows

    def wait():
        for copy in copies:
            copy.wait()

    return wait


def flat(blocks):
    return [each for block in blocks for each in (block if isinstance(block, tuple) else (block,))]


def shaped(refs, blocks):
    refs = iter(refs)
    return [
        tuple(next(refs) for _ in block) if isinstance(block, tuple) else next(refs)
        for block in blocks
    ]


def pack_attention(w_query, w_key, w_value, w_output):
    rows = w_query.shape[0]
    widths = [w_query.shape[1], w_key.shape[1], w_value.shape[1], w_output.shape[0]]

    def kernel(query, key, value, output, out, query_in, output_in, sems):
        wait_query = fetch(None, [query], query_in, sems.at[pl.ds(0, 1)])
        wait_output = fetch(None, [output], output_in, sems.at[pl.ds(1, 1)])
        at = query.shape[1]
        pair = jnp.concatenate([key[...], value[...]], 0).T
        out[:, at : at + pair.shape[1]] = pair
        wait_query()
        out[:, :at] = query_in[...]
        wait_output()
        out[:, at + pair.shape[1] :] = output_in[...].T

    return pl.pallas_call(
        kernel,
        out_shape=jax.ShapeDtypeStruct((rows, sum(widths)), w_query.dtype),
        in_specs=[ANY, VMEM, VMEM, ANY],
        scratch_shapes=[
            pltpu.VMEM(w_query.shape, w_query.dtype),
            pltpu.VMEM(w_output.shape, w_query.dtype),
            pltpu.SemaphoreType.DMA((2,)),
        ],
        compiler_params=pltpu.CompilerParams(vmem_limit_bytes=60 * MIB),
    )(w_query, w_key.T, w_value.T, w_output)


LANES = 128


def pack_ffn(w_gate, w_up, w_down):
    rows, units = w_gate.shape

    def kernel(gate, up, down, out, gate_in, up_in, down_in, sems):
        wait_gate = fetch(None, [gate], gate_in, sems.at[pl.ds(0, 1)])
        wait_up = fetch(None, [up], up_in, sems.at[pl.ds(1, 1)])
        wait_down = fetch(None, [down], down_in, sems.at[pl.ds(2, 1)])
        wait_gate()
        for j in range(units // LANES):
            at = j * LANES
            out[:, 2 * at : 2 * at + LANES] = gate_in[:, at : at + LANES]
        wait_up()
        for j in range(units // LANES):
            at = j * LANES
            out[:, 2 * at + LANES : 2 * at + 2 * LANES] = up_in[:, at : at + LANES]
        wait_down()
        out[:, 2 * units :] = down_in[...].T

    return pl.pallas_call(
        kernel,
        out_shape=jax.ShapeDtypeStruct((rows, 3 * units), w_gate.dtype),
        in_specs=[ANY] * 3,
        scratch_shapes=[
            pltpu.VMEM(w_gate.shape, w_gate.dtype),
            pltpu.VMEM(w_up.shape, w_gate.dtype),
            pltpu.VMEM(w_down.shape, w_gate.dtype),
            pltpu.SemaphoreType.DMA((3,)),
        ],
        compiler_params=pltpu.CompilerParams(vmem_limit_bytes=60 * MIB),
    )(w_gate, w_up, w_down)


def across(block, step):
    return lax.ppermute(block, "dp", [(i, i ^ step) for i in range(lax.axis_size("dp"))])


def pair_sum(other, own):
    return split(add(own, across(other, 1)), lax.axis_size("dp") // 2)


def scatter_sum(blocks):
    return [blocks[0]] + [across(blocks[m], 2 * m) for m in range(1, len(blocks))]


def unpack_ffn(packed):
    rows, units = packed.shape[0], packed.shape[1] // 3
    f32 = jnp.float32

    def kernel(ref, gate, up, down):
        for j in range(units // LANES):
            at = j * LANES
            gate[:, at : at + LANES] = ref[:, 2 * at : 2 * at + LANES].astype(f32)
            up[:, at : at + LANES] = ref[:, 2 * at + LANES : 2 * at + 2 * LANES].astype(f32)
            down[at : at + LANES] = ref[:, 2 * units + at : 2 * units + at + LANES].T.astype(f32)

    return pl.pallas_call(
        kernel,
        out_shape=(
            jax.ShapeDtypeStruct((rows, units), f32),
            jax.ShapeDtypeStruct((rows, units), f32),
            jax.ShapeDtypeStruct((units, rows), f32),
        ),
        compiler_params=pltpu.CompilerParams(vmem_limit_bytes=24 * MIB),
    )(packed)


def unpack_attention(parts, width, kv_width):
    rows = parts[0].shape[0]
    f32 = jnp.float32
    ends = [width, width + kv_width, width + 2 * kv_width, 2 * width + 2 * kv_width]

    def kernel(*refs):
        (query, key, value, output, gains), refs = refs[-5:], refs[:-5]

        def columns(at, end):
            return sum_of([ref[:, at:end] for ref in refs])

        query[...] = columns(0, ends[0])
        pair = columns(ends[0], ends[2]).T
        key[...] = pair[:kv_width]
        value[...] = pair[kv_width:]
        output[...] = columns(ends[2], ends[3]).T
        gains[...] = columns(ends[3], ends[3] + LANES).T[:8]

    return pl.pallas_call(
        kernel,
        out_shape=(
            jax.ShapeDtypeStruct((rows, width), f32),
            jax.ShapeDtypeStruct((kv_width, rows), f32),
            jax.ShapeDtypeStruct((kv_width, rows), f32),
            jax.ShapeDtypeStruct((width, rows), f32),
            jax.ShapeDtypeStruct((8, rows), f32),
        ),
        compiler_params=pltpu.CompilerParams(vmem_limit_bytes=24 * MIB),
    )(*parts)


def grads_kernel(lefts, block, here, *refs):
    refs = list(refs)
    given = []
    for blocks in lefts:
        count = len(flat(blocks))
        given.append((shaped(refs[:count], blocks), refs[count]))
        del refs[: count + 1]
    out, *held, sems = refs
    step = pl.program_id(0)

    def dots(first):
        at = 0
        if first:
            waits = [
                (
                    fetch(here, left, held[2 * k], sems.at[k]),
                    fetch(here, [right], held[2 * k + 1], sems.at[k, pl.ds(4, 1)]),
                )
                for k, (left, right) in enumerate(given)
            ]
        for k in range(len(given)):
            left, right = held[2 * k], held[2 * k + 1]
            if first:
                for wait in waits[k]:
                    wait()
            width = right.shape[1]
            columns = pl.ds(pl.multiple_of(step * block, block), block)
            out[:, at : at + width] = inner(left[:, columns], right[...]).astype(out.dtype)
            at += width

    pl.when(step == 0)(lambda: dots(True))
    pl.when(step != 0)(lambda: dots(False))


def grads_of(here, pairs):
    bf16 = jnp.bfloat16
    rows, depth = pairs[0][1].shape[0], flat(pairs[0][0])[0].shape[1]
    block = min(256, depth)
    width = sum(right.shape[1] for _, right in pairs)
    given = [each for left, right in pairs for each in (*flat(left), right)]
    held = [
        pltpu.VMEM(shape, bf16) for _, right in pairs for shape in ((rows, depth), right.shape)
    ]
    return pl.pallas_call(
        functools.partial(grads_kernel, [left for left, _ in pairs], block),
        grid=(depth // block,),
        out_shape=jax.ShapeDtypeStruct((depth, width), bf16),
        in_specs=[SMEM] + [ANY] * len(given),
        out_specs=pl.BlockSpec((block, width), lambda i: (i, 0)),
        scratch_shapes=[*held, pltpu.SemaphoreType.DMA((len(pairs), 5))],
        cost_estimate=pl.CostEstimate(
            flops=2 * rows * depth * width,
            bytes_accessed=2 * (depth * width + rows * width + 2 * rows * depth),
            transcendentals=0,
        ),
        compiler_params=pltpu.CompilerParams(vmem_limit_bytes=60 * MIB),
    )(here, *given)


def ffn_kernel(shapes, here, *refs):
    refs = list(refs)
    lefts = []
    for blocks in shapes:
        count = len(flat(blocks))
        lefts.append(shaped(refs[:count], blocks))
        del refs[:count]
    w_pair, w_down = refs[:2]
    act_ref, d_pair_ref, rows_ref, cot_ref, sems = refs[-5:]

    @pl.when(pl.program_id(0) == 0)
    def _():
        waits = [
            fetch(here, given, into, sems.at[k])
            for k, (into, given) in enumerate(zip((rows_ref, cot_ref), lefts))
        ]
        for wait in waits:
            wait()

    pairs = dot(rows_ref[...], w_pair[...])
    d_acts = dot(cot_ref[...], w_down[...])
    for k in range(d_acts.shape[1] // LANES):
        at = k * LANES
        gate, up = pairs[:, 2 * at : 2 * at + LANES], pairs[:, 2 * at + LANES : 2 * at + 2 * LANES]
        d_act = d_acts[:, at : at + LANES]
        sigma = jax.nn.sigmoid(gate)
        swish = gate * sigma
        act_ref[:, at : at + LANES] = (swish * up).astype(act_ref.dtype)
        d_gate = d_act * up * (sigma * (1.0 + gate * (1.0 - sigma)))
        d_pair_ref[:, 2 * at : 2 * at + LANES] = d_gate.astype(d_pair_ref.dtype)
        d_pair_ref[:, 2 * at + LANES : 2 * at + 2 * LANES] = (d_act * swish).astype(
            d_pair_ref.dtype
        )


def ffn(side, here, rows, cots, pack, before=()):
    block, depth = flat(rows)[0].shape
    units = pack.shape[1] // 3
    wide = 2 * LANES if (2 * units) % (2 * LANES) == 0 else LANES
    bf16 = jnp.bfloat16
    given = [here, *flat(rows), *flat(cots), pack, pack, *before]
    specs = [SMEM] + [ANY] * (len(given) - 3 - len(before))
    specs.append(pl.BlockSpec((depth, 2 * wide), lambda j: (0, j)))
    specs.append(pl.BlockSpec((depth, wide), lambda j: (0, 2 * units // wide + j)))
    specs += [ANY for _ in before]
    return pl.pallas_call(
        functools.partial(ffn_kernel, (rows, cots)),
        grid=(pl.cdiv(units, wide),),
        out_shape=(
            jax.ShapeDtypeStruct((4 * block, units), bf16),
            jax.ShapeDtypeStruct((4 * block, 2 * units), bf16),
        ),
        in_specs=specs,
        out_specs=(
            pl.BlockSpec((2 * block, wide), lambda j: (side, j)),
            pl.BlockSpec((2 * block, 2 * wide), lambda j: (side, j)),
        ),
        scratch_shapes=[
            pltpu.VMEM((2 * block, depth), bf16),
            pltpu.VMEM((2 * block, depth), bf16),
            pltpu.SemaphoreType.DMA((2, 2)),
        ],
        input_output_aliases={len(given) - 2: 0, len(given) - 1: 1} if before else {},
        cost_estimate=pl.CostEstimate(
            flops=4 * block * depth * 3 * units,
            bytes_accessed=2 * (depth * 3 * units + 4 * block * depth + 6 * block * units),
            transcendentals=2 * block * units,
        ),
        compiler_params=pltpu.CompilerParams(vmem_limit_bytes=60 * MIB),
    )(*given)


def sum_of(parts):
    total = parts[0].astype(jnp.float32)
    for part in parts[1:]:
        total = total + part.astype(jnp.float32)
    return total


def turn(block, cosine, sine):
    half = HEAD_DIM // 2
    first, second = block[:half], block[half:]
    return jnp.concatenate([first * cosine - second * sine, second * cosine + first * sine], 0)

def mask_bias(row_ref, col_ref, bias):
    allowed = (col_ref[:, 0:1] == row_ref[0:1, :]) & (col_ref[:, 1:2] <= row_ref[1:2, :])
    bias[...] = jnp.where(allowed, 0.0, NEG_FILL)

def attend_kernel(q_width, kv_width, here, own, one, two, three, far, gain_ref, pack_ref, cos_ref,
                  sin_ref, row_ref, col_ref, out_0, out_1, out_2, out_3, normed_ref, heads_ref,
                  attended_ref, sums_ref, bias, rows_ref, pack, sems):
    bf16 = jnp.bfloat16
    scale = 1.0 / math.sqrt(HEAD_DIM)
    q_heads, kv_heads = q_width // HEAD_DIM, kv_width // HEAD_DIM
    qkv = q_width + 2 * kv_width
    wait_rows = fetch(here, (own, one, two, (three, far)), rows_ref, sems)
    wait_pack = fetch(here, [pack_ref], pack, sems.at[pl.ds(4, 1)])
    mask_bias(row_ref, col_ref, bias)
    wait_rows()
    x = rows_ref[...].astype(jnp.float32)
    inv = lax.rsqrt(jnp.mean(x * x, -1, keepdims=True) + EPS)
    normed_ref[...] = (x * inv * gain_ref[...]).astype(bf16)
    wait_pack()
    cosine, sine = cos_ref[...], sin_ref[...]
    heads = dot(normed_ref[...], pack[:, :qkv]).T
    for h in range(q_heads + kv_heads):
        at = h * HEAD_DIM
        turned = turn(heads[at : at + HEAD_DIM], cosine, sine).astype(bf16)
        heads_ref[at : at + HEAD_DIM] = turned * bf16(scale) if h < q_heads else turned
    heads_ref[q_width + kv_width :] = heads[q_width + kv_width :].astype(bf16)
    parts = []
    for h in range(q_heads):
        c = h * kv_heads // q_heads
        at = q_width + c * HEAD_DIM
        key = heads_ref[at : at + HEAD_DIM].T
        value_t = heads_ref[at + kv_width : at + kv_width + HEAD_DIM]
        scores = dot(key, heads_ref[h * HEAD_DIM : (h + 1) * HEAD_DIM]) + bias[...]
        top = jnp.max(scores, 0, keepdims=True)
        raised = jnp.exp(scores - top)
        total = jnp.sum(raised, 0, keepdims=True)
        sums_ref[h : h + 1] = top + jnp.log(total)
        parts.append(dot(value_t, raised.astype(bf16)) / total)
    attended_ref[...] = jnp.concatenate(parts, 0).T.astype(bf16)
    for k, out in enumerate((out_0, out_1, out_2, out_3)):
        rows = out.shape[0]
        out[...] = outer_t(attended_ref[k * rows : (k + 1) * rows], pack[:, qkv:]).astype(bf16)

def attend(here, blocks, gain, pack, cosine, sine, row, col, q_width, kv_width):
    rows, depth = 4 * blocks[0].shape[0], blocks[0].shape[1]
    bf16 = jnp.bfloat16
    qkv = q_width + 2 * kv_width
    return pl.pallas_call(
        functools.partial(attend_kernel, q_width, kv_width),
        out_shape=(
            *[jax.ShapeDtypeStruct((rows // 4, depth), bf16)] * 4,
            jax.ShapeDtypeStruct((rows, depth), bf16),
            jax.ShapeDtypeStruct((qkv, rows), bf16),
            jax.ShapeDtypeStruct((rows, q_width), bf16),
            jax.ShapeDtypeStruct((q_width // HEAD_DIM, rows), jnp.float32),
        ),
        in_specs=[SMEM] + [ANY] * 5 + [VMEM, ANY] + [VMEM] * 4,
        scratch_shapes=[
            pltpu.VMEM((rows, rows), jnp.float32),
            pltpu.VMEM((rows, depth), bf16),
            pltpu.VMEM(pack.shape, bf16),
            pltpu.SemaphoreType.DMA((5,)),
        ],
        cost_estimate=pl.CostEstimate(
            flops=2 * rows * depth * (qkv + q_width) + 4 * rows * rows * q_width,
            bytes_accessed=2 * (3 * rows * depth + depth * (qkv + q_width)),
            transcendentals=rows * rows * q_width // HEAD_DIM,
        ),
        compiler_params=pltpu.CompilerParams(vmem_limit_bytes=60 * MIB),
    )(here, *flat(blocks), gain, pack, cosine, sine, row, col)

def attend_back_kernel(q_width, kv_width, owners, here, own, one, two, three, far, normed_ref,
                       gain_ref, pack_ref, cos_ref, sin_ref, row_ref, col_ref, heads_ref, sums_ref,
                       attended_ref, gain_two_ref, out_0, out_1, out_2, out_3, other_ref, own_ref,
                       bias, d_att_t, d_heads_t, rows_ref, normed, pack, out, d_qkv, gain_rows,
                       gain_columns, lefts, blocks, sems, out_sems):
    bf16 = jnp.bfloat16
    scale = 1.0 / math.sqrt(HEAD_DIM)
    q_heads, kv_heads = q_width // HEAD_DIM, kv_width // HEAD_DIM
    qkv = q_width + 2 * kv_width
    wait_rows = fetch(here, (own, one, two, (three, far)), rows_ref, sems)
    wait_pack = fetch(here, [pack_ref], pack, sems.at[pl.ds(4, 1)])
    wait_normed = fetch(here, [normed_ref], normed, sems.at[pl.ds(5, 1)])
    mask_bias(row_ref, col_ref, bias)
    wait_rows()
    wait_pack()
    d_att_t[...] = dot(rows_ref[...], pack[:, qkv:]).T.astype(bf16)
    cosine, sine = cos_ref[...], sin_ref[...]
    for c in range(kv_heads):
        at = q_width + c * HEAD_DIM
        key_t = heads_ref[at : at + HEAD_DIM]
        key = key_t.T
        value = heads_ref[at + kv_width : at + kv_width + HEAD_DIM].T
        d_key = d_value = 0.0
        for h in range(c * q_heads // kv_heads, (c + 1) * q_heads // kv_heads):
            query_t = heads_ref[h * HEAD_DIM : (h + 1) * HEAD_DIM]
            d_out_t = d_att_t[h * HEAD_DIM : (h + 1) * HEAD_DIM]
            prob = jnp.exp(dot(key, query_t) + bias[...] - sums_ref[h : h + 1])
            d_prob = dot(value, d_out_t)
            delta = jnp.sum(prob * d_prob, 0, keepdims=True)
            d_scores = (prob * (d_prob - delta)).astype(bf16)
            d_value = d_value + outer_t(prob.astype(bf16), d_out_t)
            d_key = d_key + outer_t(d_scores, query_t)
            d_query = dot(key_t, d_scores) * scale
            d_heads_t[h * HEAD_DIM : (h + 1) * HEAD_DIM] = turn(d_query, cosine, -sine)
        d_heads_t[at : at + HEAD_DIM] = turn(d_key.T, cosine, -sine)
        d_heads_t[at + kv_width : at + kv_width + HEAD_DIM] = d_value.T
    d_qkv[...] = d_heads_t[...].T.astype(bf16)
    d_normed = outer_t(d_qkv[...], pack[:, :qkv])
    out[...] = d_normed.astype(bf16)
    pending = []
    for k, part in enumerate((out_0, out_1, out_2, out_3)):
        rows = part.shape[0]
        pending.append(
            pltpu.make_async_copy(out.at[pl.ds(k * rows, rows)], part, out_sems.at[4 + k])
        )
        pending[-1].start()

    wait_normed()
    gain_rows[...] = jnp.zeros_like(gain_rows)
    with_gain = jnp.sum(d_normed * normed[...].astype(jnp.float32), 0, keepdims=True)
    gain_rows[0:1] = with_gain / gain_ref[...]
    gain_rows[1:2] = gain_two_ref[...]
    gain_columns[...] = gain_rows[...].T.astype(bf16)
    lefts[0] = normed[...].T
    lefts[1] = rows_ref[...].T
    block = lefts.shape[1] // owners
    for half, target in enumerate((other_ref, own_ref)):

        def step(m, carry, half=half, target=target):
            owner = here[1] ^ (1 - half) ^ (2 * m)
            rows = pl.ds(pl.multiple_of(owner * block, block), block)
            slot = 2 * half + m % 2
            copy = pltpu.make_async_copy(
                blocks.at[slot], target.at[pl.ds(m * block, block)], out_sems.at[slot]
            )
            pl.when(m >= 2)(copy.wait)
            blocks[slot, :, :qkv] = dot(lefts[0, rows], d_qkv[...]).astype(bf16)
            blocks[slot, :, qkv : qkv + q_width] = dot(lefts[1, rows], attended_ref[...]).astype(
                bf16
            )
            blocks[slot, :, qkv + q_width :] = gain_columns[rows]
            copy.start()
            return carry

        lax.fori_loop(0, owners // 2, step, 0)
        for slot in (2 * half, 2 * half + 1):
            pending.append(
                pltpu.make_async_copy(
                    blocks.at[slot], target.at[pl.ds(0, block)], out_sems.at[slot]
                )
            )
    for copy in pending:
        copy.wait()


def attend_back(
    here,
    blocks,
    normed,
    gain,
    pack,
    cosine,
    sine,
    row,
    col,
    heads,
    sums,
    attended,
    gain_two,
    owners,
    q_width,
    kv_width,
):
    rows, depth = normed.shape
    bf16 = jnp.bfloat16
    f32 = jnp.float32
    qkv = q_width + 2 * kv_width
    width = qkv + q_width + LANES
    return pl.pallas_call(
        functools.partial(attend_back_kernel, q_width, kv_width, owners),
        out_shape=(
            *[jax.ShapeDtypeStruct((rows // 4, depth), bf16)] * 4,
            jax.ShapeDtypeStruct((depth // 2, width), bf16),
            jax.ShapeDtypeStruct((depth // 2, width), bf16),
        ),
        in_specs=[SMEM] + [ANY] * 6 + [VMEM, ANY] + [VMEM] * 8,
        out_specs=[ANY] * 6,
        scratch_shapes=[
            pltpu.VMEM((rows, rows), f32),
            pltpu.VMEM((q_width, rows), bf16),
            pltpu.VMEM((qkv, rows), f32),
            pltpu.VMEM((rows, depth), bf16),
            pltpu.VMEM((rows, depth), bf16),
            pltpu.VMEM(pack.shape, bf16),
            pltpu.VMEM((rows, depth), bf16),
            pltpu.VMEM((rows, qkv), bf16),
            pltpu.VMEM((LANES, depth), f32),
            pltpu.VMEM((depth, LANES), bf16),
            pltpu.VMEM((2, depth, rows), bf16),
            pltpu.VMEM((4, depth // owners, width), bf16),
            pltpu.SemaphoreType.DMA((6,)),
            pltpu.SemaphoreType.DMA((8,)),
        ],
        cost_estimate=pl.CostEstimate(
            flops=4 * rows * depth * (qkv + q_width) + 10 * rows * rows * q_width,
            bytes_accessed=2 * (3 * rows * depth + 2 * depth * (qkv + q_width)),
            transcendentals=rows * rows * q_width // HEAD_DIM,
        ),
        compiler_params=pltpu.CompilerParams(vmem_limit_bytes=60 * MIB),
    )(
        here,
        *flat(blocks),
        normed,
        gain,
        pack,
        cosine,
        sine,
        row,
        col,
        heads,
        sums,
        attended,
        gain_two,
    )


def body(
    tokens,
    lengths,
    attn_gain,
    w_query,
    w_key,
    w_value,
    w_output,
    ffn_gain,
    w_gate,
    w_up,
    w_down,
    cotangent,
):
    bf16 = jnp.bfloat16
    count = lax.axis_size("tensor")
    local_rows = tokens.shape[0]
    width = w_query.shape[1]
    kv_width = w_key.shape[1]
    hidden_units = w_gate.shape[1]
    here = position()

    token_rows = spread(tokens)
    attn_pack = lax.all_gather(
        pack_attention(w_query, w_key, w_value, w_output), "dp", axis=0, tiled=True
    )
    gains = lax.all_gather(
        jnp.stack([attn_gain, ffn_gain])[None], "dp", axis=0, tiled=True
    ).astype(jnp.float32)
    gain_one = gains[:, 0].reshape(1, -1)
    gain_two = gains[:, 1].reshape(1, -1)
    ffn_pack = lax.all_gather(pack_ffn(w_gate, w_up, w_down), "dp", axis=0, tiled=True)
    cot_own, token_rows = lax.optimization_barrier((cotangent, token_rows))
    cot_one, cot_three = beside(cot_own), between(cot_own)
    full_pair = ffn_pack[:, : 2 * hidden_units]
    full_down = ffn_pack[:, 2 * hidden_units :]

    order = lax.axis_index("tensor") ^ jnp.arange(count, dtype=jnp.int32)
    places = (order[:, None] * local_rows + jnp.arange(local_rows, dtype=jnp.int32)[None]).reshape(
        -1
    )
    segment, offset = seq_layout(lengths[0], places)
    cosine, sine = rope_tables(offset)
    as_row = jnp.stack([segment, places])
    as_column = jnp.stack([segment, places], 1)
    *parts, normed_one, heads, attended, log_sums = attend(
        here,
        [tokens, *token_rows],
        gain_one,
        attn_pack,
        cosine,
        sine,
        as_row,
        as_column,
        width,
        kv_width,
    )
    parts, cot_one, cot_three = lax.optimization_barrier((parts, cot_one, cot_three))
    far, cot_two, cot_near = inward(parts[3]), between(cot_one), outward(cot_three)
    parts, far, cot_two, cot_near = lax.optimization_barrier((parts, far, cot_two, cot_near))
    near, two, cot_far = inward(parts[2]), between(add(parts[2], far)), outward(cot_two)
    parts, near, two, cot_far = lax.optimization_barrier((parts, near, two, cot_far))
    three, one = between(add(parts[3], near)), beside(add(parts[1], two))
    cot_rows = [cotangent, cot_one, (cot_two, cot_near), (cot_three, cot_far)]
    resid = tokens.astype(jnp.float32)
    hidden = resid + sum_of([parts[0], one, three])

    inv_two = lax.rsqrt(jnp.mean(hidden * hidden, -1, keepdims=True) + EPS)
    unit_two = hidden * inv_two
    own_two = (unit_two * gain_two).astype(bf16)
    two_rows = spread_in_turn(own_two)
    two_rows = [own_two, *two_rows]
    halfway = ffn(0, here, two_rows[:2], cot_rows[:2], ffn_pack)
    activation, d_pair = ffn(1, here, two_rows[2:], cot_rows[2:], ffn_pack, halfway)
    half = 2 * local_rows
    two_parts = split(outer_t(d_pair[half:], full_pair).astype(bf16), 2)
    two_parts = split(outer_t(d_pair[:half], full_pair).astype(bf16), 2) + two_parts
    two_parts, activation, d_pair = collect(two_parts, activation, d_pair)
    ffn_local = grads_of(
        here, [(two_rows, d_pair), (cot_rows, activation)]
    )
    down_total = outer_t(activation, full_down).astype(bf16)
    two_parts, ffn_local, down_total = lax.optimization_barrier((two_parts, ffn_local, down_total))
    ffn_grads = lax.psum_scatter(ffn_local, "dp", scatter_dimension=0, tiled=True)
    d_normed_two = sum_of(two_parts)

    gain_two_part = jnp.sum(d_normed_two * unit_two, 0, keepdims=True)
    d_hidden = cotangent.astype(jnp.float32) + norm_back(d_normed_two, unit_two, inv_two, gain_two)
    own_back = d_hidden.astype(bf16)
    back_rows = spread_in_turn(own_back)
    parts = split(after(down_total, back_rows[1]), count)
    far = inward(parts[3])
    parts, far, back_rows = lax.optimization_barrier((parts, far, back_rows))
    near, two = inward(parts[2]), between(add(parts[2], far))
    *one_total, other_local, own_local = attend_back(
        here,
        [own_back, *back_rows],
        normed_one,
        gain_one,
        attn_pack,
        cosine,
        sine,
        as_row,
        as_column,
        heads,
        log_sums,
        attended,
        gain_two_part,
        lax.axis_size("dp"),
        width,
        kv_width,
    )
    one_total, outer, inner_sum = lax.optimization_barrier(
        (one_total, add(parts[1], two), add(parts[3], near))
    )
    block_out = (hidden + sum_of([parts[0], beside(outer), between(inner_sum)])).astype(bf16)
    one_parts, block_out = collect(one_total, block_out)
    attn_pairs = pair_sum(other_local, own_local)
    attn_parts = scatter_sum(attn_pairs)
    ffn_grads = unpack_ffn(ffn_grads)
    attn_parts, ffn_grads = lax.optimization_barrier((attn_parts, ffn_grads))
    inv_one = lax.rsqrt(jnp.mean(resid * resid, -1, keepdims=True) + EPS)
    grad_tokens = (
        d_hidden + norm_back(sum_of(one_parts), resid * inv_one, inv_one, gain_one)
    ).astype(bf16)
    grad_query, grad_key, grad_value, grad_output, gain_grads = unpack_attention(
        attn_parts, width, kv_width
    )
    gain_grads = sum_of(
        [gain_grads]
        + [
            lax.ppermute(gain_grads, "tensor", [(i, (i + k) % count) for i in range(count)])
            for k in range(1, count)
        ]
    )
    return (
        block_out,
        grad_tokens,
        gain_grads[0],
        grad_query,
        grad_key.T,
        grad_value.T,
        grad_output,
        gain_grads[1],
        *ffn_grads,
    )


def solution(mesh):
    return jax.shard_map(
        body,
        mesh=mesh,
        in_specs=(
            P(("dp", "tensor"), None),
            P("dp", None),
            P("dp"),
            P("dp", "tensor"),
            P("dp", "tensor"),
            P("dp", "tensor"),
            P("tensor", "dp"),
            P("dp"),
            P("dp", "tensor"),
            P("dp", "tensor"),
            P("tensor", "dp"),
            P(("dp", "tensor"), None),
        ),
        out_specs=(
            P(("dp", "tensor"), None),
            P(("dp", "tensor"), None),
            P("dp"),
            P("dp", "tensor"),
            P("dp", "tensor"),
            P("dp", "tensor"),
            P("tensor", "dp"),
            P("dp"),
            P("dp", "tensor"),
            P("dp", "tensor"),
            P("tensor", "dp"),
        ),
        check_vma=False,
    )
```

```python
import functools
import math

import jax
import jax.numpy as jnp
from jax import lax
from jax.experimental import pallas as pl
from jax.experimental.pallas import tpu as pltpu
from jax.sharding import PartitionSpec as P

HEAD_DIM = 64
EPS = 1e-05
ROPE_BASE = 10000.0
NEG_FILL = -1e30
MIB = 1024 * 1024


def seq_layout(row_lengths, places):
    ends = jnp.cumsum(row_lengths)
    starts = ends - row_lengths
    segment = jnp.sum((places[:, None] >= ends[None, :]).astype(jnp.int32), axis=1)
    owner = segment[:, None] == jnp.arange(row_lengths.shape[0], dtype=jnp.int32)[None, :]
    begin = jnp.sum(jnp.where(owner, starts[None, :], 0), axis=1)
    return (segment, places - begin)


def rope_tables(position):
    half = HEAD_DIM // 2
    freqs = ROPE_BASE ** (-(jnp.arange(half, dtype=jnp.float32) * 2.0 / HEAD_DIM))
    angles = freqs[:, None] * position.astype(jnp.float32)[None, :]
    return (jnp.cos(angles), jnp.sin(angles))


def dot(left, right):
    return jnp.dot(left, right, preferred_element_type=jnp.float32)


def inner(left, right):
    return lax.dot_general(
        left, right, (((0,), (0,)), ((), ())), preferred_element_type=jnp.float32
    )


def outer_t(left, right):
    return lax.dot_general(
        left, right, (((1,), (1,)), ((), ())), preferred_element_type=jnp.float32
    )


def norm_back(d_normed, unit, inv, gain):
    scaled = d_normed * gain
    return inv * (scaled - unit * jnp.mean(scaled * unit, -1, keepdims=True))


def swap(block, *pairs):
    return lax.ppermute(block, "tensor", [p for i, j in pairs for p in ((i, j), (j, i))])


def outward(block):
    return lax.ppermute(block, "tensor", [(1, 0), (2, 3)])


def inward(block):
    return lax.ppermute(block, "tensor", [(0, 1), (3, 2)])


def beside(block):
    return swap(block, (0, 1), (2, 3))


def between(block):
    return swap(block, (1, 2))


def apart(block):
    return swap(block, (0, 2), (1, 3))


def spread(block):
    one, two, three = beside(block), apart(block), between(block)
    return [one, two, (three, outward(two))]


def spread_in_turn(block):
    one, two = beside(block), apart(block)
    return [one, two, (between(after(block, two)), outward(two))]


def position():
    me = lax.axis_index("tensor")
    inner_one = ((me == 1) | (me == 2)).astype(jnp.int32)
    return jnp.stack([inner_one, lax.axis_index("dp"), me])


def collect(parts, *others):
    far, three = inward(parts[3]), between(parts[3])
    far, three, parts, *others = lax.optimization_barrier((far, three, parts, *others))
    return ([parts[0], beside(parts[1]), apart(add(parts[2], far)), three], *others)


def split(total, count):
    rows = total.shape[0] // count
    return [total[k * rows : (k + 1) * rows] for k in range(count)]


def add(left, right):
    return (left.astype(jnp.float32) + right.astype(jnp.float32)).astype(left.dtype)


def after(value, *others):
    return lax.optimization_barrier((value, *others))[0]


SMEM = pl.BlockSpec(memory_space=pltpu.SMEM)
VMEM = pl.BlockSpec(memory_space=pltpu.VMEM)


ANY = pl.BlockSpec(memory_space=pl.ANY)


def rows_of(here, k, rows):
    return pl.ds(pl.multiple_of((here[2] ^ k) * rows, rows), rows)


def fetch(here, blocks, into, sems, in_order=False):
    copies, at = [], 0
    for k, block in enumerate(blocks):
        choices = block if isinstance(block, tuple) else (block,)
        rows = choices[0].shape[0]
        place = into.at[rows_of(here, k, rows) if in_order else pl.ds(at, rows)]
        options = [pltpu.make_async_copy(each, place, sems.at[k]) for each in choices]
        if len(options) == 1:
            options[0].start()
        else:
            pl.when(here[0] == 1)(options[0].start)
            pl.when(here[0] != 1)(options[1].start)
        copies.append(options[0])
        at += rows

    def wait():
        for copy in copies:
            copy.wait()

    return wait


def flat(blocks):
    return [each for block in blocks for each in (block if isinstance(block, tuple) else (block,))]


def shaped(refs, blocks):
    refs = iter(refs)
    return [
        tuple(next(refs) for _ in block) if isinstance(block, tuple) else next(refs)
        for block in blocks
    ]


def pack_attention(w_query, w_key, w_value, w_output):
    rows = w_query.shape[0]
    widths = [w_query.shape[1], w_key.shape[1], w_value.shape[1], w_output.shape[0]]

    def kernel(query, key, value, output, out, query_in, output_in, sems):
        wait_query = fetch(None, [query], query_in, sems.at[pl.ds(0, 1)])
        wait_output = fetch(None, [output], output_in, sems.at[pl.ds(1, 1)])
        at = query.shape[1]
        pair = jnp.concatenate([key[...], value[...]], 0).T
        out[:, at : at + pair.shape[1]] = pair
        wait_query()
        out[:, :at] = query_in[...]
        wait_output()
        out[:, at + pair.shape[1] :] = output_in[...].T

    return pl.pallas_call(
        kernel,
        out_shape=jax.ShapeDtypeStruct((rows, sum(widths)), w_query.dtype),
        in_specs=[ANY, VMEM, VMEM, ANY],
        scratch_shapes=[
            pltpu.VMEM(w_query.shape, w_query.dtype),
            pltpu.VMEM(w_output.shape, w_query.dtype),
            pltpu.SemaphoreType.DMA((2,)),
        ],
        compiler_params=pltpu.CompilerParams(vmem_limit_bytes=60 * MIB),
    )(w_query, w_key.T, w_value.T, w_output)


LANES = 128


def pack_ffn(w_gate, w_up, w_down):
    rows, units = w_gate.shape

    def kernel(gate, up, down, out, gate_in, up_in, down_in, sems):
        wait_gate = fetch(None, [gate], gate_in, sems.at[pl.ds(0, 1)])
        wait_up = fetch(None, [up], up_in, sems.at[pl.ds(1, 1)])
        wait_down = fetch(None, [down], down_in, sems.at[pl.ds(2, 1)])
        wait_gate()
        for j in range(units // LANES):
            at = j * LANES
            out[:, 2 * at : 2 * at + LANES] = gate_in[:, at : at + LANES]
        wait_up()
        for j in range(units // LANES):
            at = j * LANES
            out[:, 2 * at + LANES : 2 * at + 2 * LANES] = up_in[:, at : at + LANES]
        wait_down()
        out[:, 2 * units :] = down_in[...].T

    return pl.pallas_call(
        kernel,
        out_shape=jax.ShapeDtypeStruct((rows, 3 * units), w_gate.dtype),
        in_specs=[ANY] * 3,
        scratch_shapes=[
            pltpu.VMEM(w_gate.shape, w_gate.dtype),
            pltpu.VMEM(w_up.shape, w_gate.dtype),
            pltpu.VMEM(w_down.shape, w_gate.dtype),
            pltpu.SemaphoreType.DMA((3,)),
        ],
        compiler_params=pltpu.CompilerParams(vmem_limit_bytes=60 * MIB),
    )(w_gate, w_up, w_down)


def across(block, step):
    return lax.ppermute(block, "dp", [(i, i ^ step) for i in range(lax.axis_size("dp"))])


def pair_sum(other, own):
    return split(add(own, across(other, 1)), lax.axis_size("dp") // 2)


def scatter_sum(blocks):
    return [blocks[0]] + [across(blocks[m], 2 * m) for m in range(1, len(blocks))]


def unpack_ffn(packed, w_gate, w_up, gain):
    rows, units = packed.shape[0], packed.shape[1] // 3
    f32 = jnp.float32

    def kernel(ref, gate_in, up_in, gain_ref, gate, up, down, gain_out):
        total = jnp.zeros((rows, LANES), f32)
        for j in range(units // LANES):
            at = j * LANES
            span = slice(at, at + LANES)
            d_gate = ref[:, 2 * at : 2 * at + LANES].astype(f32)
            d_up = ref[:, 2 * at + LANES : 2 * at + 2 * LANES].astype(f32)
            total += d_gate * gate_in[:, span].astype(f32) + d_up * up_in[:, span].astype(f32)
            gate[:, span] = d_gate
            up[:, span] = d_up
            down[span] = ref[:, 2 * units + at : 2 * units + at + LANES].T.astype(f32)
        gain_out[...] = jnp.zeros_like(gain_out)
        gain_out[0:1] = jnp.sum(total.T, 0, keepdims=True) / gain_ref[...]

    return pl.pallas_call(
        kernel,
        out_shape=(
            jax.ShapeDtypeStruct((rows, units), f32),
            jax.ShapeDtypeStruct((rows, units), f32),
            jax.ShapeDtypeStruct((units, rows), f32),
            jax.ShapeDtypeStruct((8, rows), f32),
        ),
        compiler_params=pltpu.CompilerParams(vmem_limit_bytes=24 * MIB),
    )(packed, w_gate, w_up, gain)


def unpack_attention(parts, w_query, w_key_t, w_value_t, gain):
    rows, width = w_query.shape
    kv_width = w_key_t.shape[0]
    f32 = jnp.float32
    ends = [width, width + 2 * kv_width, 2 * width + 2 * kv_width]

    def kernel(*refs):
        query, key, value, output, gain_out = refs[-5:]
        query_in, key_in, value_in, gain_ref = refs[-9:-5]
        refs = refs[:-9]

        def columns(at, end):
            return sum_of([ref[:, at:end] for ref in refs])

        total = jnp.zeros((rows, LANES), f32)
        for at in range(0, width, LANES):
            span = slice(at, at + LANES)
            d_query = columns(at, at + LANES)
            query[:, span] = d_query
            total += d_query * query_in[:, span].astype(f32)
        pair = columns(ends[0], ends[1]).T
        key[...] = pair[:kv_width]
        value[...] = pair[kv_width:]
        total = total.T
        both = jnp.sum(total, 0, keepdims=True)
        both += jnp.sum(pair[:kv_width] * key_in[...].astype(f32), 0, keepdims=True)
        both += jnp.sum(pair[kv_width:] * value_in[...].astype(f32), 0, keepdims=True)
        gain_out[...] = jnp.zeros_like(gain_out)
        gain_out[0:1] = both / gain_ref[...]
        output[...] = columns(ends[1], ends[2]).T

    return pl.pallas_call(
        kernel,
        out_shape=(
            jax.ShapeDtypeStruct((rows, width), f32),
            jax.ShapeDtypeStruct((kv_width, rows), f32),
            jax.ShapeDtypeStruct((kv_width, rows), f32),
            jax.ShapeDtypeStruct((width, rows), f32),
            jax.ShapeDtypeStruct((8, rows), f32),
        ),
        compiler_params=pltpu.CompilerParams(vmem_limit_bytes=24 * MIB),
    )(*parts, w_query, w_key_t, w_value_t, gain)


def grads_kernel(lefts, block, here, *refs):
    refs = list(refs)
    given = []
    for blocks in lefts:
        count = len(flat(blocks))
        given.append((shaped(refs[:count], blocks), refs[count]))
        del refs[: count + 1]
    out, *held, sems = refs
    step = pl.program_id(0)

    def dots(first):
        at = 0
        if first:
            waits = [
                (
                    fetch(here, left, held[2 * k], sems.at[k]),
                    fetch(here, [right], held[2 * k + 1], sems.at[k, pl.ds(4, 1)]),
                )
                for k, (left, right) in enumerate(given)
            ]
        for k in range(len(given)):
            left, right = held[2 * k], held[2 * k + 1]
            if first:
                for wait in waits[k]:
                    wait()
            width = right.shape[1]
            columns = pl.ds(pl.multiple_of(step * block, block), block)
            out[:, at : at + width] = inner(left[:, columns], right[...]).astype(out.dtype)
            at += width

    pl.when(step == 0)(lambda: dots(True))
    pl.when(step != 0)(lambda: dots(False))


def grads_of(here, pairs):
    bf16 = jnp.bfloat16
    rows, depth = pairs[0][1].shape[0], flat(pairs[0][0])[0].shape[1]
    block = min(256, depth)
    width = sum(right.shape[1] for _, right in pairs)
    given = [each for left, right in pairs for each in (*flat(left), right)]
    held = [
        pltpu.VMEM(shape, bf16) for _, right in pairs for shape in ((rows, depth), right.shape)
    ]
    return pl.pallas_call(
        functools.partial(grads_kernel, [left for left, _ in pairs], block),
        grid=(depth // block,),
        out_shape=jax.ShapeDtypeStruct((depth, width), bf16),
        in_specs=[SMEM] + [ANY] * len(given),
        out_specs=pl.BlockSpec((block, width), lambda i: (i, 0)),
        scratch_shapes=[*held, pltpu.SemaphoreType.DMA((len(pairs), 5))],
        cost_estimate=pl.CostEstimate(
            flops=2 * rows * depth * width,
            bytes_accessed=2 * (depth * width + rows * width + 2 * rows * depth),
            transcendentals=0,
        ),
        compiler_params=pltpu.CompilerParams(vmem_limit_bytes=60 * MIB),
    )(here, *given)


def ffn_kernel(shapes, here, *refs):
    refs = list(refs)
    lefts = []
    for blocks in shapes:
        count = len(flat(blocks))
        lefts.append(shaped(refs[:count], blocks))
        del refs[:count]
    w_pair, w_down = refs[:2]
    act_ref, d_pair_ref, rows_ref, cot_ref, sems = refs[-5:]

    @pl.when(pl.program_id(0) == 0)
    def _():
        waits = [
            fetch(here, given, into, sems.at[k])
            for k, (into, given) in enumerate(zip((rows_ref, cot_ref), lefts))
        ]
        for wait in waits:
            wait()

    pairs = dot(rows_ref[...], w_pair[...])
    d_acts = dot(cot_ref[...], w_down[...])
    for k in range(d_acts.shape[1] // LANES):
        at = k * LANES
        gate, up = pairs[:, 2 * at : 2 * at + LANES], pairs[:, 2 * at + LANES : 2 * at + 2 * LANES]
        d_act = d_acts[:, at : at + LANES]
        sigma = jax.nn.sigmoid(gate)
        swish = gate * sigma
        act_ref[:, at : at + LANES] = (swish * up).astype(act_ref.dtype)
        d_gate = d_act * up * (sigma * (1.0 + gate * (1.0 - sigma)))
        d_pair_ref[:, 2 * at : 2 * at + LANES] = d_gate.astype(d_pair_ref.dtype)
        d_pair_ref[:, 2 * at + LANES : 2 * at + 2 * LANES] = (d_act * swish).astype(
            d_pair_ref.dtype
        )


def ffn(side, here, rows, cots, pack, before=()):
    block, depth = flat(rows)[0].shape
    units = pack.shape[1] // 3
    wide = 2 * LANES if (2 * units) % (2 * LANES) == 0 else LANES
    bf16 = jnp.bfloat16
    given = [here, *flat(rows), *flat(cots), pack, pack, *before]
    specs = [SMEM] + [ANY] * (len(given) - 3 - len(before))
    specs.append(pl.BlockSpec((depth, 2 * wide), lambda j: (0, j)))
    specs.append(pl.BlockSpec((depth, wide), lambda j: (0, 2 * units // wide + j)))
    specs += [ANY for _ in before]
    return pl.pallas_call(
        functools.partial(ffn_kernel, (rows, cots)),
        grid=(pl.cdiv(units, wide),),
        out_shape=(
            jax.ShapeDtypeStruct((4 * block, units), bf16),
            jax.ShapeDtypeStruct((4 * block, 2 * units), bf16),
        ),
        in_specs=specs,
        out_specs=(
            pl.BlockSpec((2 * block, wide), lambda j: (side, j)),
            pl.BlockSpec((2 * block, 2 * wide), lambda j: (side, j)),
        ),
        scratch_shapes=[
            pltpu.VMEM((2 * block, depth), bf16),
            pltpu.VMEM((2 * block, depth), bf16),
            pltpu.SemaphoreType.DMA((2, 2)),
        ],
        input_output_aliases={len(given) - 2: 0, len(given) - 1: 1} if before else {},
        cost_estimate=pl.CostEstimate(
            flops=4 * block * depth * 3 * units,
            bytes_accessed=2 * (depth * 3 * units + 4 * block * depth + 6 * block * units),
            transcendentals=2 * block * units,
        ),
        compiler_params=pltpu.CompilerParams(vmem_limit_bytes=60 * MIB),
    )(*given)


def sum_of(parts):
    total = parts[0].astype(jnp.float32)
    for part in parts[1:]:
        total = total + part.astype(jnp.float32)
    return total


def turn(block, cosine, sine):
    half = HEAD_DIM // 2
    first, second = block[:half], block[half:]
    return jnp.concatenate([first * cosine - second * sine, second * cosine + first * sine], 0)

WIDE = 640


def spans(rows):
    return [(at, min(at + WIDE, rows)) for at in range(0, rows, WIDE)]


def mask_bias(row_ref, col_ref, bias):
    rows = bias.shape[0]
    for at, end in spans(rows):
        keys = lax.broadcasted_iota(jnp.int32, (end, end - at), 0)
        queries = lax.broadcasted_iota(jnp.int32, (end, end - at), 1) + at
        allowed = (col_ref[:end] == row_ref[:, at:end]) & (keys <= queries)
        bias[:end, at:end] = jnp.where(allowed, 0.0, NEG_FILL)


def attend_kernel(q_width, kv_width, here, own, one, two, three, far, gain_ref, pack_ref, cos_ref,
                  sin_ref, row_ref, col_ref, out_0, out_1, out_2, out_3, normed_out, heads_ref,
                  attended_ref, sums_ref, bias, rows_ref, pack, normed_ref, total, sems, out_sems):
    bf16 = jnp.bfloat16
    scale = 1.0 / math.sqrt(HEAD_DIM)
    q_heads, kv_heads = q_width // HEAD_DIM, kv_width // HEAD_DIM
    qkv = q_width + 2 * kv_width
    wait_rows = fetch(here, (own, one, two, (three, far)), rows_ref, sems, in_order=True)
    wait_pack = fetch(here, [pack_ref], pack, sems.at[pl.ds(4, 1)])
    mask_bias(row_ref, col_ref, bias)
    wait_rows()
    x = rows_ref[...].astype(jnp.float32)
    inv = lax.rsqrt(jnp.mean(x * x, -1, keepdims=True) + EPS)
    normed_ref[...] = (x * inv * gain_ref[...]).astype(bf16)
    pending = [pltpu.make_async_copy(normed_ref, normed_out, out_sems.at[4])]
    pending[0].start()
    wait_pack()
    cosine, sine = cos_ref[...], sin_ref[...]
    heads = dot(normed_ref[...], pack[:, :qkv]).T
    for h in range(q_heads + kv_heads):
        at = h * HEAD_DIM
        turned = turn(heads[at : at + HEAD_DIM], cosine, sine).astype(bf16)
        heads_ref[at : at + HEAD_DIM] = turned * bf16(scale) if h < q_heads else turned
    heads_ref[q_width + kv_width :] = heads[q_width + kv_width :].astype(bf16)
    keys = [
        heads_ref[at : at + HEAD_DIM].T
        for at in range(q_width, q_width + kv_width, HEAD_DIM)
    ]
    for start, end in spans(x.shape[0]):
        parts = []
        for h in range(q_heads):
            c = h * kv_heads // q_heads
            at = q_width + kv_width + c * HEAD_DIM
            query_t = heads_ref[h * HEAD_DIM : (h + 1) * HEAD_DIM, start:end]
            scores = dot(keys[c][:end], query_t) + bias[:end, start:end]
            top = jnp.max(scores, 0, keepdims=True)
            raised = jnp.exp(scores - top)
            raised_sum = jnp.sum(raised, 0, keepdims=True)
            sums_ref[h : h + 1, start:end] = top + jnp.log(raised_sum)
            value_t = heads_ref[at : at + HEAD_DIM, :end]
            parts.append(dot(value_t, raised.astype(bf16)) / raised_sum)
        attended_ref[start:end] = jnp.concatenate(parts, 0).T.astype(bf16)
    total[...] = outer_t(attended_ref[...], pack[:, qkv:]).astype(bf16)
    for k, out in enumerate((out_0, out_1, out_2, out_3)):
        rows = rows_of(here, k, out.shape[0])
        pending.append(pltpu.make_async_copy(total.at[rows], out, out_sems.at[k]))
        pending[-1].start()
    for copy in pending:
        copy.wait()


def attend(here, blocks, gain, pack, cosine, sine, row, col, q_width, kv_width):
    rows, depth = 4 * blocks[0].shape[0], blocks[0].shape[1]
    bf16 = jnp.bfloat16
    qkv = q_width + 2 * kv_width
    return pl.pallas_call(
        functools.partial(attend_kernel, q_width, kv_width),
        out_shape=(
            *[jax.ShapeDtypeStruct((rows // 4, depth), bf16)] * 4,
            jax.ShapeDtypeStruct((rows, depth), bf16),
            jax.ShapeDtypeStruct((qkv, rows), bf16),
            jax.ShapeDtypeStruct((rows, q_width), bf16),
            jax.ShapeDtypeStruct((q_width // HEAD_DIM, rows), jnp.float32),
        ),
        in_specs=[SMEM] + [ANY] * 5 + [VMEM, ANY] + [VMEM] * 4,
        out_specs=[ANY] * 5 + [VMEM] * 3,
        scratch_shapes=[
            pltpu.VMEM((rows, rows), jnp.float32),
            pltpu.VMEM((rows, depth), bf16),
            pltpu.VMEM(pack.shape, bf16),
            pltpu.VMEM((rows, depth), bf16),
            pltpu.VMEM((rows, depth), bf16),
            pltpu.SemaphoreType.DMA((5,)),
            pltpu.SemaphoreType.DMA((5,)),
        ],
        cost_estimate=pl.CostEstimate(
            flops=2 * rows * depth * (qkv + q_width) + 4 * rows * rows * q_width,
            bytes_accessed=2 * (3 * rows * depth + depth * (qkv + q_width)),
            transcendentals=rows * rows * q_width // HEAD_DIM,
        ),
        compiler_params=pltpu.CompilerParams(vmem_limit_bytes=60 * MIB),
    )(here, *flat(blocks), gain, pack, cosine, sine, row, col)

def attend_back_kernel(q_width, kv_width, owners, here, own, one, two, three, far, normed_ref, pack_ref,
                       cos_ref, sin_ref, row_ref, col_ref, heads_ref, sums_ref, attended_ref, out_0,
                       out_1, out_2, out_3, other_ref, own_ref, bias, d_att_t, d_heads_t, d_keys,
                       rows_ref, normed, pack, out, d_qkv, lefts, blocks, sems, out_sems):
    bf16 = jnp.bfloat16
    scale = 1.0 / math.sqrt(HEAD_DIM)
    q_heads, kv_heads = q_width // HEAD_DIM, kv_width // HEAD_DIM
    qkv = q_width + 2 * kv_width
    wait_rows = fetch(here, (own, one, two, (three, far)), rows_ref, sems, in_order=True)
    wait_pack = fetch(here, [pack_ref], pack, sems.at[pl.ds(4, 1)])
    wait_normed = fetch(here, [normed_ref], normed, sems.at[pl.ds(5, 1)])
    mask_bias(row_ref, col_ref, bias)
    wait_rows()
    wait_pack()
    d_att_t[...] = dot(rows_ref[...], pack[:, qkv:]).T.astype(bf16)
    for c in range(kv_heads):
        at = q_width + c * HEAD_DIM
        key_t = heads_ref[at : at + HEAD_DIM]
        key = key_t.T
        value = heads_ref[at + kv_width : at + kv_width + HEAD_DIM].T
        d_keys[...] = jnp.zeros_like(d_keys)
        for start, end in spans(key.shape[0]):
            d_key = d_value = 0.0
            cosine, sine = cos_ref[:, start:end], sin_ref[:, start:end]
            for h in range(c * q_heads // kv_heads, (c + 1) * q_heads // kv_heads):
                head = slice(h * HEAD_DIM, (h + 1) * HEAD_DIM)
                query_t = heads_ref[head, start:end]
                d_out_t = d_att_t[head, start:end]
                prob = jnp.exp(
                    dot(key[:end], query_t) + bias[:end, start:end] - sums_ref[h : h + 1, start:end]
                )
                d_prob = dot(value[:end], d_out_t)
                delta = jnp.sum(prob * d_prob, 0, keepdims=True)
                d_scores = (prob * (d_prob - delta)).astype(bf16)
                d_value = d_value + outer_t(prob.astype(bf16), d_out_t)
                d_key = d_key + outer_t(d_scores, query_t)
                d_query = dot(key_t[:, :end], d_scores) * scale
                d_heads_t[head, start:end] = turn(d_query, cosine, -sine)
            d_keys[0, :end] += d_key
            d_keys[1, :end] += d_value
        d_heads_t[at : at + HEAD_DIM] = turn(d_keys[0].T, cos_ref[...], -sin_ref[...])
        d_heads_t[at + kv_width : at + kv_width + HEAD_DIM] = d_keys[1].T
    d_qkv[...] = d_heads_t[...].T.astype(bf16)
    out[...] = outer_t(d_qkv[...], pack[:, :qkv]).astype(bf16)
    pending = []
    for k, part in enumerate((out_0, out_1, out_2, out_3)):
        rows = rows_of(here, k, part.shape[0])
        pending.append(pltpu.make_async_copy(out.at[rows], part, out_sems.at[4 + k]))
        pending[-1].start()

    wait_normed()
    lefts[0] = normed[...].T
    lefts[1] = rows_ref[...].T
    block = lefts.shape[1] // owners
    for half, target in enumerate((other_ref, own_ref)):

        def step(m, carry, half=half, target=target):
            owner = here[1] ^ (1 - half) ^ (2 * m)
            rows = pl.ds(pl.multiple_of(owner * block, block), block)
            slot = 2 * half + m % 2
            copy = pltpu.make_async_copy(
                blocks.at[slot], target.at[pl.ds(m * block, block)], out_sems.at[slot]
            )
            pl.when(m >= 2)(copy.wait)
            blocks[slot, :, :qkv] = dot(lefts[0, rows], d_qkv[...]).astype(bf16)
            blocks[slot, :, qkv:] = dot(lefts[1, rows], attended_ref[...]).astype(bf16)
            copy.start()
            return carry

        lax.fori_loop(0, owners // 2, step, 0)
        for slot in (2 * half, 2 * half + 1):
            pending.append(
                pltpu.make_async_copy(
                    blocks.at[slot], target.at[pl.ds(0, block)], out_sems.at[slot]
                )
            )
    for copy in pending:
        copy.wait()


def attend_back(
    here,
    blocks,
    normed,
    pack,
    cosine,
    sine,
    row,
    col,
    heads,
    sums,
    attended,
    owners,
    q_width,
    kv_width,
):
    rows, depth = normed.shape
    bf16 = jnp.bfloat16
    f32 = jnp.float32
    qkv = q_width + 2 * kv_width
    width = qkv + q_width
    return pl.pallas_call(
        functools.partial(attend_back_kernel, q_width, kv_width, owners),
        out_shape=(
            *[jax.ShapeDtypeStruct((rows // 4, depth), bf16)] * 4,
            jax.ShapeDtypeStruct((depth // 2, width), bf16),
            jax.ShapeDtypeStruct((depth // 2, width), bf16),
        ),
        in_specs=[SMEM] + [ANY] * 7 + [VMEM] * 7,
        out_specs=[ANY] * 6,
        scratch_shapes=[
            pltpu.VMEM((rows, rows), f32),
            pltpu.VMEM((q_width, rows), bf16),
            pltpu.VMEM((qkv, rows), f32),
            pltpu.VMEM((2, rows, HEAD_DIM), f32),
            pltpu.VMEM((rows, depth), bf16),
            pltpu.VMEM((rows, depth), bf16),
            pltpu.VMEM(pack.shape, bf16),
            pltpu.VMEM((rows, depth), bf16),
            pltpu.VMEM((rows, qkv), bf16),
            pltpu.VMEM((2, depth, rows), bf16),
            pltpu.VMEM((4, depth // owners, width), bf16),
            pltpu.SemaphoreType.DMA((6,)),
            pltpu.SemaphoreType.DMA((8,)),
        ],
        cost_estimate=pl.CostEstimate(
            flops=4 * rows * depth * (qkv + q_width) + 10 * rows * rows * q_width,
            bytes_accessed=2 * (3 * rows * depth + 2 * depth * (qkv + q_width)),
            transcendentals=rows * rows * q_width // HEAD_DIM,
        ),
        compiler_params=pltpu.CompilerParams(vmem_limit_bytes=60 * MIB),
    )(here, *flat(blocks), normed, pack, cosine, sine, row, col, heads, sums, attended)


def back_through_norm(parts, above, rows, gain, low_too=False):
    shape = above.shape
    f32, bf16 = jnp.float32, jnp.bfloat16
    given = [*parts, above, rows]

    def kernel(*refs):
        gain_ref, *refs = refs
        ins, refs = refs[: len(given)], refs[len(given) :]
        outs, held, sems = refs[: 1 + low_too], refs[1 + low_too : -1], refs[-1]
        waits = [
            fetch(None, [ref], into, sems.at[pl.ds(k, 1)])
            for k, (ref, into) in enumerate(zip(ins, held))
        ]
        for wait in waits:
            wait()
        x = held[-1][...].astype(f32)
        inv = lax.rsqrt(jnp.mean(x * x, -1, keepdims=True) + EPS)
        back = norm_back(sum_of([part[...] for part in held[:-2]]), x * inv, inv, gain_ref[...])
        total = held[-2][...].astype(f32) + back
        for out in outs:
            out[...] = total.astype(out.dtype)

    outs = [f32, bf16] if low_too else [bf16]
    return pl.pallas_call(
        kernel,
        out_shape=[jax.ShapeDtypeStruct(shape, each) for each in outs],
        in_specs=[VMEM] + [ANY] * len(given),
        scratch_shapes=[pltpu.VMEM(each.shape, each.dtype) for each in given]
        + [pltpu.SemaphoreType.DMA((len(given),))],
        cost_estimate=pl.CostEstimate(
            flops=20 * shape[0] * shape[1],
            bytes_accessed=sum(each.size * each.dtype.itemsize for each in given),
            transcendentals=shape[0],
        ),
        compiler_params=pltpu.CompilerParams(vmem_limit_bytes=60 * MIB),
    )(gain, *given)


def body(
    tokens,
    lengths,
    attn_gain,
    w_query,
    w_key,
    w_value,
    w_output,
    ffn_gain,
    w_gate,
    w_up,
    w_down,
    cotangent,
):
    bf16 = jnp.bfloat16
    count = lax.axis_size("tensor")
    local_rows = tokens.shape[0]
    width = w_query.shape[1]
    kv_width = w_key.shape[1]
    hidden_units = w_gate.shape[1]
    here = position()

    token_rows = spread(tokens)
    attn_pack = lax.all_gather(
        pack_attention(w_query, w_key, w_value, w_output), "dp", axis=0, tiled=True
    )
    gains = lax.all_gather(
        jnp.stack([attn_gain, ffn_gain])[None], "dp", axis=0, tiled=True
    ).astype(jnp.float32)
    gain_one = gains[:, 0].reshape(1, -1)
    gain_two = gains[:, 1].reshape(1, -1)
    ffn_pack = lax.all_gather(pack_ffn(w_gate, w_up, w_down), "dp", axis=0, tiled=True)
    cot_own, token_rows = lax.optimization_barrier((cotangent, token_rows))
    cot_one, cot_three = beside(cot_own), between(cot_own)
    full_pair = ffn_pack[:, : 2 * hidden_units]
    full_down = ffn_pack[:, 2 * hidden_units :]

    segment, offset = seq_layout(
        lengths[0], jnp.arange(count * local_rows, dtype=jnp.int32)
    )
    cosine, sine = rope_tables(offset)
    as_row, as_column = segment[None], segment[:, None]
    *parts, normed_one, heads, attended, log_sums = attend(
        here,
        [tokens, *token_rows],
        gain_one,
        attn_pack,
        cosine,
        sine,
        as_row,
        as_column,
        width,
        kv_width,
    )
    parts, cot_one, cot_three = lax.optimization_barrier((parts, cot_one, cot_three))
    far, cot_two, cot_near = inward(parts[3]), between(cot_one), outward(cot_three)
    parts, far, cot_two, cot_near = lax.optimization_barrier((parts, far, cot_two, cot_near))
    near, two, cot_far = inward(parts[2]), between(add(parts[2], far)), outward(cot_two)
    parts, near, two, cot_far = lax.optimization_barrier((parts, near, two, cot_far))
    three, one = between(add(parts[3], near)), beside(add(parts[1], two))
    cot_rows = [cotangent, cot_one, (cot_two, cot_near), (cot_three, cot_far)]
    resid = tokens.astype(jnp.float32)
    hidden = resid + sum_of([parts[0], one, three])

    inv_two = lax.rsqrt(jnp.mean(hidden * hidden, -1, keepdims=True) + EPS)
    unit_two = hidden * inv_two
    own_two = (unit_two * gain_two).astype(bf16)
    two_rows = spread_in_turn(own_two)
    two_rows = [own_two, *two_rows]
    halfway = ffn(0, here, two_rows[:2], cot_rows[:2], ffn_pack)
    activation, d_pair = ffn(1, here, two_rows[2:], cot_rows[2:], ffn_pack, halfway)
    half = 2 * local_rows
    two_parts = split(outer_t(d_pair[half:], full_pair).astype(bf16), 2)
    two_parts = split(outer_t(d_pair[:half], full_pair).astype(bf16), 2) + two_parts
    two_parts, activation, d_pair = collect(two_parts, activation, d_pair)
    ffn_local = grads_of(
        here, [(two_rows, d_pair), (cot_rows, activation)]
    )
    two_parts, ffn_local = lax.optimization_barrier((two_parts, ffn_local))
    ffn_grads = lax.psum_scatter(ffn_local, "dp", scatter_dimension=0, tiled=True)

    d_hidden, own_back = back_through_norm(two_parts, cotangent, hidden, gain_two, low_too=True)
    back_rows = spread_in_turn(own_back)
    down_total = outer_t(after(activation, own_back), full_down).astype(bf16)
    parts = split(after(down_total, back_rows[1]), count)
    far = inward(parts[3])
    parts, far, back_rows = lax.optimization_barrier((parts, far, back_rows))
    near, two = inward(parts[2]), between(add(parts[2], far))
    back_rows = [own_back, *back_rows]
    *one_total, other_local, own_local = attend_back(
        here,
        back_rows,
        normed_one,
        attn_pack,
        cosine,
        sine,
        as_row,
        as_column,
        heads,
        log_sums,
        attended,
        lax.axis_size("dp"),
        width,
        kv_width,
    )
    other_local, outer, inner_sum = lax.optimization_barrier(
        (other_local, add(parts[1], two), add(parts[3], near))
    )
    block_out = (hidden + sum_of([parts[0], beside(outer), between(inner_sum)])).astype(bf16)
    (one_parts,) = collect(one_total)
    attn_pairs = pair_sum(other_local, own_local)
    attn_parts = scatter_sum(attn_pairs)
    attn_parts, block_out = lax.optimization_barrier((attn_parts, block_out))
    (grad_tokens,) = back_through_norm(one_parts, d_hidden, tokens, gain_one)
    own_gains = [each.astype(jnp.float32).reshape(1, -1) for each in (attn_gain, ffn_gain)]
    *ffn_grads, ffn_gain_part = unpack_ffn(ffn_grads, w_gate, w_up, own_gains[1])
    attn_parts, ffn_grads = lax.optimization_barrier((attn_parts, ffn_grads))
    grad_query, grad_key, grad_value, grad_output, attn_gain_part = unpack_attention(
        attn_parts, w_query, w_key.T, w_value.T, own_gains[0]
    )
    gain_parts = jnp.concatenate([attn_gain_part[:1], ffn_gain_part[:1]], 0)
    gain_grads = sum_of(
        [gain_parts]
        + [
            lax.ppermute(gain_parts, "tensor", [(i, (i + k) % count) for i in range(count)])
            for k in range(1, count)
        ]
    )
    return (
        block_out,
        grad_tokens,
        gain_grads[0],
        grad_query,
        grad_key.T,
        grad_value.T,
        grad_output,
        gain_grads[1],
        *ffn_grads,
    )


def solution(mesh):
    return jax.shard_map(
        body,
        mesh=mesh,
        in_specs=(
            P(("dp", "tensor"), None),
            P("dp", None),
            P("dp"),
            P("dp", "tensor"),
            P("dp", "tensor"),
            P("dp", "tensor"),
            P("tensor", "dp"),
            P("dp"),
            P("dp", "tensor"),
            P("dp", "tensor"),
            P("tensor", "dp"),
            P(("dp", "tensor"), None),
        ),
        out_specs=(
            P(("dp", "tensor"), None),
            P(("dp", "tensor"), None),
            P("dp"),
            P("dp", "tensor"),
            P("dp", "tensor"),
            P("dp", "tensor"),
            P("tensor", "dp"),
            P("dp"),
            P("dp", "tensor"),
            P("dp", "tensor"),
            P("tensor", "dp"),
        ),
        check_vma=False,
    )
```

```python
import functools
import math

import jax
import jax.numpy as jnp
from jax import lax
from jax.experimental import pallas as pl
from jax.experimental.pallas import tpu as pltpu
from jax.sharding import PartitionSpec as P

HEAD_DIM = 64
EPS = 1e-05
ROPE_BASE = 10000.0
NEG_FILL = -1e30
MIB = 1024 * 1024


def seq_layout(row_lengths, places):
    ends = jnp.cumsum(row_lengths)
    starts = ends - row_lengths
    segment = jnp.sum((places[:, None] >= ends[None, :]).astype(jnp.int32), axis=1)
    owner = segment[:, None] == jnp.arange(row_lengths.shape[0], dtype=jnp.int32)[None, :]
    begin = jnp.sum(jnp.where(owner, starts[None, :], 0), axis=1)
    return (segment, places - begin)


def rope_tables(position):
    half = HEAD_DIM // 2
    freqs = ROPE_BASE ** (-(jnp.arange(half, dtype=jnp.float32) * 2.0 / HEAD_DIM))
    angles = freqs[:, None] * position.astype(jnp.float32)[None, :]
    return (jnp.cos(angles), jnp.sin(angles))


def dot(left, right):
    return jnp.dot(left, right, preferred_element_type=jnp.float32)


def inner(left, right):
    return lax.dot_general(
        left, right, (((0,), (0,)), ((), ())), preferred_element_type=jnp.float32
    )


def outer_t(left, right):
    return lax.dot_general(
        left, right, (((1,), (1,)), ((), ())), preferred_element_type=jnp.float32
    )


def norm_back(d_normed, unit, inv, gain):
    scaled = d_normed * gain
    return inv * (scaled - unit * jnp.mean(scaled * unit, -1, keepdims=True))


def swap(block, *pairs):
    return lax.ppermute(block, "tensor", [p for i, j in pairs for p in ((i, j), (j, i))])


def outward(block):
    return lax.ppermute(block, "tensor", [(1, 0), (2, 3)])


def inward(block):
    return lax.ppermute(block, "tensor", [(0, 1), (3, 2)])


def beside(block):
    return swap(block, (0, 1), (2, 3))


def between(block):
    return swap(block, (1, 2))


def apart(block):
    return swap(block, (0, 2), (1, 3))


def spread(block):
    one, two, three = beside(block), apart(block), between(block)
    return [one, two, (three, outward(two))]


def spread_in_turn(block):
    one, two = beside(block), apart(block)
    return [one, two, (between(after(block, two)), outward(two))]


def position():
    me = lax.axis_index("tensor")
    inner_one = ((me == 1) | (me == 2)).astype(jnp.int32)
    return jnp.stack([inner_one, lax.axis_index("dp"), me])


def collect(parts, *others):
    far, three = inward(parts[3]), between(parts[3])
    far, three, parts, *others = lax.optimization_barrier((far, three, parts, *others))
    return ([parts[0], beside(parts[1]), apart(add(parts[2], far)), three], *others)


def split(total, count):
    rows = total.shape[0] // count
    return [total[k * rows : (k + 1) * rows] for k in range(count)]


def add(left, right):
    return (left.astype(jnp.float32) + right.astype(jnp.float32)).astype(left.dtype)


def after(value, *others):
    return lax.optimization_barrier((value, *others))[0]


SMEM = pl.BlockSpec(memory_space=pltpu.SMEM)
VMEM = pl.BlockSpec(memory_space=pltpu.VMEM)


ANY = pl.BlockSpec(memory_space=pl.ANY)


def rows_of(here, k, rows):
    return pl.ds(pl.multiple_of((here[2] ^ k) * rows, rows), rows)


def fetch(here, blocks, into, sems, in_order=False):
    copies, at = [], 0
    for k, block in enumerate(blocks):
        choices = block if isinstance(block, tuple) else (block,)
        rows = choices[0].shape[0]
        place = into.at[rows_of(here, k, rows) if in_order else pl.ds(at, rows)]
        options = [pltpu.make_async_copy(each, place, sems.at[k]) for each in choices]
        if len(options) == 1:
            options[0].start()
        else:
            pl.when(here[0] == 1)(options[0].start)
            pl.when(here[0] != 1)(options[1].start)
        copies.append(options[0])
        at += rows

    def wait():
        for copy in copies:
            copy.wait()

    return wait


def flat(blocks):
    return [each for block in blocks for each in (block if isinstance(block, tuple) else (block,))]


def shaped(refs, blocks):
    refs = iter(refs)
    return [
        tuple(next(refs) for _ in block) if isinstance(block, tuple) else next(refs)
        for block in blocks
    ]


LANES = 128


def pack_weights(w_query, w_key, w_value, w_output, w_gate, w_up, w_down):
    rows, units = w_gate.shape
    kind = w_gate.dtype
    widths = [w_query.shape[1], w_key.shape[1], w_value.shape[1], w_output.shape[0]]
    given = [w_query, w_output, w_gate, w_up, w_down]

    def kernel(key, value, *refs):
        ins, refs = refs[:5], refs[5:]
        attention, ffn_out, refs = refs[0], refs[1], refs[2:]
        (query_in, output_in, gate_in, up_in, down_in), refs = refs[:5], refs[5:]
        attention_held, ffn_held, sems, out_sems = refs
        waits = [
            fetch(None, [each], into, sems.at[pl.ds(k, 1)])
            for k, (each, into) in enumerate(
                zip(ins, (query_in, output_in, gate_in, up_in, down_in))
            )
        ]
        at = query_in.shape[1]
        pair = jnp.concatenate([key[...], value[...]], 0).T
        attention_held[:, at : at + pair.shape[1]] = pair
        waits[0]()
        attention_held[:, :at] = query_in[...]
        waits[1]()
        attention_held[:, at + pair.shape[1] :] = output_in[...].T
        first = pltpu.make_async_copy(attention_held, attention, out_sems.at[0])
        first.start()
        waits[2]()
        waits[3]()
        for j in range(units // LANES):
            at = j * LANES
            ffn_held[:, 2 * at : 2 * at + LANES] = gate_in[:, at : at + LANES]
            ffn_held[:, 2 * at + LANES : 2 * at + 2 * LANES] = up_in[:, at : at + LANES]
        second = pltpu.make_async_copy(
            ffn_held.at[:, pl.ds(0, 2 * units)], ffn_out.at[:, pl.ds(0, 2 * units)], out_sems.at[1]
        )
        second.start()
        waits[4]()
        ffn_held[:, 2 * units :] = down_in[...].T
        third = pltpu.make_async_copy(
            ffn_held.at[:, pl.ds(2 * units, units)],
            ffn_out.at[:, pl.ds(2 * units, units)],
            out_sems.at[2],
        )
        third.start()
        for copy in (first, second, third):
            copy.wait()

    return pl.pallas_call(
        kernel,
        out_shape=(
            jax.ShapeDtypeStruct((rows, sum(widths)), kind),
            jax.ShapeDtypeStruct((rows, 3 * units), kind),
        ),
        in_specs=[VMEM, VMEM] + [ANY] * 5,
        out_specs=[ANY] * 2,
        scratch_shapes=[pltpu.VMEM(each.shape, kind) for each in given]
        + [
            pltpu.VMEM((rows, sum(widths)), kind),
            pltpu.VMEM((rows, 3 * units), kind),
            pltpu.SemaphoreType.DMA((5,)),
            pltpu.SemaphoreType.DMA((3,)),
        ],
        compiler_params=pltpu.CompilerParams(vmem_limit_bytes=60 * MIB),
    )(w_key.T, w_value.T, *given)


def across(block, step):
    return lax.ppermute(block, "dp", [(i, i ^ step) for i in range(lax.axis_size("dp"))])


def pair_sum(other, own):
    return split(add(own, across(other, 1)), lax.axis_size("dp") // 2)


def scatter_sum(blocks):
    return [blocks[0]] + [across(blocks[m], 2 * m) for m in range(1, len(blocks))]


def unpack_ffn(packed, w_gate, w_up, gain):
    rows, units = packed.shape[0], packed.shape[1] // 3
    f32 = jnp.float32

    def kernel(ref, gate_in, up_in, gain_ref, gate, up, down, gain_out):
        total = jnp.zeros((rows, LANES), f32)
        for j in range(units // LANES):
            at = j * LANES
            span = slice(at, at + LANES)
            d_gate = ref[:, 2 * at : 2 * at + LANES].astype(f32)
            d_up = ref[:, 2 * at + LANES : 2 * at + 2 * LANES].astype(f32)
            total += d_gate * gate_in[:, span].astype(f32) + d_up * up_in[:, span].astype(f32)
            gate[:, span] = d_gate
            up[:, span] = d_up
            down[span] = ref[:, 2 * units + at : 2 * units + at + LANES].T.astype(f32)
        gain_out[...] = jnp.zeros_like(gain_out)
        gain_out[0:1] = jnp.sum(total.T, 0, keepdims=True) / gain_ref[...]

    return pl.pallas_call(
        kernel,
        out_shape=(
            jax.ShapeDtypeStruct((rows, units), f32),
            jax.ShapeDtypeStruct((rows, units), f32),
            jax.ShapeDtypeStruct((units, rows), f32),
            jax.ShapeDtypeStruct((8, rows), f32),
        ),
        compiler_params=pltpu.CompilerParams(vmem_limit_bytes=24 * MIB),
    )(packed, w_gate, w_up, gain)


def unpack_attention(parts, w_query, w_key_t, w_value_t, gain):
    rows, width = w_query.shape
    kv_width = w_key_t.shape[0]
    f32 = jnp.float32
    ends = [width, width + 2 * kv_width, 2 * width + 2 * kv_width]

    def kernel(*refs):
        query, key, value, output, gain_out = refs[-5:]
        query_in, key_in, value_in, gain_ref = refs[-9:-5]
        refs = refs[:-9]

        def columns(at, end):
            return sum_of([ref[:, at:end] for ref in refs])

        total = jnp.zeros((rows, LANES), f32)
        for at in range(0, width, LANES):
            span = slice(at, at + LANES)
            d_query = columns(at, at + LANES)
            query[:, span] = d_query
            total += d_query * query_in[:, span].astype(f32)
        pair = columns(ends[0], ends[1]).T
        key[...] = pair[:kv_width]
        value[...] = pair[kv_width:]
        total = total.T
        both = jnp.sum(total, 0, keepdims=True)
        both += jnp.sum(pair[:kv_width] * key_in[...].astype(f32), 0, keepdims=True)
        both += jnp.sum(pair[kv_width:] * value_in[...].astype(f32), 0, keepdims=True)
        gain_out[...] = jnp.zeros_like(gain_out)
        gain_out[0:1] = both / gain_ref[...]
        output[...] = columns(ends[1], ends[2]).T

    return pl.pallas_call(
        kernel,
        out_shape=(
            jax.ShapeDtypeStruct((rows, width), f32),
            jax.ShapeDtypeStruct((kv_width, rows), f32),
            jax.ShapeDtypeStruct((kv_width, rows), f32),
            jax.ShapeDtypeStruct((width, rows), f32),
            jax.ShapeDtypeStruct((8, rows), f32),
        ),
        compiler_params=pltpu.CompilerParams(vmem_limit_bytes=24 * MIB),
    )(*parts, w_query, w_key_t, w_value_t, gain)


def grads_kernel(lefts, block, here, *refs):
    refs = list(refs)
    given = []
    for blocks in lefts:
        count = len(flat(blocks))
        given.append((shaped(refs[:count], blocks), refs[count]))
        del refs[: count + 1]
    out, *held, sems = refs
    step = pl.program_id(0)

    def dots(first):
        at = 0
        if first:
            waits = [
                (
                    fetch(here, left, held[2 * k], sems.at[k]),
                    fetch(here, [right], held[2 * k + 1], sems.at[k, pl.ds(4, 1)]),
                )
                for k, (left, right) in enumerate(given)
            ]
        for k in range(len(given)):
            left, right = held[2 * k], held[2 * k + 1]
            if first:
                for wait in waits[k]:
                    wait()
            width = right.shape[1]
            columns = pl.ds(pl.multiple_of(step * block, block), block)
            out[:, at : at + width] = inner(left[:, columns], right[...]).astype(out.dtype)
            at += width

    pl.when(step == 0)(lambda: dots(True))
    pl.when(step != 0)(lambda: dots(False))


def grads_of(here, pairs):
    bf16 = jnp.bfloat16
    rows, depth = pairs[0][1].shape[0], flat(pairs[0][0])[0].shape[1]
    block = min(256, depth)
    width = sum(right.shape[1] for _, right in pairs)
    given = [each for left, right in pairs for each in (*flat(left), right)]
    held = [
        pltpu.VMEM(shape, bf16) for _, right in pairs for shape in ((rows, depth), right.shape)
    ]
    return pl.pallas_call(
        functools.partial(grads_kernel, [left for left, _ in pairs], block),
        grid=(depth // block,),
        out_shape=jax.ShapeDtypeStruct((depth, width), bf16),
        in_specs=[SMEM] + [ANY] * len(given),
        out_specs=pl.BlockSpec((block, width), lambda i: (i, 0)),
        scratch_shapes=[*held, pltpu.SemaphoreType.DMA((len(pairs), 5))],
        cost_estimate=pl.CostEstimate(
            flops=2 * rows * depth * width,
            bytes_accessed=2 * (depth * width + rows * width + 2 * rows * depth),
            transcendentals=0,
        ),
        compiler_params=pltpu.CompilerParams(vmem_limit_bytes=60 * MIB),
    )(here, *given)


def ffn_kernel(shapes, here, *refs):
    refs = list(refs)
    lefts = []
    for blocks in shapes:
        count = len(flat(blocks))
        lefts.append(shaped(refs[:count], blocks))
        del refs[:count]
    w_pair, w_down = refs[:2]
    act_ref, d_pair_ref, rows_ref, cot_ref, sems = refs[-5:]

    @pl.when(pl.program_id(0) == 0)
    def _():
        waits = [
            fetch(here, given, into, sems.at[k])
            for k, (into, given) in enumerate(zip((rows_ref, cot_ref), lefts))
        ]
        for wait in waits:
            wait()

    pairs = dot(rows_ref[...], w_pair[...])
    d_acts = dot(cot_ref[...], w_down[...])
    for k in range(d_acts.shape[1] // LANES):
        at = k * LANES
        gate, up = pairs[:, 2 * at : 2 * at + LANES], pairs[:, 2 * at + LANES : 2 * at + 2 * LANES]
        d_act = d_acts[:, at : at + LANES]
        sigma = jax.nn.sigmoid(gate)
        swish = gate * sigma
        act_ref[:, at : at + LANES] = (swish * up).astype(act_ref.dtype)
        d_gate = d_act * up * (sigma * (1.0 + gate * (1.0 - sigma)))
        d_pair_ref[:, 2 * at : 2 * at + LANES] = d_gate.astype(d_pair_ref.dtype)
        d_pair_ref[:, 2 * at + LANES : 2 * at + 2 * LANES] = (d_act * swish).astype(
            d_pair_ref.dtype
        )


def ffn(side, here, rows, cots, pack, before=()):
    block, depth = flat(rows)[0].shape
    units = pack.shape[1] // 3
    wide = 2 * LANES if (2 * units) % (2 * LANES) == 0 else LANES
    bf16 = jnp.bfloat16
    given = [here, *flat(rows), *flat(cots), pack, pack, *before]
    specs = [SMEM] + [ANY] * (len(given) - 3 - len(before))
    specs.append(pl.BlockSpec((depth, 2 * wide), lambda j: (0, j)))
    specs.append(pl.BlockSpec((depth, wide), lambda j: (0, 2 * units // wide + j)))
    specs += [ANY for _ in before]
    return pl.pallas_call(
        functools.partial(ffn_kernel, (rows, cots)),
        grid=(pl.cdiv(units, wide),),
        out_shape=(
            jax.ShapeDtypeStruct((4 * block, units), bf16),
            jax.ShapeDtypeStruct((4 * block, 2 * units), bf16),
        ),
        in_specs=specs,
        out_specs=(
            pl.BlockSpec((2 * block, wide), lambda j: (side, j)),
            pl.BlockSpec((2 * block, 2 * wide), lambda j: (side, j)),
        ),
        scratch_shapes=[
            pltpu.VMEM((2 * block, depth), bf16),
            pltpu.VMEM((2 * block, depth), bf16),
            pltpu.SemaphoreType.DMA((2, 2)),
        ],
        input_output_aliases={len(given) - 2: 0, len(given) - 1: 1} if before else {},
        cost_estimate=pl.CostEstimate(
            flops=4 * block * depth * 3 * units,
            bytes_accessed=2 * (depth * 3 * units + 4 * block * depth + 6 * block * units),
            transcendentals=2 * block * units,
        ),
        compiler_params=pltpu.CompilerParams(vmem_limit_bytes=60 * MIB),
    )(*given)


def sum_of(parts):
    total = parts[0].astype(jnp.float32)
    for part in parts[1:]:
        total = total + part.astype(jnp.float32)
    return total


def turn(block, cosine, sine):
    half = HEAD_DIM // 2
    first, second = block[:half], block[half:]
    return jnp.concatenate([first * cosine - second * sine, second * cosine + first * sine], 0)

WIDE = 640


def spans(rows):
    return [(at, min(at + WIDE, rows)) for at in range(0, rows, WIDE)]


def mask_bias(row_ref, col_ref, bias):
    rows = bias.shape[0]
    for at, end in spans(rows):
        keys = lax.broadcasted_iota(jnp.int32, (end, end - at), 0)
        queries = lax.broadcasted_iota(jnp.int32, (end, end - at), 1) + at
        allowed = (col_ref[:end] == row_ref[:, at:end]) & (keys <= queries)
        bias[:end, at:end] = jnp.where(allowed, 0.0, NEG_FILL)


def attend_kernel(q_width, kv_width, here, own, one, two, three, far, gain_ref, pack_ref, cos_ref,
                  sin_ref, row_ref, col_ref, out_0, out_1, out_2, out_3, normed_out, heads_ref,
                  attended_ref, sums_ref, bias, rows_ref, pack, normed_ref, total, sems, out_sems):
    bf16 = jnp.bfloat16
    scale = 1.0 / math.sqrt(HEAD_DIM)
    q_heads, kv_heads = q_width // HEAD_DIM, kv_width // HEAD_DIM
    qkv = q_width + 2 * kv_width
    wait_rows = fetch(here, (own, one, two, (three, far)), rows_ref, sems, in_order=True)
    wait_pack = fetch(here, [pack_ref], pack, sems.at[pl.ds(4, 1)])
    mask_bias(row_ref, col_ref, bias)
    wait_rows()
    x = rows_ref[...].astype(jnp.float32)
    inv = lax.rsqrt(jnp.mean(x * x, -1, keepdims=True) + EPS)
    normed_ref[...] = (x * inv * gain_ref[...]).astype(bf16)
    pending = [pltpu.make_async_copy(normed_ref, normed_out, out_sems.at[4])]
    pending[0].start()
    wait_pack()
    cosine, sine = cos_ref[...], sin_ref[...]
    heads = dot(normed_ref[...], pack[:, :qkv]).T
    for h in range(q_heads + kv_heads):
        at = h * HEAD_DIM
        turned = turn(heads[at : at + HEAD_DIM], cosine, sine).astype(bf16)
        heads_ref[at : at + HEAD_DIM] = turned * bf16(scale) if h < q_heads else turned
    heads_ref[q_width + kv_width :] = heads[q_width + kv_width :].astype(bf16)
    keys = [
        heads_ref[at : at + HEAD_DIM].T
        for at in range(q_width, q_width + kv_width, HEAD_DIM)
    ]
    for start, end in spans(x.shape[0]):
        parts = []
        for h in range(q_heads):
            c = h * kv_heads // q_heads
            at = q_width + kv_width + c * HEAD_DIM
            query_t = heads_ref[h * HEAD_DIM : (h + 1) * HEAD_DIM, start:end]
            scores = dot(keys[c][:end], query_t) + bias[:end, start:end]
            top = jnp.max(scores, 0, keepdims=True)
            raised = jnp.exp(scores - top)
            raised_sum = jnp.sum(raised, 0, keepdims=True)
            sums_ref[h : h + 1, start:end] = top + jnp.log(raised_sum)
            value_t = heads_ref[at : at + HEAD_DIM, :end]
            parts.append(dot(value_t, raised.astype(bf16)) / raised_sum)
        attended_ref[start:end] = jnp.concatenate(parts, 0).T.astype(bf16)
    total[...] = outer_t(attended_ref[...], pack[:, qkv:]).astype(bf16)
    for k, out in enumerate((out_0, out_1, out_2, out_3)):
        rows = rows_of(here, k, out.shape[0])
        pending.append(pltpu.make_async_copy(total.at[rows], out, out_sems.at[k]))
        pending[-1].start()
    for copy in pending:
        copy.wait()


def attend(here, blocks, gain, pack, cosine, sine, row, col, q_width, kv_width):
    rows, depth = 4 * blocks[0].shape[0], blocks[0].shape[1]
    bf16 = jnp.bfloat16
    qkv = q_width + 2 * kv_width
    return pl.pallas_call(
        functools.partial(attend_kernel, q_width, kv_width),
        out_shape=(
            *[jax.ShapeDtypeStruct((rows // 4, depth), bf16)] * 4,
            jax.ShapeDtypeStruct((rows, depth), bf16),
            jax.ShapeDtypeStruct((qkv, rows), bf16),
            jax.ShapeDtypeStruct((rows, q_width), bf16),
            jax.ShapeDtypeStruct((q_width // HEAD_DIM, rows), jnp.float32),
        ),
        in_specs=[SMEM] + [ANY] * 5 + [VMEM, ANY] + [VMEM] * 4,
        out_specs=[ANY] * 5 + [VMEM] * 3,
        scratch_shapes=[
            pltpu.VMEM((rows, rows), jnp.float32),
            pltpu.VMEM((rows, depth), bf16),
            pltpu.VMEM(pack.shape, bf16),
            pltpu.VMEM((rows, depth), bf16),
            pltpu.VMEM((rows, depth), bf16),
            pltpu.SemaphoreType.DMA((5,)),
            pltpu.SemaphoreType.DMA((5,)),
        ],
        cost_estimate=pl.CostEstimate(
            flops=2 * rows * depth * (qkv + q_width) + 4 * rows * rows * q_width,
            bytes_accessed=2 * (3 * rows * depth + depth * (qkv + q_width)),
            transcendentals=rows * rows * q_width // HEAD_DIM,
        ),
        compiler_params=pltpu.CompilerParams(vmem_limit_bytes=60 * MIB),
    )(here, *flat(blocks), gain, pack, cosine, sine, row, col)

def attend_back_kernel(q_width, kv_width, owners, here, own, one, two, three, far, normed_ref, pack_ref,
                       cos_ref, sin_ref, row_ref, col_ref, heads_ref, sums_ref, attended_ref, out_0,
                       out_1, out_2, out_3, other_ref, own_ref, bias, d_att_t, d_heads_t, d_keys,
                       rows_ref, normed, pack, out, d_qkv, lefts, blocks, sems, out_sems):
    bf16 = jnp.bfloat16
    scale = 1.0 / math.sqrt(HEAD_DIM)
    q_heads, kv_heads = q_width // HEAD_DIM, kv_width // HEAD_DIM
    qkv = q_width + 2 * kv_width
    wait_rows = fetch(here, (own, one, two, (three, far)), rows_ref, sems, in_order=True)
    wait_pack = fetch(here, [pack_ref], pack, sems.at[pl.ds(4, 1)])
    wait_normed = fetch(here, [normed_ref], normed, sems.at[pl.ds(5, 1)])
    mask_bias(row_ref, col_ref, bias)
    wait_rows()
    wait_pack()
    d_att_t[...] = dot(rows_ref[...], pack[:, qkv:]).T.astype(bf16)
    for c in range(kv_heads):
        at = q_width + c * HEAD_DIM
        key_t = heads_ref[at : at + HEAD_DIM]
        key = key_t.T
        value = heads_ref[at + kv_width : at + kv_width + HEAD_DIM].T
        d_keys[...] = jnp.zeros_like(d_keys)
        for start, end in spans(key.shape[0]):
            d_key = d_value = 0.0
            cosine, sine = cos_ref[:, start:end], sin_ref[:, start:end]
            for h in range(c * q_heads // kv_heads, (c + 1) * q_heads // kv_heads):
                head = slice(h * HEAD_DIM, (h + 1) * HEAD_DIM)
                query_t = heads_ref[head, start:end]
                d_out_t = d_att_t[head, start:end]
                prob = jnp.exp(
                    dot(key[:end], query_t) + bias[:end, start:end] - sums_ref[h : h + 1, start:end]
                )
                d_prob = dot(value[:end], d_out_t)
                delta = jnp.sum(prob * d_prob, 0, keepdims=True)
                d_scores = (prob * (d_prob - delta)).astype(bf16)
                d_value = d_value + outer_t(prob.astype(bf16), d_out_t)
                d_key = d_key + outer_t(d_scores, query_t)
                d_query = dot(key_t[:, :end], d_scores) * scale
                d_heads_t[head, start:end] = turn(d_query, cosine, -sine)
            d_keys[0, :end] += d_key
            d_keys[1, :end] += d_value
        d_heads_t[at : at + HEAD_DIM] = turn(d_keys[0].T, cos_ref[...], -sin_ref[...])
        d_heads_t[at + kv_width : at + kv_width + HEAD_DIM] = d_keys[1].T
    d_qkv[...] = d_heads_t[...].T.astype(bf16)
    out[...] = outer_t(d_qkv[...], pack[:, :qkv]).astype(bf16)
    pending = []
    for k, part in enumerate((out_0, out_1, out_2, out_3)):
        rows = rows_of(here, k, part.shape[0])
        pending.append(pltpu.make_async_copy(out.at[rows], part, out_sems.at[4 + k]))
        pending[-1].start()

    wait_normed()
    lefts[0] = normed[...].T
    lefts[1] = rows_ref[...].T
    block = lefts.shape[1] // owners
    for half, target in enumerate((other_ref, own_ref)):

        def step(m, carry, half=half, target=target):
            owner = here[1] ^ (1 - half) ^ (2 * m)
            rows = pl.ds(pl.multiple_of(owner * block, block), block)
            slot = 2 * half + m % 2
            copy = pltpu.make_async_copy(
                blocks.at[slot], target.at[pl.ds(m * block, block)], out_sems.at[slot]
            )
            pl.when(m >= 2)(copy.wait)
            blocks[slot, :, :qkv] = dot(lefts[0, rows], d_qkv[...]).astype(bf16)
            blocks[slot, :, qkv:] = dot(lefts[1, rows], attended_ref[...]).astype(bf16)
            copy.start()
            return carry

        lax.fori_loop(0, owners // 2, step, 0)
        for slot in (2 * half, 2 * half + 1):
            pending.append(
                pltpu.make_async_copy(
                    blocks.at[slot], target.at[pl.ds(0, block)], out_sems.at[slot]
                )
            )
    for copy in pending:
        copy.wait()


def attend_back(
    here,
    blocks,
    normed,
    pack,
    cosine,
    sine,
    row,
    col,
    heads,
    sums,
    attended,
    owners,
    q_width,
    kv_width,
):
    rows, depth = normed.shape
    bf16 = jnp.bfloat16
    f32 = jnp.float32
    qkv = q_width + 2 * kv_width
    width = qkv + q_width
    return pl.pallas_call(
        functools.partial(attend_back_kernel, q_width, kv_width, owners),
        out_shape=(
            *[jax.ShapeDtypeStruct((rows // 4, depth), bf16)] * 4,
            jax.ShapeDtypeStruct((depth // 2, width), bf16),
            jax.ShapeDtypeStruct((depth // 2, width), bf16),
        ),
        in_specs=[SMEM] + [ANY] * 7 + [VMEM] * 7,
        out_specs=[ANY] * 6,
        scratch_shapes=[
            pltpu.VMEM((rows, rows), f32),
            pltpu.VMEM((q_width, rows), bf16),
            pltpu.VMEM((qkv, rows), f32),
            pltpu.VMEM((2, rows, HEAD_DIM), f32),
            pltpu.VMEM((rows, depth), bf16),
            pltpu.VMEM((rows, depth), bf16),
            pltpu.VMEM(pack.shape, bf16),
            pltpu.VMEM((rows, depth), bf16),
            pltpu.VMEM((rows, qkv), bf16),
            pltpu.VMEM((2, depth, rows), bf16),
            pltpu.VMEM((4, depth // owners, width), bf16),
            pltpu.SemaphoreType.DMA((6,)),
            pltpu.SemaphoreType.DMA((8,)),
        ],
        cost_estimate=pl.CostEstimate(
            flops=4 * rows * depth * (qkv + q_width) + 10 * rows * rows * q_width,
            bytes_accessed=2 * (3 * rows * depth + 2 * depth * (qkv + q_width)),
            transcendentals=rows * rows * q_width // HEAD_DIM,
        ),
        compiler_params=pltpu.CompilerParams(vmem_limit_bytes=60 * MIB),
    )(here, *flat(blocks), normed, pack, cosine, sine, row, col, heads, sums, attended)


def back_through_norm(parts, above, rows, gain, low_too=False):
    shape = above.shape
    f32, bf16 = jnp.float32, jnp.bfloat16
    given = [*parts, above, rows]
    half = pl.BlockSpec((shape[0] // 2, shape[1]), lambda i: (i, 0))

    def kernel(gain_ref, *refs):
        *parts_in, above_ref, rows_ref = refs[: len(given)]
        x = rows_ref[...].astype(f32)
        inv = lax.rsqrt(jnp.mean(x * x, -1, keepdims=True) + EPS)
        back = norm_back(sum_of([part[...] for part in parts_in]), x * inv, inv, gain_ref[...])
        total = above_ref[...].astype(f32) + back
        for out in refs[len(given) :]:
            out[...] = total.astype(out.dtype)

    outs = [f32, bf16] if low_too else [bf16]
    return pl.pallas_call(
        kernel,
        grid=(2,),
        out_shape=[jax.ShapeDtypeStruct(shape, each) for each in outs],
        in_specs=[pl.BlockSpec(gain.shape, lambda i: (0, 0))] + [half] * len(given),
        out_specs=[half] * len(outs),
        cost_estimate=pl.CostEstimate(
            flops=20 * shape[0] * shape[1],
            bytes_accessed=sum(each.size * each.dtype.itemsize for each in given),
            transcendentals=shape[0],
        ),
        compiler_params=pltpu.CompilerParams(vmem_limit_bytes=60 * MIB),
    )(gain, *given)


def body(
    tokens,
    lengths,
    attn_gain,
    w_query,
    w_key,
    w_value,
    w_output,
    ffn_gain,
    w_gate,
    w_up,
    w_down,
    cotangent,
):
    bf16 = jnp.bfloat16
    count = lax.axis_size("tensor")
    local_rows = tokens.shape[0]
    width = w_query.shape[1]
    kv_width = w_key.shape[1]
    hidden_units = w_gate.shape[1]
    here = position()

    token_rows = spread(tokens)
    attn_pack, ffn_pack = pack_weights(
        w_query, w_key, w_value, w_output, w_gate, w_up, w_down
    )
    attn_pack = lax.all_gather(attn_pack, "dp", axis=0, tiled=True)
    gains = lax.all_gather(
        jnp.stack([attn_gain, ffn_gain])[None], "dp", axis=0, tiled=True
    ).astype(jnp.float32)
    gain_one = gains[:, 0].reshape(1, -1)
    gain_two = gains[:, 1].reshape(1, -1)
    ffn_pack = lax.all_gather(ffn_pack, "dp", axis=0, tiled=True)
    cot_own, token_rows = lax.optimization_barrier((cotangent, token_rows))
    cot_one, cot_three = beside(cot_own), between(cot_own)
    full_pair = ffn_pack[:, : 2 * hidden_units]
    full_down = ffn_pack[:, 2 * hidden_units :]

    segment, offset = seq_layout(
        lengths[0], jnp.arange(count * local_rows, dtype=jnp.int32)
    )
    cosine, sine = rope_tables(offset)
    as_row, as_column = segment[None], segment[:, None]
    *parts, normed_one, heads, attended, log_sums = attend(
        here,
        [tokens, *token_rows],
        gain_one,
        attn_pack,
        cosine,
        sine,
        as_row,
        as_column,
        width,
        kv_width,
    )
    parts, cot_one, cot_three = lax.optimization_barrier((parts, cot_one, cot_three))
    far, cot_two, cot_near = inward(parts[3]), between(cot_one), outward(cot_three)
    parts, far, cot_two, cot_near = lax.optimization_barrier((parts, far, cot_two, cot_near))
    near, two, cot_far = inward(parts[2]), between(add(parts[2], far)), outward(cot_two)
    parts, near, two, cot_far = lax.optimization_barrier((parts, near, two, cot_far))
    three, one = between(add(parts[3], near)), beside(add(parts[1], two))
    cot_rows = [cotangent, cot_one, (cot_two, cot_near), (cot_three, cot_far)]
    resid = tokens.astype(jnp.float32)
    hidden = resid + sum_of([parts[0], one, three])

    inv_two = lax.rsqrt(jnp.mean(hidden * hidden, -1, keepdims=True) + EPS)
    unit_two = hidden * inv_two
    own_two = (unit_two * gain_two).astype(bf16)
    two_rows = spread_in_turn(own_two)
    two_rows = [own_two, *two_rows]
    halfway = ffn(0, here, two_rows[:2], cot_rows[:2], ffn_pack)
    activation, d_pair = ffn(1, here, two_rows[2:], cot_rows[2:], ffn_pack, halfway)
    half = 2 * local_rows
    two_parts = split(outer_t(d_pair[half:], full_pair).astype(bf16), 2)
    two_parts = split(outer_t(d_pair[:half], full_pair).astype(bf16), 2) + two_parts
    two_parts, activation, d_pair = collect(two_parts, activation, d_pair)
    ffn_local = grads_of(
        here, [(two_rows, d_pair), (cot_rows, activation)]
    )
    two_parts, ffn_local = lax.optimization_barrier((two_parts, ffn_local))
    ffn_grads = lax.psum_scatter(ffn_local, "dp", scatter_dimension=0, tiled=True)

    d_hidden, own_back = back_through_norm(two_parts, cotangent, hidden, gain_two, low_too=True)
    back_rows = spread_in_turn(own_back)
    down_total = outer_t(after(activation, own_back), full_down).astype(bf16)
    parts = split(after(down_total, back_rows[1]), count)
    far = inward(parts[3])
    parts, far, back_rows = lax.optimization_barrier((parts, far, back_rows))
    near, two = inward(parts[2]), between(add(parts[2], far))
    back_rows = [own_back, *back_rows]
    *one_total, other_local, own_local = attend_back(
        here,
        back_rows,
        normed_one,
        attn_pack,
        cosine,
        sine,
        as_row,
        as_column,
        heads,
        log_sums,
        attended,
        lax.axis_size("dp"),
        width,
        kv_width,
    )
    other_local, outer, inner_sum = lax.optimization_barrier(
        (other_local, add(parts[1], two), add(parts[3], near))
    )
    block_out = (hidden + sum_of([parts[0], beside(outer), between(inner_sum)])).astype(bf16)
    (one_parts,) = collect(one_total)
    attn_pairs = pair_sum(other_local, own_local)
    attn_parts = scatter_sum(attn_pairs)
    (grad_tokens,) = back_through_norm(one_parts, d_hidden, tokens, gain_one)
    own_gains = [each.astype(jnp.float32).reshape(1, -1) for each in (attn_gain, ffn_gain)]
    *ffn_grads, ffn_gain_part = unpack_ffn(ffn_grads, w_gate, w_up, own_gains[1])
    attn_parts, ffn_grads = lax.optimization_barrier((attn_parts, ffn_grads))
    grad_query, grad_key, grad_value, grad_output, attn_gain_part = unpack_attention(
        attn_parts, w_query, w_key.T, w_value.T, own_gains[0]
    )
    gain_parts = jnp.concatenate([attn_gain_part[:1], ffn_gain_part[:1]], 0)
    gain_parts, block_out = lax.optimization_barrier((gain_parts, block_out))
    gain_grads = sum_of(
        [gain_parts]
        + [
            lax.ppermute(gain_parts, "tensor", [(i, (i + k) % count) for i in range(count)])
            for k in range(1, count)
        ]
    )
    return (
        block_out,
        grad_tokens,
        gain_grads[0],
        grad_query,
        grad_key.T,
        grad_value.T,
        grad_output,
        gain_grads[1],
        *ffn_grads,
    )


def solution(mesh):
    return jax.shard_map(
        body,
        mesh=mesh,
        in_specs=(
            P(("dp", "tensor"), None),
            P("dp", None),
            P("dp"),
            P("dp", "tensor"),
            P("dp", "tensor"),
            P("dp", "tensor"),
            P("tensor", "dp"),
            P("dp"),
            P("dp", "tensor"),
            P("dp", "tensor"),
            P("tensor", "dp"),
            P(("dp", "tensor"), None),
        ),
        out_specs=(
            P(("dp", "tensor"), None),
            P(("dp", "tensor"), None),
            P("dp"),
            P("dp", "tensor"),
            P("dp", "tensor"),
            P("dp", "tensor"),
            P("tensor", "dp"),
            P("dp"),
            P("dp", "tensor"),
            P("dp", "tensor"),
            P("tensor", "dp"),
        ),
        check_vma=False,
    )
```

```python
import functools
import math

import jax
import jax.numpy as jnp
from jax import lax
from jax.experimental import pallas as pl
from jax.experimental.pallas import tpu as pltpu
from jax.sharding import PartitionSpec as P

HEAD_DIM = 64
EPS = 1e-05
ROPE_BASE = 10000.0
NEG_FILL = -1e30
MIB = 1024 * 1024


def seq_layout(row_lengths, places):
    ends = jnp.cumsum(row_lengths)
    starts = ends - row_lengths
    segment = jnp.sum((places[:, None] >= ends[None, :]).astype(jnp.int32), axis=1)
    owner = segment[:, None] == jnp.arange(row_lengths.shape[0], dtype=jnp.int32)[None, :]
    begin = jnp.sum(jnp.where(owner, starts[None, :], 0), axis=1)
    return (segment, places - begin)


def rope_tables(position):
    half = HEAD_DIM // 2
    freqs = ROPE_BASE ** (-(jnp.arange(half, dtype=jnp.float32) * 2.0 / HEAD_DIM))
    angles = freqs[:, None] * position.astype(jnp.float32)[None, :]
    return (jnp.cos(angles), jnp.sin(angles))


def dot(left, right):
    return jnp.dot(left, right, preferred_element_type=jnp.float32)


def inner(left, right):
    return lax.dot_general(
        left, right, (((0,), (0,)), ((), ())), preferred_element_type=jnp.float32
    )


def outer_t(left, right):
    return lax.dot_general(
        left, right, (((1,), (1,)), ((), ())), preferred_element_type=jnp.float32
    )


def norm_back(d_normed, unit, inv, gain):
    scaled = d_normed * gain
    return inv * (scaled - unit * jnp.mean(scaled * unit, -1, keepdims=True))


def swap(block, *pairs):
    return lax.ppermute(block, "tensor", [p for i, j in pairs for p in ((i, j), (j, i))])


def outward(block):
    return lax.ppermute(block, "tensor", [(1, 0), (2, 3)])


def inward(block):
    return lax.ppermute(block, "tensor", [(0, 1), (3, 2)])


def beside(block):
    return swap(block, (0, 1), (2, 3))


def between(block):
    return swap(block, (1, 2))


def apart(block):
    return swap(block, (0, 2), (1, 3))


def spread(block):
    one, two, three = beside(block), apart(block), between(block)
    return [one, two, (three, outward(two))]


def spread_in_turn(block):
    one, two = beside(block), apart(block)
    return [one, two, (between(after(block, two)), outward(two))]


def position():
    me = lax.axis_index("tensor")
    inner_one = ((me == 1) | (me == 2)).astype(jnp.int32)
    return jnp.stack([inner_one, lax.axis_index("dp"), me])


def collect(parts, *others):
    far, three = inward(parts[3]), between(parts[3])
    far, three, parts, *others = lax.optimization_barrier((far, three, parts, *others))
    return ([parts[0], beside(parts[1]), apart(add(parts[2], far)), three], *others)


def split(total, count):
    rows = total.shape[0] // count
    return [total[k * rows : (k + 1) * rows] for k in range(count)]


def add(left, right):
    return (left.astype(jnp.float32) + right.astype(jnp.float32)).astype(left.dtype)


def after(value, *others):
    return lax.optimization_barrier((value, *others))[0]


SMEM = pl.BlockSpec(memory_space=pltpu.SMEM)
VMEM = pl.BlockSpec(memory_space=pltpu.VMEM)


ANY = pl.BlockSpec(memory_space=pl.ANY)


def rows_of(here, k, rows):
    return pl.ds(pl.multiple_of((here[2] ^ k) * rows, rows), rows)


def fetch(here, blocks, into, sems, in_order=False):
    copies, at = [], 0
    for k, block in enumerate(blocks):
        choices = block if isinstance(block, tuple) else (block,)
        rows = choices[0].shape[0]
        place = into.at[rows_of(here, k, rows) if in_order else pl.ds(at, rows)]
        options = [pltpu.make_async_copy(each, place, sems.at[k]) for each in choices]
        if len(options) == 1:
            options[0].start()
        else:
            pl.when(here[0] == 1)(options[0].start)
            pl.when(here[0] != 1)(options[1].start)
        copies.append(options[0])
        at += rows

    def wait():
        for copy in copies:
            copy.wait()

    return wait


def flat(blocks):
    return [each for block in blocks for each in (block if isinstance(block, tuple) else (block,))]


def shaped(refs, blocks):
    refs = iter(refs)
    return [
        tuple(next(refs) for _ in block) if isinstance(block, tuple) else next(refs)
        for block in blocks
    ]


LANES = 128


def pack_weights(w_query, w_key, w_value, w_output, w_gate, w_up, w_down):
    rows, units = w_gate.shape
    kind = w_gate.dtype
    widths = [w_query.shape[1], w_key.shape[1], w_value.shape[1], w_output.shape[0]]
    given = [w_query, w_output, w_gate, w_up, w_down]

    def kernel(key, value, *refs):
        ins, refs = refs[:5], refs[5:]
        attention, ffn_out, refs = refs[0], refs[1], refs[2:]
        (query_in, output_in, gate_in, up_in, down_in), refs = refs[:5], refs[5:]
        attention_held, ffn_held, sems, out_sems = refs
        waits = [
            fetch(None, [each], into, sems.at[pl.ds(k, 1)])
            for k, (each, into) in enumerate(
                zip(ins, (query_in, output_in, gate_in, up_in, down_in))
            )
        ]
        at = query_in.shape[1]
        pair = jnp.concatenate([key[...], value[...]], 0).T
        attention_held[:, at : at + pair.shape[1]] = pair
        waits[0]()
        attention_held[:, :at] = query_in[...]
        waits[1]()
        attention_held[:, at + pair.shape[1] :] = output_in[...].T
        first = pltpu.make_async_copy(attention_held, attention, out_sems.at[0])
        first.start()
        waits[2]()
        waits[3]()
        for j in range(units // LANES):
            at = j * LANES
            ffn_held[:, 2 * at : 2 * at + LANES] = gate_in[:, at : at + LANES]
            ffn_held[:, 2 * at + LANES : 2 * at + 2 * LANES] = up_in[:, at : at + LANES]
        second = pltpu.make_async_copy(
            ffn_held.at[:, pl.ds(0, 2 * units)], ffn_out.at[:, pl.ds(0, 2 * units)], out_sems.at[1]
        )
        second.start()
        waits[4]()
        ffn_held[:, 2 * units :] = down_in[...].T
        third = pltpu.make_async_copy(
            ffn_held.at[:, pl.ds(2 * units, units)],
            ffn_out.at[:, pl.ds(2 * units, units)],
            out_sems.at[2],
        )
        third.start()
        for copy in (first, second, third):
            copy.wait()

    return pl.pallas_call(
        kernel,
        out_shape=(
            jax.ShapeDtypeStruct((rows, sum(widths)), kind),
            jax.ShapeDtypeStruct((rows, 3 * units), kind),
        ),
        in_specs=[VMEM, VMEM] + [ANY] * 5,
        out_specs=[ANY] * 2,
        scratch_shapes=[pltpu.VMEM(each.shape, kind) for each in given]
        + [
            pltpu.VMEM((rows, sum(widths)), kind),
            pltpu.VMEM((rows, 3 * units), kind),
            pltpu.SemaphoreType.DMA((5,)),
            pltpu.SemaphoreType.DMA((3,)),
        ],
        compiler_params=pltpu.CompilerParams(vmem_limit_bytes=60 * MIB),
    )(w_key.T, w_value.T, *given)


def across(block, step):
    return lax.ppermute(block, "dp", [(i, i ^ step) for i in range(lax.axis_size("dp"))])


def pair_sum(other, own):
    return split(add(own, across(other, 1)), lax.axis_size("dp") // 2)


def scatter_sum(blocks):
    return [blocks[0]] + [across(blocks[m], 2 * m) for m in range(1, len(blocks))]


def unpack_ffn(packed, w_gate, w_up, gain):
    rows, units = packed.shape[0], packed.shape[1] // 3
    f32 = jnp.float32

    def kernel(ref, gate_in, up_in, gain_ref, gate, up, down, gain_out):
        total = jnp.zeros((rows, LANES), f32)
        for j in range(units // LANES):
            at = j * LANES
            span = slice(at, at + LANES)
            d_gate = ref[:, 2 * at : 2 * at + LANES].astype(f32)
            d_up = ref[:, 2 * at + LANES : 2 * at + 2 * LANES].astype(f32)
            total += d_gate * gate_in[:, span].astype(f32) + d_up * up_in[:, span].astype(f32)
            gate[:, span] = d_gate
            up[:, span] = d_up
            down[span] = ref[:, 2 * units + at : 2 * units + at + LANES].T.astype(f32)
        gain_out[...] = jnp.zeros_like(gain_out)
        gain_out[0:1] = jnp.sum(total.T, 0, keepdims=True) / gain_ref[...]

    return pl.pallas_call(
        kernel,
        out_shape=(
            jax.ShapeDtypeStruct((rows, units), f32),
            jax.ShapeDtypeStruct((rows, units), f32),
            jax.ShapeDtypeStruct((units, rows), f32),
            jax.ShapeDtypeStruct((8, rows), f32),
        ),
        compiler_params=pltpu.CompilerParams(vmem_limit_bytes=24 * MIB),
    )(packed, w_gate, w_up, gain)


def unpack_attention(parts, w_query, w_key_t, w_value_t, gain):
    rows, width = w_query.shape
    kv_width = w_key_t.shape[0]
    f32 = jnp.float32
    ends = [width, width + 2 * kv_width, 2 * width + 2 * kv_width]

    def kernel(*refs):
        query, key, value, output, gain_out = refs[-5:]
        query_in, key_in, value_in, gain_ref = refs[-9:-5]
        refs = refs[:-9]

        def columns(at, end):
            return sum_of([ref[:, at:end] for ref in refs])

        total = jnp.zeros((rows, LANES), f32)
        for at in range(0, width, LANES):
            span = slice(at, at + LANES)
            d_query = columns(at, at + LANES)
            query[:, span] = d_query
            total += d_query * query_in[:, span].astype(f32)
        pair = columns(ends[0], ends[1]).T
        key[...] = pair[:kv_width]
        value[...] = pair[kv_width:]
        total = total.T
        both = jnp.sum(total, 0, keepdims=True)
        both += jnp.sum(pair[:kv_width] * key_in[...].astype(f32), 0, keepdims=True)
        both += jnp.sum(pair[kv_width:] * value_in[...].astype(f32), 0, keepdims=True)
        gain_out[...] = jnp.zeros_like(gain_out)
        gain_out[0:1] = both / gain_ref[...]
        output[...] = columns(ends[1], ends[2]).T

    return pl.pallas_call(
        kernel,
        out_shape=(
            jax.ShapeDtypeStruct((rows, width), f32),
            jax.ShapeDtypeStruct((kv_width, rows), f32),
            jax.ShapeDtypeStruct((kv_width, rows), f32),
            jax.ShapeDtypeStruct((width, rows), f32),
            jax.ShapeDtypeStruct((8, rows), f32),
        ),
        compiler_params=pltpu.CompilerParams(vmem_limit_bytes=24 * MIB),
    )(*parts, w_query, w_key_t, w_value_t, gain)


def grads_kernel(lefts, block, here, *refs):
    refs = list(refs)
    given = []
    for blocks in lefts:
        count = len(flat(blocks))
        given.append((shaped(refs[:count], blocks), refs[count]))
        del refs[: count + 1]
    out, *held, sems = refs
    step = pl.program_id(0)

    def dots(first):
        at = 0
        if first:
            waits = [
                (
                    fetch(here, left, held[2 * k], sems.at[k]),
                    fetch(here, [right], held[2 * k + 1], sems.at[k, pl.ds(4, 1)]),
                )
                for k, (left, right) in enumerate(given)
            ]
        for k in range(len(given)):
            left, right = held[2 * k], held[2 * k + 1]
            if first:
                for wait in waits[k]:
                    wait()
            width = right.shape[1]
            columns = pl.ds(pl.multiple_of(step * block, block), block)
            out[:, at : at + width] = inner(left[:, columns], right[...]).astype(out.dtype)
            at += width

    pl.when(step == 0)(lambda: dots(True))
    pl.when(step != 0)(lambda: dots(False))


def grads_of(here, pairs):
    bf16 = jnp.bfloat16
    rows, depth = pairs[0][1].shape[0], flat(pairs[0][0])[0].shape[1]
    block = min(256, depth)
    width = sum(right.shape[1] for _, right in pairs)
    given = [each for left, right in pairs for each in (*flat(left), right)]
    held = [
        pltpu.VMEM(shape, bf16) for _, right in pairs for shape in ((rows, depth), right.shape)
    ]
    return pl.pallas_call(
        functools.partial(grads_kernel, [left for left, _ in pairs], block),
        grid=(depth // block,),
        out_shape=jax.ShapeDtypeStruct((depth, width), bf16),
        in_specs=[SMEM] + [ANY] * len(given),
        out_specs=pl.BlockSpec((block, width), lambda i: (i, 0)),
        scratch_shapes=[*held, pltpu.SemaphoreType.DMA((len(pairs), 5))],
        cost_estimate=pl.CostEstimate(
            flops=2 * rows * depth * width,
            bytes_accessed=2 * (depth * width + rows * width + 2 * rows * depth),
            transcendentals=0,
        ),
        compiler_params=pltpu.CompilerParams(vmem_limit_bytes=60 * MIB),
    )(here, *given)


def ffn_kernel(shapes, units, here, *refs):
    refs = list(refs)
    lefts = []
    for blocks in shapes:
        count = len(flat(blocks))
        lefts.append(shaped(refs[:count], blocks))
        del refs[:count]
    w_pair, w_down = refs[:2]
    act_ref, d_pair_ref, rows_ref, cot_ref, sems = refs[-5:]

    @pl.when(pl.program_id(0) == 0)
    def _():
        waits = [
            fetch(here, given, into, sems.at[k])
            for k, (into, given) in enumerate(zip((rows_ref, cot_ref), lefts))
        ]
        for wait in waits:
            wait()

    def columns(blocks):
        pairs = dot(rows_ref[...], w_pair[:, : 2 * blocks * LANES])
        d_acts = dot(cot_ref[...], w_down[:, : blocks * LANES])
        for k in range(blocks):
            at = k * LANES
            gate, up = pairs[:, 2 * at : 2 * at + LANES], pairs[:, 2 * at + LANES : 2 * at + 2 * LANES]
            d_act = d_acts[:, at : at + LANES]
            sigma = jax.nn.sigmoid(gate)
            swish = gate * sigma
            act_ref[:, at : at + LANES] = (swish * up).astype(act_ref.dtype)
            d_gate = d_act * up * (sigma * (1.0 + gate * (1.0 - sigma)))
            d_pair_ref[:, 2 * at : 2 * at + LANES] = d_gate.astype(d_pair_ref.dtype)
            d_pair_ref[:, 2 * at + LANES : 2 * at + 2 * LANES] = (d_act * swish).astype(
                d_pair_ref.dtype
            )

    wide = w_down.shape[1] // LANES
    last, left = pl.num_programs(0) - 1, units // LANES % wide
    pl.when((pl.program_id(0) < last) | (left == 0))(lambda: columns(wide))
    if left:
        pl.when(pl.program_id(0) == last)(lambda: columns(left))


def ffn(side, here, rows, cots, pack, before=()):
    block, depth = flat(rows)[0].shape
    units = pack.shape[1] // 3
    wide = 2 * LANES if (2 * units) % (2 * LANES) == 0 else LANES
    bf16 = jnp.bfloat16
    given = [here, *flat(rows), *flat(cots), pack, pack, *before]
    specs = [SMEM] + [ANY] * (len(given) - 3 - len(before))
    specs.append(pl.BlockSpec((depth, 2 * wide), lambda j: (0, j)))
    specs.append(pl.BlockSpec((depth, wide), lambda j: (0, 2 * units // wide + j)))
    specs += [ANY for _ in before]
    return pl.pallas_call(
        functools.partial(ffn_kernel, (rows, cots), units),
        grid=(pl.cdiv(units, wide),),
        out_shape=(
            jax.ShapeDtypeStruct((4 * block, units), bf16),
            jax.ShapeDtypeStruct((4 * block, 2 * units), bf16),
        ),
        in_specs=specs,
        out_specs=(
            pl.BlockSpec((2 * block, wide), lambda j: (side, j)),
            pl.BlockSpec((2 * block, 2 * wide), lambda j: (side, j)),
        ),
        scratch_shapes=[
            pltpu.VMEM((2 * block, depth), bf16),
            pltpu.VMEM((2 * block, depth), bf16),
            pltpu.SemaphoreType.DMA((2, 2)),
        ],
        input_output_aliases={len(given) - 2: 0, len(given) - 1: 1} if before else {},
        cost_estimate=pl.CostEstimate(
            flops=4 * block * depth * 3 * units,
            bytes_accessed=2 * (depth * 3 * units + 4 * block * depth + 6 * block * units),
            transcendentals=2 * block * units,
        ),
        compiler_params=pltpu.CompilerParams(vmem_limit_bytes=60 * MIB),
    )(*given)


def sum_of(parts):
    total = parts[0].astype(jnp.float32)
    for part in parts[1:]:
        total = total + part.astype(jnp.float32)
    return total


def turn(block, cosine, sine):
    half = HEAD_DIM // 2
    first, second = block[:half], block[half:]
    return jnp.concatenate([first * cosine - second * sine, second * cosine + first * sine], 0)

WIDE = 640


def spans(rows):
    return [(at, min(at + WIDE, rows)) for at in range(0, rows, WIDE)]


def mask_bias(row_ref, col_ref, bias):
    rows = bias.shape[0]
    for at, end in spans(rows):
        keys = lax.broadcasted_iota(jnp.int32, (end, end - at), 0)
        queries = lax.broadcasted_iota(jnp.int32, (end, end - at), 1) + at
        allowed = (col_ref[:end] == row_ref[:, at:end]) & (keys <= queries)
        bias[:end, at:end] = jnp.where(allowed, 0.0, NEG_FILL)


def attend_kernel(q_width, kv_width, here, own, one, two, three, far, gain_ref, pack_ref, cos_ref,
                  sin_ref, row_ref, col_ref, out_0, out_1, out_2, out_3, normed_out, heads_ref,
                  attended_ref, sums_ref, bias, rows_ref, pack, normed_ref, total, sems, out_sems):
    bf16 = jnp.bfloat16
    scale = 1.0 / math.sqrt(HEAD_DIM)
    q_heads, kv_heads = q_width // HEAD_DIM, kv_width // HEAD_DIM
    qkv = q_width + 2 * kv_width
    wait_rows = fetch(here, (own, one, two, (three, far)), rows_ref, sems, in_order=True)
    copies = [
        pltpu.make_async_copy(
            pack_ref.at[:, pl.ds(at, size)], pack.at[:, pl.ds(at, size)], sems.at[4 + k]
        )
        for k, (at, size) in enumerate(((0, qkv), (qkv, q_width)))
    ]
    for copy in copies:
        copy.start()
    mask_bias(row_ref, col_ref, bias)
    wait_rows()
    x = rows_ref[...].astype(jnp.float32)
    inv = lax.rsqrt(jnp.mean(x * x, -1, keepdims=True) + EPS)
    normed_ref[...] = (x * inv * gain_ref[...]).astype(bf16)
    pending = [pltpu.make_async_copy(normed_ref, normed_out, out_sems.at[4])]
    pending[0].start()
    copies[0].wait()
    cosine, sine = cos_ref[...], sin_ref[...]
    heads = dot(normed_ref[...], pack[:, :qkv]).T
    for h in range(q_heads + kv_heads):
        at = h * HEAD_DIM
        turned = turn(heads[at : at + HEAD_DIM], cosine, sine).astype(bf16)
        heads_ref[at : at + HEAD_DIM] = turned * bf16(scale) if h < q_heads else turned
    heads_ref[q_width + kv_width :] = heads[q_width + kv_width :].astype(bf16)
    keys = [
        heads_ref[at : at + HEAD_DIM].T
        for at in range(q_width, q_width + kv_width, HEAD_DIM)
    ]
    for start, end in spans(x.shape[0]):
        parts = []
        for h in range(q_heads):
            c = h * kv_heads // q_heads
            at = q_width + kv_width + c * HEAD_DIM
            query_t = heads_ref[h * HEAD_DIM : (h + 1) * HEAD_DIM, start:end]
            scores = dot(keys[c][:end], query_t) + bias[:end, start:end]
            top = jnp.max(scores, 0, keepdims=True)
            raised = jnp.exp(scores - top)
            raised_sum = jnp.sum(raised, 0, keepdims=True)
            sums_ref[h : h + 1, start:end] = top + jnp.log(raised_sum)
            value_t = heads_ref[at : at + HEAD_DIM, :end]
            parts.append(dot(value_t, raised.astype(bf16)) / raised_sum)
        attended_ref[start:end] = jnp.concatenate(parts, 0).T.astype(bf16)
    copies[1].wait()
    total[...] = outer_t(attended_ref[...], pack[:, qkv:]).astype(bf16)
    for k, out in enumerate((out_0, out_1, out_2, out_3)):
        rows = rows_of(here, k, out.shape[0])
        pending.append(pltpu.make_async_copy(total.at[rows], out, out_sems.at[k]))
        pending[-1].start()
    for copy in pending:
        copy.wait()


def attend(here, blocks, gain, pack, cosine, sine, row, col, q_width, kv_width):
    rows, depth = 4 * blocks[0].shape[0], blocks[0].shape[1]
    bf16 = jnp.bfloat16
    qkv = q_width + 2 * kv_width
    return pl.pallas_call(
        functools.partial(attend_kernel, q_width, kv_width),
        out_shape=(
            *[jax.ShapeDtypeStruct((rows // 4, depth), bf16)] * 4,
            jax.ShapeDtypeStruct((rows, depth), bf16),
            jax.ShapeDtypeStruct((qkv, rows), bf16),
            jax.ShapeDtypeStruct((rows, q_width), bf16),
            jax.ShapeDtypeStruct((q_width // HEAD_DIM, rows), jnp.float32),
        ),
        in_specs=[SMEM] + [ANY] * 5 + [VMEM, ANY] + [VMEM] * 4,
        out_specs=[ANY] * 5 + [VMEM] * 3,
        scratch_shapes=[
            pltpu.VMEM((rows, rows), jnp.float32),
            pltpu.VMEM((rows, depth), bf16),
            pltpu.VMEM(pack.shape, bf16),
            pltpu.VMEM((rows, depth), bf16),
            pltpu.VMEM((rows, depth), bf16),
            pltpu.SemaphoreType.DMA((6,)),
            pltpu.SemaphoreType.DMA((5,)),
        ],
        cost_estimate=pl.CostEstimate(
            flops=2 * rows * depth * (qkv + q_width) + 4 * rows * rows * q_width,
            bytes_accessed=2 * (3 * rows * depth + depth * (qkv + q_width)),
            transcendentals=rows * rows * q_width // HEAD_DIM,
        ),
        compiler_params=pltpu.CompilerParams(vmem_limit_bytes=60 * MIB),
    )(here, *flat(blocks), gain, pack, cosine, sine, row, col)

def attend_back_kernel(q_width, kv_width, owners, here, own, one, two, three, far, normed_ref, pack_ref,
                       cos_ref, sin_ref, row_ref, col_ref, heads_ref, sums_ref, attended_ref, out_0,
                       out_1, out_2, out_3, other_ref, own_ref, bias, d_att_t, d_heads_t, d_keys,
                       rows_ref, normed, pack, out, d_qkv, lefts, blocks, sems, out_sems):
    bf16 = jnp.bfloat16
    scale = 1.0 / math.sqrt(HEAD_DIM)
    q_heads, kv_heads = q_width // HEAD_DIM, kv_width // HEAD_DIM
    qkv = q_width + 2 * kv_width
    wait_rows = fetch(here, (own, one, two, (three, far)), rows_ref, sems, in_order=True)
    copies = [
        pltpu.make_async_copy(
            pack_ref.at[:, pl.ds(at, size)], pack.at[:, pl.ds(at, size)], sems.at[5 + k]
        )
        for k, (at, size) in enumerate(((qkv, q_width), (0, qkv)))
    ]
    for copy in copies:
        copy.start()
    wait_normed = fetch(here, [normed_ref], normed, sems.at[pl.ds(4, 1)])
    mask_bias(row_ref, col_ref, bias)
    wait_rows()
    copies[0].wait()
    d_att_t[...] = dot(rows_ref[...], pack[:, qkv:]).T.astype(bf16)
    for c in range(kv_heads):
        at = q_width + c * HEAD_DIM
        key_t = heads_ref[at : at + HEAD_DIM]
        key = key_t.T
        value = heads_ref[at + kv_width : at + kv_width + HEAD_DIM].T
        d_keys[...] = jnp.zeros_like(d_keys)
        for start, end in spans(key.shape[0]):
            d_key = d_value = 0.0
            cosine, sine = cos_ref[:, start:end], sin_ref[:, start:end]
            for h in range(c * q_heads // kv_heads, (c + 1) * q_heads // kv_heads):
                head = slice(h * HEAD_DIM, (h + 1) * HEAD_DIM)
                query_t = heads_ref[head, start:end]
                d_out_t = d_att_t[head, start:end]
                prob = jnp.exp(
                    dot(key[:end], query_t) + bias[:end, start:end] - sums_ref[h : h + 1, start:end]
                )
                d_prob = dot(value[:end], d_out_t)
                delta = jnp.sum(prob * d_prob, 0, keepdims=True)
                d_scores = (prob * (d_prob - delta)).astype(bf16)
                d_value = d_value + outer_t(prob.astype(bf16), d_out_t)
                d_key = d_key + outer_t(d_scores, query_t)
                d_query = dot(key_t[:, :end], d_scores) * scale
                d_heads_t[head, start:end] = turn(d_query, cosine, -sine)
            d_keys[0, :end] += d_key
            d_keys[1, :end] += d_value
        d_heads_t[at : at + HEAD_DIM] = turn(d_keys[0].T, cos_ref[...], -sin_ref[...])
        d_heads_t[at + kv_width : at + kv_width + HEAD_DIM] = d_keys[1].T
    d_qkv[...] = d_heads_t[...].T.astype(bf16)
    copies[1].wait()
    out[...] = outer_t(d_qkv[...], pack[:, :qkv]).astype(bf16)
    pending = []
    for k, part in enumerate((out_0, out_1, out_2, out_3)):
        rows = rows_of(here, k, part.shape[0])
        pending.append(pltpu.make_async_copy(out.at[rows], part, out_sems.at[4 + k]))
        pending[-1].start()

    wait_normed()
    lefts[0] = normed[...].T
    lefts[1] = rows_ref[...].T
    block = lefts.shape[1] // owners
    for half, target in enumerate((other_ref, own_ref)):

        def step(m, carry, half=half, target=target):
            owner = here[1] ^ (1 - half) ^ (2 * m)
            rows = pl.ds(pl.multiple_of(owner * block, block), block)
            slot = 2 * half + m % 2
            copy = pltpu.make_async_copy(
                blocks.at[slot], target.at[pl.ds(m * block, block)], out_sems.at[slot]
            )
            pl.when(m >= 2)(copy.wait)
            blocks[slot, :, :qkv] = dot(lefts[0, rows], d_qkv[...]).astype(bf16)
            blocks[slot, :, qkv:] = dot(lefts[1, rows], attended_ref[...]).astype(bf16)
            copy.start()
            return carry

        lax.fori_loop(0, owners // 2, step, 0)
        for slot in (2 * half, 2 * half + 1):
            pending.append(
                pltpu.make_async_copy(
                    blocks.at[slot], target.at[pl.ds(0, block)], out_sems.at[slot]
                )
            )
    for copy in pending:
        copy.wait()


def attend_back(
    here,
    blocks,
    normed,
    pack,
    cosine,
    sine,
    row,
    col,
    heads,
    sums,
    attended,
    owners,
    q_width,
    kv_width,
):
    rows, depth = normed.shape
    bf16 = jnp.bfloat16
    f32 = jnp.float32
    qkv = q_width + 2 * kv_width
    width = qkv + q_width
    return pl.pallas_call(
        functools.partial(attend_back_kernel, q_width, kv_width, owners),
        out_shape=(
            *[jax.ShapeDtypeStruct((rows // 4, depth), bf16)] * 4,
            jax.ShapeDtypeStruct((depth // 2, width), bf16),
            jax.ShapeDtypeStruct((depth // 2, width), bf16),
        ),
        in_specs=[SMEM] + [ANY] * 7 + [VMEM] * 7,
        out_specs=[ANY] * 6,
        scratch_shapes=[
            pltpu.VMEM((rows, rows), f32),
            pltpu.VMEM((q_width, rows), bf16),
            pltpu.VMEM((qkv, rows), f32),
            pltpu.VMEM((2, rows, HEAD_DIM), f32),
            pltpu.VMEM((rows, depth), bf16),
            pltpu.VMEM((rows, depth), bf16),
            pltpu.VMEM(pack.shape, bf16),
            pltpu.VMEM((rows, depth), bf16),
            pltpu.VMEM((rows, qkv), bf16),
            pltpu.VMEM((2, depth, rows), bf16),
            pltpu.VMEM((4, depth // owners, width), bf16),
            pltpu.SemaphoreType.DMA((7,)),
            pltpu.SemaphoreType.DMA((8,)),
        ],
        cost_estimate=pl.CostEstimate(
            flops=4 * rows * depth * (qkv + q_width) + 10 * rows * rows * q_width,
            bytes_accessed=2 * (3 * rows * depth + 2 * depth * (qkv + q_width)),
            transcendentals=rows * rows * q_width // HEAD_DIM,
        ),
        compiler_params=pltpu.CompilerParams(vmem_limit_bytes=60 * MIB),
    )(here, *flat(blocks), normed, pack, cosine, sine, row, col, heads, sums, attended)


def back_through_norm(parts, above, rows, gain, low_too=False):
    shape = above.shape
    f32, bf16 = jnp.float32, jnp.bfloat16
    given = [*parts, above, rows]
    half = pl.BlockSpec((shape[0] // 2, shape[1]), lambda i: (i, 0))

    def kernel(gain_ref, *refs):
        *parts_in, above_ref, rows_ref = refs[: len(given)]
        x = rows_ref[...].astype(f32)
        inv = lax.rsqrt(jnp.mean(x * x, -1, keepdims=True) + EPS)
        back = norm_back(sum_of([part[...] for part in parts_in]), x * inv, inv, gain_ref[...])
        total = above_ref[...].astype(f32) + back
        for out in refs[len(given) :]:
            out[...] = total.astype(out.dtype)

    outs = [f32, bf16] if low_too else [bf16]
    return pl.pallas_call(
        kernel,
        grid=(2,),
        out_shape=[jax.ShapeDtypeStruct(shape, each) for each in outs],
        in_specs=[pl.BlockSpec(gain.shape, lambda i: (0, 0))] + [half] * len(given),
        out_specs=[half] * len(outs),
        cost_estimate=pl.CostEstimate(
            flops=20 * shape[0] * shape[1],
            bytes_accessed=sum(each.size * each.dtype.itemsize for each in given),
            transcendentals=shape[0],
        ),
        compiler_params=pltpu.CompilerParams(vmem_limit_bytes=60 * MIB),
    )(gain, *given)


def body(
    tokens,
    lengths,
    attn_gain,
    w_query,
    w_key,
    w_value,
    w_output,
    ffn_gain,
    w_gate,
    w_up,
    w_down,
    cotangent,
):
    bf16 = jnp.bfloat16
    count = lax.axis_size("tensor")
    local_rows = tokens.shape[0]
    width = w_query.shape[1]
    kv_width = w_key.shape[1]
    hidden_units = w_gate.shape[1]
    here = position()

    token_rows = spread(tokens)
    attn_pack, ffn_pack = pack_weights(
        w_query, w_key, w_value, w_output, w_gate, w_up, w_down
    )
    attn_pack = lax.all_gather(attn_pack, "dp", axis=0, tiled=True)
    gains = lax.all_gather(
        jnp.stack([attn_gain, ffn_gain])[None], "dp", axis=0, tiled=True
    ).astype(jnp.float32)
    gain_one = gains[:, 0].reshape(1, -1)
    gain_two = gains[:, 1].reshape(1, -1)
    ffn_pack = lax.all_gather(ffn_pack, "dp", axis=0, tiled=True)
    cot_own, token_rows = lax.optimization_barrier((cotangent, token_rows))
    cot_one, cot_three = beside(cot_own), between(cot_own)
    full_pair = ffn_pack[:, : 2 * hidden_units]
    full_down = ffn_pack[:, 2 * hidden_units :]

    segment, offset = seq_layout(
        lengths[0], jnp.arange(count * local_rows, dtype=jnp.int32)
    )
    cosine, sine = rope_tables(offset)
    as_row, as_column = segment[None], segment[:, None]
    *parts, normed_one, heads, attended, log_sums = attend(
        here,
        [tokens, *token_rows],
        gain_one,
        attn_pack,
        cosine,
        sine,
        as_row,
        as_column,
        width,
        kv_width,
    )
    parts, cot_one, cot_three = lax.optimization_barrier((parts, cot_one, cot_three))
    far, cot_two, cot_near = inward(parts[3]), between(cot_one), outward(cot_three)
    parts, far, cot_two, cot_near = lax.optimization_barrier((parts, far, cot_two, cot_near))
    near, two, cot_far = inward(parts[2]), between(add(parts[2], far)), outward(cot_two)
    three, one = between(add(parts[3], near)), beside(add(parts[1], two))
    cot_rows = [cotangent, cot_one, (cot_two, cot_near), (cot_three, cot_far)]
    resid = tokens.astype(jnp.float32)
    hidden = resid + sum_of([parts[0], one, three])

    inv_two = lax.rsqrt(jnp.mean(hidden * hidden, -1, keepdims=True) + EPS)
    unit_two = hidden * inv_two
    own_two = (unit_two * gain_two).astype(bf16)
    two_rows = spread_in_turn(own_two)
    two_rows = [own_two, *two_rows]
    halfway = ffn(0, here, two_rows[:2], cot_rows[:2], ffn_pack)
    activation, d_pair = ffn(1, here, two_rows[2:], cot_rows[2:], ffn_pack, halfway)
    half = 2 * local_rows
    two_parts = split(outer_t(d_pair[half:], full_pair).astype(bf16), 2)
    two_parts = split(outer_t(d_pair[:half], full_pair).astype(bf16), 2) + two_parts
    two_parts, activation, d_pair = collect(two_parts, activation, d_pair)
    ffn_local = grads_of(
        here, [(two_rows, d_pair), (cot_rows, activation)]
    )
    two_parts, ffn_local = lax.optimization_barrier((two_parts, ffn_local))
    ffn_grads = lax.psum_scatter(ffn_local, "dp", scatter_dimension=0, tiled=True)

    d_hidden, own_back = back_through_norm(two_parts, cotangent, hidden, gain_two, low_too=True)
    back_rows = spread_in_turn(own_back)
    down_total = outer_t(after(activation, own_back), full_down).astype(bf16)
    parts = split(after(down_total, back_rows[1]), count)
    far = inward(parts[3])
    parts, far, back_rows = lax.optimization_barrier((parts, far, back_rows))
    near, two = inward(parts[2]), between(add(parts[2], far))
    back_rows = [own_back, *back_rows]
    *one_total, other_local, own_local = attend_back(
        here,
        back_rows,
        normed_one,
        attn_pack,
        cosine,
        sine,
        as_row,
        as_column,
        heads,
        log_sums,
        attended,
        lax.axis_size("dp"),
        width,
        kv_width,
    )
    other_local, outer, inner_sum = lax.optimization_barrier(
        (other_local, add(parts[1], two), add(parts[3], near))
    )
    block_out = (hidden + sum_of([parts[0], beside(outer), between(inner_sum)])).astype(bf16)
    (one_parts,) = collect(one_total)
    attn_pairs = pair_sum(other_local, own_local)
    attn_parts = scatter_sum(attn_pairs)
    (grad_tokens,) = back_through_norm(one_parts, d_hidden, tokens, gain_one)
    own_gains = [each.astype(jnp.float32).reshape(1, -1) for each in (attn_gain, ffn_gain)]
    *ffn_grads, ffn_gain_part = unpack_ffn(ffn_grads, w_gate, w_up, own_gains[1])
    attn_parts, ffn_grads = lax.optimization_barrier((attn_parts, ffn_grads))
    grad_query, grad_key, grad_value, grad_output, attn_gain_part = unpack_attention(
        attn_parts, w_query, w_key.T, w_value.T, own_gains[0]
    )
    gain_parts = jnp.concatenate([attn_gain_part[:1], ffn_gain_part[:1]], 0)
    gain_parts, block_out = lax.optimization_barrier((gain_parts, block_out))
    gain_grads = sum_of(
        [gain_parts]
        + [
            lax.ppermute(gain_parts, "tensor", [(i, (i + k) % count) for i in range(count)])
            for k in range(1, count)
        ]
    )
    return (
        block_out,
        grad_tokens,
        gain_grads[0],
        grad_query,
        grad_key.T,
        grad_value.T,
        grad_output,
        gain_grads[1],
        *ffn_grads,
    )


def solution(mesh):
    return jax.shard_map(
        body,
        mesh=mesh,
        in_specs=(
            P(("dp", "tensor"), None),
            P("dp", None),
            P("dp"),
            P("dp", "tensor"),
            P("dp", "tensor"),
            P("dp", "tensor"),
            P("tensor", "dp"),
            P("dp"),
            P("dp", "tensor"),
            P("dp", "tensor"),
            P("tensor", "dp"),
            P(("dp", "tensor"), None),
        ),
        out_specs=(
            P(("dp", "tensor"), None),
            P(("dp", "tensor"), None),
            P("dp"),
            P("dp", "tensor"),
            P("dp", "tensor"),
            P("dp", "tensor"),
            P("tensor", "dp"),
            P("dp"),
            P("dp", "tensor"),
            P("dp", "tensor"),
            P("tensor", "dp"),
        ),
        check_vma=False,
    )
```

```python
import functools
import math

import jax
import jax.numpy as jnp
from jax import lax
from jax.experimental import pallas as pl
from jax.experimental.pallas import tpu as pltpu
from jax.sharding import PartitionSpec as P

HEAD_DIM = 64
EPS = 1e-05
ROPE_BASE = 10000.0
NEG_FILL = -1e30
MIB = 1024 * 1024


def seq_layout(row_lengths, places):
    ends = jnp.cumsum(row_lengths)
    starts = ends - row_lengths
    segment = jnp.sum((places[:, None] >= ends[None, :]).astype(jnp.int32), axis=1)
    owner = segment[:, None] == jnp.arange(row_lengths.shape[0], dtype=jnp.int32)[None, :]
    begin = jnp.sum(jnp.where(owner, starts[None, :], 0), axis=1)
    return (segment, places - begin)


def rope_tables(position):
    half = HEAD_DIM // 2
    freqs = ROPE_BASE ** (-(jnp.arange(half, dtype=jnp.float32) * 2.0 / HEAD_DIM))
    angles = freqs[:, None] * position.astype(jnp.float32)[None, :]
    return (jnp.cos(angles), jnp.sin(angles))


def dot(left, right):
    return jnp.dot(left, right, preferred_element_type=jnp.float32)


def inner(left, right):
    return lax.dot_general(
        left, right, (((0,), (0,)), ((), ())), preferred_element_type=jnp.float32
    )


def outer_t(left, right):
    return lax.dot_general(
        left, right, (((1,), (1,)), ((), ())), preferred_element_type=jnp.float32
    )


def norm_back(d_normed, unit, inv, gain):
    scaled = d_normed * gain
    return inv * (scaled - unit * jnp.mean(scaled * unit, -1, keepdims=True))


def swap(block, *pairs):
    return lax.ppermute(block, "tensor", [p for i, j in pairs for p in ((i, j), (j, i))])


def outward(block):
    return lax.ppermute(block, "tensor", [(1, 0), (2, 3)])


def inward(block):
    return lax.ppermute(block, "tensor", [(0, 1), (3, 2)])


def beside(block):
    return swap(block, (0, 1), (2, 3))


def between(block):
    return swap(block, (1, 2))


def apart(block):
    return swap(block, (0, 2), (1, 3))


def spread(block):
    one, two, three = beside(block), apart(block), between(block)
    return [one, two, (three, outward(two))]


def spread_in_turn(block):
    one, two = beside(block), apart(block)
    return [one, two, (between(after(block, two)), outward(two))]


def position():
    me = lax.axis_index("tensor")
    inner_one = ((me == 1) | (me == 2)).astype(jnp.int32)
    return jnp.stack([inner_one, lax.axis_index("dp"), me])


def collect(parts, *others):
    far, three = inward(parts[3]), between(parts[3])
    far, three, parts, *others = lax.optimization_barrier((far, three, parts, *others))
    return ([parts[0], beside(parts[1]), apart(add(parts[2], far)), three], *others)


def split(total, count):
    rows = total.shape[0] // count
    return [total[k * rows : (k + 1) * rows] for k in range(count)]


def add(left, right):
    return (left.astype(jnp.float32) + right.astype(jnp.float32)).astype(left.dtype)


def after(value, *others):
    return lax.optimization_barrier((value, *others))[0]


SMEM = pl.BlockSpec(memory_space=pltpu.SMEM)
VMEM = pl.BlockSpec(memory_space=pltpu.VMEM)


ANY = pl.BlockSpec(memory_space=pl.ANY)


def rows_of(here, k, rows):
    return pl.ds(pl.multiple_of((here[2] ^ k) * rows, rows), rows)


def fetch(here, blocks, into, sems, in_order=False):
    copies, at = [], 0
    for k, block in enumerate(blocks):
        choices = block if isinstance(block, tuple) else (block,)
        rows = choices[0].shape[0]
        place = into.at[rows_of(here, k, rows) if in_order else pl.ds(at, rows)]
        options = [pltpu.make_async_copy(each, place, sems.at[k]) for each in choices]
        if len(options) == 1:
            options[0].start()
        else:
            pl.when(here[0] == 1)(options[0].start)
            pl.when(here[0] != 1)(options[1].start)
        copies.append(options[0])
        at += rows

    def wait():
        for copy in copies:
            copy.wait()

    return wait


def flat(blocks):
    return [each for block in blocks for each in (block if isinstance(block, tuple) else (block,))]


def shaped(refs, blocks):
    refs = iter(refs)
    return [
        tuple(next(refs) for _ in block) if isinstance(block, tuple) else next(refs)
        for block in blocks
    ]


LANES = 128


def pack_weights(w_query, w_key, w_value, w_output, w_gate, w_up, w_down):
    rows, units = w_gate.shape
    kind = w_gate.dtype
    widths = [w_query.shape[1], w_key.shape[1], w_value.shape[1], w_output.shape[0]]
    given = [w_query, w_output, w_gate, w_up, w_down]

    def kernel(key, value, *refs):
        ins, refs = refs[:5], refs[5:]
        attention, ffn_out, refs = refs[0], refs[1], refs[2:]
        (query_in, output_in, gate_in, up_in, down_in), refs = refs[:5], refs[5:]
        attention_held, ffn_held, sems, out_sems = refs
        waits = [
            fetch(None, [each], into, sems.at[pl.ds(k, 1)])
            for k, (each, into) in enumerate(
                zip(ins, (query_in, output_in, gate_in, up_in, down_in))
            )
        ]
        at = query_in.shape[1]
        pair = jnp.concatenate([key[...], value[...]], 0).T
        attention_held[:, at : at + pair.shape[1]] = pair
        waits[0]()
        attention_held[:, :at] = query_in[...]
        waits[1]()
        attention_held[:, at + pair.shape[1] :] = output_in[...].T
        first = pltpu.make_async_copy(attention_held, attention, out_sems.at[0])
        first.start()
        waits[2]()
        waits[3]()
        for j in range(units // LANES):
            at = j * LANES
            ffn_held[:, 2 * at : 2 * at + LANES] = gate_in[:, at : at + LANES]
            ffn_held[:, 2 * at + LANES : 2 * at + 2 * LANES] = up_in[:, at : at + LANES]
        second = pltpu.make_async_copy(
            ffn_held.at[:, pl.ds(0, 2 * units)], ffn_out.at[:, pl.ds(0, 2 * units)], out_sems.at[1]
        )
        second.start()
        waits[4]()
        ffn_held[:, 2 * units :] = down_in[...].T
        third = pltpu.make_async_copy(
            ffn_held.at[:, pl.ds(2 * units, units)],
            ffn_out.at[:, pl.ds(2 * units, units)],
            out_sems.at[2],
        )
        third.start()
        for copy in (first, second, third):
            copy.wait()

    return pl.pallas_call(
        kernel,
        out_shape=(
            jax.ShapeDtypeStruct((rows, sum(widths)), kind),
            jax.ShapeDtypeStruct((rows, 3 * units), kind),
        ),
        in_specs=[VMEM, VMEM] + [ANY] * 5,
        out_specs=[ANY] * 2,
        scratch_shapes=[pltpu.VMEM(each.shape, kind) for each in given]
        + [
            pltpu.VMEM((rows, sum(widths)), kind),
            pltpu.VMEM((rows, 3 * units), kind),
            pltpu.SemaphoreType.DMA((5,)),
            pltpu.SemaphoreType.DMA((3,)),
        ],
        compiler_params=pltpu.CompilerParams(vmem_limit_bytes=60 * MIB),
    )(w_key.T, w_value.T, *given)


def across(block, step):
    return lax.ppermute(block, "dp", [(i, i ^ step) for i in range(lax.axis_size("dp"))])


def pair_sum(other, own):
    return split(add(own, across(other, 1)), lax.axis_size("dp") // 2)


def scatter_sum(blocks):
    return [blocks[0]] + [across(blocks[m], 2 * m) for m in range(1, len(blocks))]


def unpack_ffn(packed, w_gate, w_up, gain):
    rows, units = packed.shape[0], packed.shape[1] // 3
    f32 = jnp.float32

    def kernel(ref, gate_in, up_in, gain_ref, gate, up, down, gain_out):
        total = jnp.zeros((rows, LANES), f32)
        for j in range(units // LANES):
            at = j * LANES
            span = slice(at, at + LANES)
            d_gate = ref[:, 2 * at : 2 * at + LANES].astype(f32)
            d_up = ref[:, 2 * at + LANES : 2 * at + 2 * LANES].astype(f32)
            total += d_gate * gate_in[:, span].astype(f32) + d_up * up_in[:, span].astype(f32)
            gate[:, span] = d_gate
            up[:, span] = d_up
            down[span] = ref[:, 2 * units + at : 2 * units + at + LANES].T.astype(f32)
        gain_out[...] = jnp.zeros_like(gain_out)
        gain_out[0:1] = jnp.sum(total.T, 0, keepdims=True) / gain_ref[...]

    return pl.pallas_call(
        kernel,
        out_shape=(
            jax.ShapeDtypeStruct((rows, units), f32),
            jax.ShapeDtypeStruct((rows, units), f32),
            jax.ShapeDtypeStruct((units, rows), f32),
            jax.ShapeDtypeStruct((8, rows), f32),
        ),
        compiler_params=pltpu.CompilerParams(vmem_limit_bytes=24 * MIB),
    )(packed, w_gate, w_up, gain)


def unpack_attention(parts, w_query, w_key_t, w_value_t, gain):
    rows, width = w_query.shape
    kv_width = w_key_t.shape[0]
    f32 = jnp.float32
    ends = [width, width + 2 * kv_width, 2 * width + 2 * kv_width]

    def kernel(*refs):
        query, key, value, output, gain_out = refs[-5:]
        query_in, key_in, value_in, gain_ref = refs[-9:-5]
        refs = refs[:-9]

        def columns(at, end):
            return sum_of([ref[:, at:end] for ref in refs])

        total = jnp.zeros((rows, LANES), f32)
        for at in range(0, width, LANES):
            span = slice(at, at + LANES)
            d_query = columns(at, at + LANES)
            query[:, span] = d_query
            total += d_query * query_in[:, span].astype(f32)
        pair = columns(ends[0], ends[1]).T
        key[...] = pair[:kv_width]
        value[...] = pair[kv_width:]
        total = total.T
        both = jnp.sum(total, 0, keepdims=True)
        both += jnp.sum(pair[:kv_width] * key_in[...].astype(f32), 0, keepdims=True)
        both += jnp.sum(pair[kv_width:] * value_in[...].astype(f32), 0, keepdims=True)
        gain_out[...] = jnp.zeros_like(gain_out)
        gain_out[0:1] = both / gain_ref[...]
        output[...] = columns(ends[1], ends[2]).T

    return pl.pallas_call(
        kernel,
        out_shape=(
            jax.ShapeDtypeStruct((rows, width), f32),
            jax.ShapeDtypeStruct((kv_width, rows), f32),
            jax.ShapeDtypeStruct((kv_width, rows), f32),
            jax.ShapeDtypeStruct((width, rows), f32),
            jax.ShapeDtypeStruct((8, rows), f32),
        ),
        compiler_params=pltpu.CompilerParams(vmem_limit_bytes=24 * MIB),
    )(*parts, w_query, w_key_t, w_value_t, gain)


def grads_kernel(lefts, block, here, *refs):
    refs = list(refs)
    given = []
    for blocks in lefts:
        count = len(flat(blocks))
        given.append((shaped(refs[:count], blocks), refs[count]))
        del refs[: count + 1]
    out, *held, sems = refs
    step = pl.program_id(0)

    def dots(first):
        at = 0
        if first:
            waits = [
                (
                    fetch(here, left, held[2 * k], sems.at[k]),
                    fetch(here, [right], held[2 * k + 1], sems.at[k, pl.ds(4, 1)]),
                )
                for k, (left, right) in enumerate(given)
            ]
        for k in range(len(given)):
            left, right = held[2 * k], held[2 * k + 1]
            if first:
                for wait in waits[k]:
                    wait()
            width = right.shape[1]
            columns = pl.ds(pl.multiple_of(step * block, block), block)
            out[:, at : at + width] = inner(left[:, columns], right[...]).astype(out.dtype)
            at += width

    pl.when(step == 0)(lambda: dots(True))
    pl.when(step != 0)(lambda: dots(False))


def grads_of(here, pairs):
    bf16 = jnp.bfloat16
    rows, depth = pairs[0][1].shape[0], flat(pairs[0][0])[0].shape[1]
    block = min(256, depth)
    width = sum(right.shape[1] for _, right in pairs)
    given = [each for left, right in pairs for each in (*flat(left), right)]
    held = [
        pltpu.VMEM(shape, bf16) for _, right in pairs for shape in ((rows, depth), right.shape)
    ]
    return pl.pallas_call(
        functools.partial(grads_kernel, [left for left, _ in pairs], block),
        grid=(depth // block,),
        out_shape=jax.ShapeDtypeStruct((depth, width), bf16),
        in_specs=[SMEM] + [ANY] * len(given),
        out_specs=pl.BlockSpec((block, width), lambda i: (i, 0)),
        scratch_shapes=[*held, pltpu.SemaphoreType.DMA((len(pairs), 5))],
        cost_estimate=pl.CostEstimate(
            flops=2 * rows * depth * width,
            bytes_accessed=2 * (depth * width + rows * width + 2 * rows * depth),
            transcendentals=0,
        ),
        compiler_params=pltpu.CompilerParams(vmem_limit_bytes=60 * MIB),
    )(here, *given)


def ffn_kernel(shapes, units, here, *refs):
    refs = list(refs)
    lefts = []
    for blocks in shapes:
        count = len(flat(blocks))
        lefts.append(shaped(refs[:count], blocks))
        del refs[:count]
    w_pair, w_down = refs[:2]
    act_ref, d_pair_ref, rows_ref, cot_ref, sems = refs[-5:]

    @pl.when(pl.program_id(0) == 0)
    def _():
        waits = [
            fetch(here, given, into, sems.at[k])
            for k, (into, given) in enumerate(zip((rows_ref, cot_ref), lefts))
        ]
        for wait in waits:
            wait()

    def columns(blocks):
        pairs = dot(rows_ref[...], w_pair[:, : 2 * blocks * LANES])
        d_acts = dot(cot_ref[...], w_down[:, : blocks * LANES])
        for k in range(blocks):
            at = k * LANES
            gate, up = pairs[:, 2 * at : 2 * at + LANES], pairs[:, 2 * at + LANES : 2 * at + 2 * LANES]
            d_act = d_acts[:, at : at + LANES]
            sigma = jax.nn.sigmoid(gate)
            swish = gate * sigma
            act_ref[:, at : at + LANES] = (swish * up).astype(act_ref.dtype)
            d_gate = d_act * up * (sigma * (1.0 + gate * (1.0 - sigma)))
            d_pair_ref[:, 2 * at : 2 * at + LANES] = d_gate.astype(d_pair_ref.dtype)
            d_pair_ref[:, 2 * at + LANES : 2 * at + 2 * LANES] = (d_act * swish).astype(
                d_pair_ref.dtype
            )

    wide = w_down.shape[1] // LANES
    last, left = pl.num_programs(0) - 1, units // LANES % wide
    pl.when((pl.program_id(0) < last) | (left == 0))(lambda: columns(wide))
    if left:
        pl.when(pl.program_id(0) == last)(lambda: columns(left))


def ffn(side, here, rows, cots, pack, before=()):
    block, depth = flat(rows)[0].shape
    units = pack.shape[1] // 3
    wide = 2 * LANES if (2 * units) % (2 * LANES) == 0 else LANES
    bf16 = jnp.bfloat16
    given = [here, *flat(rows), *flat(cots), pack, pack, *before]
    specs = [SMEM] + [ANY] * (len(given) - 3 - len(before))
    specs.append(pl.BlockSpec((depth, 2 * wide), lambda j: (0, j)))
    specs.append(pl.BlockSpec((depth, wide), lambda j: (0, 2 * units // wide + j)))
    specs += [ANY for _ in before]
    return pl.pallas_call(
        functools.partial(ffn_kernel, (rows, cots), units),
        grid=(pl.cdiv(units, wide),),
        out_shape=(
            jax.ShapeDtypeStruct((4 * block, units), bf16),
            jax.ShapeDtypeStruct((4 * block, 2 * units), bf16),
        ),
        in_specs=specs,
        out_specs=(
            pl.BlockSpec((2 * block, wide), lambda j: (side, j)),
            pl.BlockSpec((2 * block, 2 * wide), lambda j: (side, j)),
        ),
        scratch_shapes=[
            pltpu.VMEM((2 * block, depth), bf16),
            pltpu.VMEM((2 * block, depth), bf16),
            pltpu.SemaphoreType.DMA((2, 2)),
        ],
        input_output_aliases={len(given) - 2: 0, len(given) - 1: 1} if before else {},
        cost_estimate=pl.CostEstimate(
            flops=4 * block * depth * 3 * units,
            bytes_accessed=2 * (depth * 3 * units + 4 * block * depth + 6 * block * units),
            transcendentals=2 * block * units,
        ),
        compiler_params=pltpu.CompilerParams(vmem_limit_bytes=60 * MIB),
    )(*given)


def sum_of(parts):
    total = parts[0].astype(jnp.float32)
    for part in parts[1:]:
        total = total + part.astype(jnp.float32)
    return total


def turn(block, cosine, sine):
    half = HEAD_DIM // 2
    first, second = block[:half], block[half:]
    return jnp.concatenate([first * cosine - second * sine, second * cosine + first * sine], 0)

WIDE = 640


def spans(rows):
    return [(at, min(at + WIDE, rows)) for at in range(0, rows, WIDE)]


def mask_bias(row_ref, col_ref, bias):
    rows = bias.shape[0]
    for at, end in spans(rows):
        keys = lax.broadcasted_iota(jnp.int32, (end, end - at), 0)
        queries = lax.broadcasted_iota(jnp.int32, (end, end - at), 1) + at
        allowed = (col_ref[:end] == row_ref[:, at:end]) & (keys <= queries)
        bias[:end, at:end] = jnp.where(allowed, 0.0, NEG_FILL)


def attend_kernel(q_width, kv_width, here, own, one, two, three, far, gain_ref, pack_ref, cos_ref,
                  sin_ref, row_ref, col_ref, out_0, out_1, out_2, out_3, normed_out, heads_ref,
                  attended_ref, sums_ref, bias, rows_ref, pack, normed_ref, total, sems, out_sems):
    bf16 = jnp.bfloat16
    scale = 1.0 / math.sqrt(HEAD_DIM)
    q_heads, kv_heads = q_width // HEAD_DIM, kv_width // HEAD_DIM
    qkv = q_width + 2 * kv_width
    wait_rows = fetch(here, (own, one, two, (three, far)), rows_ref, sems, in_order=True)
    copies = [
        pltpu.make_async_copy(
            pack_ref.at[:, pl.ds(at, size)], pack.at[:, pl.ds(at, size)], sems.at[4 + k]
        )
        for k, (at, size) in enumerate(((0, qkv), (qkv, q_width)))
    ]
    for copy in copies:
        copy.start()
    mask_bias(row_ref, col_ref, bias)
    wait_rows()
    x = rows_ref[...].astype(jnp.float32)
    inv = lax.rsqrt(jnp.mean(x * x, -1, keepdims=True) + EPS)
    normed_ref[...] = (x * inv * gain_ref[...]).astype(bf16)
    pending = [pltpu.make_async_copy(normed_ref, normed_out, out_sems.at[4])]
    pending[0].start()
    copies[0].wait()
    cosine, sine = cos_ref[...], sin_ref[...]
    heads = dot(normed_ref[...], pack[:, :qkv]).T
    for h in range(q_heads + kv_heads):
        at = h * HEAD_DIM
        turned = turn(heads[at : at + HEAD_DIM], cosine, sine).astype(bf16)
        heads_ref[at : at + HEAD_DIM] = turned * bf16(scale) if h < q_heads else turned
    heads_ref[q_width + kv_width :] = heads[q_width + kv_width :].astype(bf16)
    keys = [
        heads_ref[at : at + HEAD_DIM].T
        for at in range(q_width, q_width + kv_width, HEAD_DIM)
    ]
    for start, end in spans(x.shape[0]):
        parts = []
        for h in range(q_heads):
            c = h * kv_heads // q_heads
            at = q_width + kv_width + c * HEAD_DIM
            query_t = heads_ref[h * HEAD_DIM : (h + 1) * HEAD_DIM, start:end]
            scores = dot(keys[c][:end], query_t) + bias[:end, start:end]
            top = jnp.max(scores, 0, keepdims=True)
            raised = jnp.exp(scores - top)
            raised_sum = jnp.sum(raised, 0, keepdims=True)
            sums_ref[h : h + 1, start:end] = top + jnp.log(raised_sum)
            value_t = heads_ref[at : at + HEAD_DIM, :end]
            parts.append(dot(value_t, raised.astype(bf16)) / raised_sum)
        attended_ref[start:end] = jnp.concatenate(parts, 0).T.astype(bf16)
    copies[1].wait()
    total[...] = outer_t(attended_ref[...], pack[:, qkv:]).astype(bf16)
    for k, out in enumerate((out_0, out_1, out_2, out_3)):
        rows = rows_of(here, k, out.shape[0])
        pending.append(pltpu.make_async_copy(total.at[rows], out, out_sems.at[k]))
        pending[-1].start()
    for copy in pending:
        copy.wait()


def attend(here, blocks, gain, pack, cosine, sine, row, col, q_width, kv_width):
    rows, depth = 4 * blocks[0].shape[0], blocks[0].shape[1]
    bf16 = jnp.bfloat16
    qkv = q_width + 2 * kv_width
    return pl.pallas_call(
        functools.partial(attend_kernel, q_width, kv_width),
        out_shape=(
            *[jax.ShapeDtypeStruct((rows // 4, depth), bf16)] * 4,
            jax.ShapeDtypeStruct((rows, depth), bf16),
            jax.ShapeDtypeStruct((qkv, rows), bf16),
            jax.ShapeDtypeStruct((rows, q_width), bf16),
            jax.ShapeDtypeStruct((q_width // HEAD_DIM, rows), jnp.float32),
        ),
        in_specs=[SMEM] + [ANY] * 5 + [VMEM, ANY] + [VMEM] * 4,
        out_specs=[ANY] * 5 + [VMEM] * 3,
        scratch_shapes=[
            pltpu.VMEM((rows, rows), jnp.float32),
            pltpu.VMEM((rows, depth), bf16),
            pltpu.VMEM(pack.shape, bf16),
            pltpu.VMEM((rows, depth), bf16),
            pltpu.VMEM((rows, depth), bf16),
            pltpu.SemaphoreType.DMA((6,)),
            pltpu.SemaphoreType.DMA((5,)),
        ],
        cost_estimate=pl.CostEstimate(
            flops=2 * rows * depth * (qkv + q_width) + 4 * rows * rows * q_width,
            bytes_accessed=2 * (3 * rows * depth + depth * (qkv + q_width)),
            transcendentals=rows * rows * q_width // HEAD_DIM,
        ),
        compiler_params=pltpu.CompilerParams(vmem_limit_bytes=60 * MIB),
    )(here, *flat(blocks), gain, pack, cosine, sine, row, col)

def attend_back_kernel(q_width, kv_width, owners, here, own, one, two, three, far, normed_ref, pack_ref,
                       cos_ref, sin_ref, row_ref, col_ref, heads_ref, sums_ref, attended_ref, out_0,
                       out_1, out_2, out_3, other_ref, own_ref, bias, d_att_t, d_heads_t, d_keys,
                       rows_ref, normed, pack, out, d_qkv, lefts, blocks, sems, out_sems):
    bf16 = jnp.bfloat16
    scale = 1.0 / math.sqrt(HEAD_DIM)
    q_heads, kv_heads = q_width // HEAD_DIM, kv_width // HEAD_DIM
    qkv = q_width + 2 * kv_width
    wait_rows = fetch(here, (own, one, two, (three, far)), rows_ref, sems, in_order=True)
    copies = [
        pltpu.make_async_copy(
            pack_ref.at[:, pl.ds(at, size)], pack.at[:, pl.ds(at, size)], sems.at[5 + k]
        )
        for k, (at, size) in enumerate(((qkv, q_width), (0, qkv)))
    ]
    for copy in copies:
        copy.start()
    wait_normed = fetch(here, [normed_ref], normed, sems.at[pl.ds(4, 1)])
    mask_bias(row_ref, col_ref, bias)
    wait_rows()
    copies[0].wait()
    d_att_t[...] = dot(rows_ref[...], pack[:, qkv:]).T.astype(bf16)
    for c in range(kv_heads):
        at = q_width + c * HEAD_DIM
        key_t = heads_ref[at : at + HEAD_DIM]
        key = key_t.T
        value = heads_ref[at + kv_width : at + kv_width + HEAD_DIM].T
        d_keys[...] = jnp.zeros_like(d_keys)
        for start, end in spans(key.shape[0]):
            d_key = d_value = 0.0
            cosine, sine = cos_ref[:, start:end], sin_ref[:, start:end]
            for h in range(c * q_heads // kv_heads, (c + 1) * q_heads // kv_heads):
                head = slice(h * HEAD_DIM, (h + 1) * HEAD_DIM)
                query_t = heads_ref[head, start:end]
                d_out_t = d_att_t[head, start:end]
                prob = jnp.exp(
                    dot(key[:end], query_t) + bias[:end, start:end] - sums_ref[h : h + 1, start:end]
                )
                d_prob = dot(value[:end], d_out_t)
                delta = jnp.sum(prob * d_prob, 0, keepdims=True)
                d_scores = (prob * (d_prob - delta)).astype(bf16)
                d_value = d_value + outer_t(prob.astype(bf16), d_out_t)
                d_key = d_key + outer_t(d_scores, query_t)
                d_query = dot(key_t[:, :end], d_scores) * scale
                d_heads_t[head, start:end] = turn(d_query, cosine, -sine)
            d_keys[0, :end] += d_key
            d_keys[1, :end] += d_value
        d_heads_t[at : at + HEAD_DIM] = turn(d_keys[0].T, cos_ref[...], -sin_ref[...])
        d_heads_t[at + kv_width : at + kv_width + HEAD_DIM] = d_keys[1].T
    d_qkv[...] = d_heads_t[...].T.astype(bf16)
    copies[1].wait()
    out[...] = outer_t(d_qkv[...], pack[:, :qkv]).astype(bf16)
    pending = []
    for k, part in enumerate((out_0, out_1, out_2, out_3)):
        rows = rows_of(here, k, part.shape[0])
        pending.append(pltpu.make_async_copy(out.at[rows], part, out_sems.at[owners + k]))
        pending[-1].start()

    wait_normed()
    lefts[0] = normed[...].T
    lefts[1] = rows_ref[...].T
    block = lefts.shape[1] // owners
    for c in range(owners // 2):
        rows = slice(2 * c * block, 2 * (c + 1) * block)
        both = dot(lefts[0, rows], d_qkv[...]).astype(bf16)
        blocks[rows, :qkv] = both
        blocks[rows, qkv:] = dot(lefts[1, rows], attended_ref[...]).astype(bf16)
        for owner in (2 * c, 2 * c + 1):
            away = here[1] ^ owner
            place = pl.ds(pl.multiple_of(lax.shift_right_logical(away, 1) * block, block), block)
            from_here = blocks.at[pl.ds(owner * block, block)]
            own, other = [
                pltpu.make_async_copy(from_here, target.at[place], out_sems.at[owner])
                for target in (own_ref, other_ref)
            ]
            pl.when((away & 1) == 0)(own.start)
            pl.when((away & 1) != 0)(other.start)
            pending.append(own)
    for copy in pending:
        copy.wait()


def attend_back(
    here,
    blocks,
    normed,
    pack,
    cosine,
    sine,
    row,
    col,
    heads,
    sums,
    attended,
    owners,
    q_width,
    kv_width,
):
    rows, depth = normed.shape
    bf16 = jnp.bfloat16
    f32 = jnp.float32
    qkv = q_width + 2 * kv_width
    width = qkv + q_width
    return pl.pallas_call(
        functools.partial(attend_back_kernel, q_width, kv_width, owners),
        out_shape=(
            *[jax.ShapeDtypeStruct((rows // 4, depth), bf16)] * 4,
            jax.ShapeDtypeStruct((depth // 2, width), bf16),
            jax.ShapeDtypeStruct((depth // 2, width), bf16),
        ),
        in_specs=[SMEM] + [ANY] * 7 + [VMEM] * 7,
        out_specs=[ANY] * 6,
        scratch_shapes=[
            pltpu.VMEM((rows, rows), f32),
            pltpu.VMEM((q_width, rows), bf16),
            pltpu.VMEM((qkv, rows), f32),
            pltpu.VMEM((2, rows, HEAD_DIM), f32),
            pltpu.VMEM((rows, depth), bf16),
            pltpu.VMEM((rows, depth), bf16),
            pltpu.VMEM(pack.shape, bf16),
            pltpu.VMEM((rows, depth), bf16),
            pltpu.VMEM((rows, qkv), bf16),
            pltpu.VMEM((2, depth, rows), bf16),
            pltpu.VMEM((depth, width), bf16),
            pltpu.SemaphoreType.DMA((7,)),
            pltpu.SemaphoreType.DMA((owners + 4,)),
        ],
        cost_estimate=pl.CostEstimate(
            flops=4 * rows * depth * (qkv + q_width) + 10 * rows * rows * q_width,
            bytes_accessed=2 * (3 * rows * depth + 2 * depth * (qkv + q_width)),
            transcendentals=rows * rows * q_width // HEAD_DIM,
        ),
        compiler_params=pltpu.CompilerParams(vmem_limit_bytes=60 * MIB),
    )(here, *flat(blocks), normed, pack, cosine, sine, row, col, heads, sums, attended)


def back_through_norm(parts, above, rows, gain, low_too=False):
    shape = above.shape
    f32, bf16 = jnp.float32, jnp.bfloat16
    given = [*parts, above, rows]
    half = pl.BlockSpec((shape[0] // 2, shape[1]), lambda i: (i, 0))

    def kernel(gain_ref, *refs):
        *parts_in, above_ref, rows_ref = refs[: len(given)]
        x = rows_ref[...].astype(f32)
        inv = lax.rsqrt(jnp.mean(x * x, -1, keepdims=True) + EPS)
        back = norm_back(sum_of([part[...] for part in parts_in]), x * inv, inv, gain_ref[...])
        total = above_ref[...].astype(f32) + back
        for out in refs[len(given) :]:
            out[...] = total.astype(out.dtype)

    outs = [f32, bf16] if low_too else [bf16]
    return pl.pallas_call(
        kernel,
        grid=(2,),
        out_shape=[jax.ShapeDtypeStruct(shape, each) for each in outs],
        in_specs=[pl.BlockSpec(gain.shape, lambda i: (0, 0))] + [half] * len(given),
        out_specs=[half] * len(outs),
        cost_estimate=pl.CostEstimate(
            flops=20 * shape[0] * shape[1],
            bytes_accessed=sum(each.size * each.dtype.itemsize for each in given),
            transcendentals=shape[0],
        ),
        compiler_params=pltpu.CompilerParams(vmem_limit_bytes=60 * MIB),
    )(gain, *given)


def body(
    tokens,
    lengths,
    attn_gain,
    w_query,
    w_key,
    w_value,
    w_output,
    ffn_gain,
    w_gate,
    w_up,
    w_down,
    cotangent,
):
    bf16 = jnp.bfloat16
    count = lax.axis_size("tensor")
    local_rows = tokens.shape[0]
    width = w_query.shape[1]
    kv_width = w_key.shape[1]
    hidden_units = w_gate.shape[1]
    here = position()

    token_rows = spread(tokens)
    attn_pack, ffn_pack = pack_weights(
        w_query, w_key, w_value, w_output, w_gate, w_up, w_down
    )
    attn_pack = lax.all_gather(attn_pack, "dp", axis=0, tiled=True)
    gains = lax.all_gather(
        jnp.stack([attn_gain, ffn_gain])[None], "dp", axis=0, tiled=True
    ).astype(jnp.float32)
    gain_one = gains[:, 0].reshape(1, -1)
    gain_two = gains[:, 1].reshape(1, -1)
    ffn_pack = lax.all_gather(ffn_pack, "dp", axis=0, tiled=True)
    cot_own, token_rows = lax.optimization_barrier((cotangent, token_rows))
    cot_one, cot_three = beside(cot_own), between(cot_own)
    full_pair = ffn_pack[:, : 2 * hidden_units]
    full_down = ffn_pack[:, 2 * hidden_units :]

    segment, offset = seq_layout(
        lengths[0], jnp.arange(count * local_rows, dtype=jnp.int32)
    )
    cosine, sine = rope_tables(offset)
    as_row, as_column = segment[None], segment[:, None]
    *parts, normed_one, heads, attended, log_sums = attend(
        here,
        [tokens, *token_rows],
        gain_one,
        attn_pack,
        cosine,
        sine,
        as_row,
        as_column,
        width,
        kv_width,
    )
    parts, cot_one, cot_three = lax.optimization_barrier((parts, cot_one, cot_three))
    far, cot_two, cot_near = inward(parts[3]), between(cot_one), outward(cot_three)
    parts, far, cot_two, cot_near = lax.optimization_barrier((parts, far, cot_two, cot_near))
    near, two, cot_far = inward(parts[2]), between(add(parts[2], far)), outward(cot_two)
    three, one = between(add(parts[3], near)), beside(add(parts[1], two))
    cot_rows = [cotangent, cot_one, (cot_two, cot_near), (cot_three, cot_far)]
    resid = tokens.astype(jnp.float32)
    hidden = resid + sum_of([parts[0], one, three])

    inv_two = lax.rsqrt(jnp.mean(hidden * hidden, -1, keepdims=True) + EPS)
    unit_two = hidden * inv_two
    own_two = (unit_two * gain_two).astype(bf16)
    two_rows = spread_in_turn(own_two)
    two_rows = [own_two, *two_rows]
    halfway = ffn(0, here, two_rows[:2], cot_rows[:2], ffn_pack)
    activation, d_pair = ffn(1, here, two_rows[2:], cot_rows[2:], ffn_pack, halfway)
    half = 2 * local_rows
    two_parts = split(outer_t(d_pair[half:], full_pair).astype(bf16), 2)
    two_parts = split(outer_t(d_pair[:half], full_pair).astype(bf16), 2) + two_parts
    two_parts, activation, d_pair = collect(two_parts, activation, d_pair)
    ffn_local = grads_of(
        here, [(two_rows, d_pair), (cot_rows, activation)]
    )
    two_parts, ffn_local = lax.optimization_barrier((two_parts, ffn_local))
    ffn_grads = lax.psum_scatter(ffn_local, "dp", scatter_dimension=0, tiled=True)

    d_hidden, own_back = back_through_norm(two_parts, cotangent, hidden, gain_two, low_too=True)
    back_rows = spread_in_turn(own_back)
    down_total = outer_t(after(activation, own_back), full_down).astype(bf16)
    parts = split(after(down_total, back_rows[1]), count)
    far = inward(parts[3])
    parts, far, back_rows = lax.optimization_barrier((parts, far, back_rows))
    near, two = inward(parts[2]), between(add(parts[2], far))
    back_rows = [own_back, *back_rows]
    *one_total, other_local, own_local = attend_back(
        here,
        back_rows,
        normed_one,
        attn_pack,
        cosine,
        sine,
        as_row,
        as_column,
        heads,
        log_sums,
        attended,
        lax.axis_size("dp"),
        width,
        kv_width,
    )
    other_local, outer, inner_sum = lax.optimization_barrier(
        (other_local, add(parts[1], two), add(parts[3], near))
    )
    block_out = (hidden + sum_of([parts[0], beside(outer), between(inner_sum)])).astype(bf16)
    (one_parts,) = collect(one_total)
    attn_pairs = pair_sum(other_local, own_local)
    attn_parts = scatter_sum(attn_pairs)
    (grad_tokens,) = back_through_norm(one_parts, d_hidden, tokens, gain_one)
    own_gains = [each.astype(jnp.float32).reshape(1, -1) for each in (attn_gain, ffn_gain)]
    *ffn_grads, ffn_gain_part = unpack_ffn(ffn_grads, w_gate, w_up, own_gains[1])
    attn_parts, ffn_grads = lax.optimization_barrier((attn_parts, ffn_grads))
    grad_query, grad_key, grad_value, grad_output, attn_gain_part = unpack_attention(
        attn_parts, w_query, w_key.T, w_value.T, own_gains[0]
    )
    gain_parts = jnp.concatenate([attn_gain_part[:1], ffn_gain_part[:1]], 0)
    gain_parts, block_out = lax.optimization_barrier((gain_parts, block_out))
    gain_grads = sum_of(
        [gain_parts]
        + [
            lax.ppermute(gain_parts, "tensor", [(i, (i + k) % count) for i in range(count)])
            for k in range(1, count)
        ]
    )
    return (
        block_out,
        grad_tokens,
        gain_grads[0],
        grad_query,
        grad_key.T,
        grad_value.T,
        grad_output,
        gain_grads[1],
        *ffn_grads,
    )


def solution(mesh):
    return jax.shard_map(
        body,
        mesh=mesh,
        in_specs=(
            P(("dp", "tensor"), None),
            P("dp", None),
            P("dp"),
            P("dp", "tensor"),
            P("dp", "tensor"),
            P("dp", "tensor"),
            P("tensor", "dp"),
            P("dp"),
            P("dp", "tensor"),
            P("dp", "tensor"),
            P("tensor", "dp"),
            P(("dp", "tensor"), None),
        ),
        out_specs=(
            P(("dp", "tensor"), None),
            P(("dp", "tensor"), None),
            P("dp"),
            P("dp", "tensor"),
            P("dp", "tensor"),
            P("dp", "tensor"),
            P("tensor", "dp"),
            P("dp"),
            P("dp", "tensor"),
            P("dp", "tensor"),
            P("tensor", "dp"),
        ),
        check_vma=False,
    )
```
